32 devices in a mesh: blk: 8 (over y, x, core), inner: 4 (over z).
Axes of the slice: x: 2, y: 2, z: 4, core: 2. Of those that a mesh axis runs over, the one named last changes fastest.
Arguments:
- teacher: bfloat16 [2048, 1536], P(('blk', 'inner')), may hold values from -50 to 50
- student: bfloat16 [2048, 768], P(('blk', 'inner')), may hold values from -50 to 50
Outputs:
- loss: float32 [], replicated
- student_grad: float32 [2048, 768], P(('blk', 'inner'))
The draws below stay inside these ranges and needn't reach their ends.
All inputs are finite; a program needn't handle non-finite values.
Results may differ from the reference program's by a relative error of at most 0.00055.
The reference program's roundings to bfloat16 on the way (of `weights`) count: a program that leaves them out, or rounds other values in their place, can miss the bound.
Values may be sent and summed in bfloat16 or wider, within the bound.
No kernel may reach another device: no remote copies, remote signals or barrier semaphores. Data moves between devices by JAX's collectives and lax.ppermute only.
A program may use at most 64 MiB of HBM per device.

```python
import math
import jax
import jax.numpy as jnp
from jax import lax

DT = 1536
DS = 768
ROWS = 64
TOTAL = 2048
N_INNER = 4


def draw_teacher(key, part):
    key = jax.random.fold_in(key, 11)
    first, second = jax.random.split(key, 2)
    base = jnp.clip(jax.random.normal(first, (TOTAL, DT), jnp.float32), -5.0, 5.0)
    scales = jnp.exp(jax.random.uniform(second, (TOTAL, 1), jnp.float32, 0.0, math.log(10.0)))
    return (base * scales).astype(jnp.bfloat16)


def draw_student(key, part):
    key = jax.random.fold_in(key, 23)
    first, second = jax.random.split(key, 2)
    base = jnp.clip(jax.random.normal(first, (TOTAL, DS), jnp.float32), -5.0, 5.0)
    scales = jnp.exp(jax.random.uniform(second, (TOTAL, 1), jnp.float32, 0.0, math.log(10.0)))
    return (base * scales).astype(jnp.bfloat16)


def setup_inputs(seed: int = 0) -> dict:
    streams_of = jax.random.split(jax.random.key(seed), 3)
    teacher = draw_teacher(jax.random.fold_in(streams_of[2], 71), 0)
    student = draw_student(jax.random.fold_in(streams_of[2], 71), 0)
    return dict(teacher=teacher, student=student)


EPSILON = 1e-06

def coefficients(sq_student, sq_teacher, cross, total):
    norm_student = jnp.sqrt(sq_student + EPSILON)
    norm_teacher = jnp.sqrt(sq_teacher + EPSILON)
    factor = 2.0 * math.sqrt(total * DS) / total
    cubed = norm_student * norm_student * norm_student
    alpha = factor * (EPSILON / norm_student + cross / norm_teacher) / cubed
    beta = factor / (norm_student * norm_teacher)
    terms = sq_student / (norm_student * norm_student) + sq_teacher / (norm_teacher * norm_teacher) - 2.0 * cross / (norm_student * norm_teacher)
    return (alpha, beta, terms)

def reference(teacher, student):
    block = ROWS * N_INNER
    count = TOTAL // block
    teacher_blocks = teacher.reshape(count, block, DT)
    student_blocks = student.reshape(count, block, DS)

    def first(pair):
        rows_t, rows_s = pair
        gram_s = jnp.dot(rows_s, student.T, preferred_element_type=jnp.float32)
        gram_t = jnp.dot(rows_t, teacher.T, preferred_element_type=jnp.float32)
        return (lax.optimization_barrier(jnp.sum(gram_s * gram_s, 1)), lax.optimization_barrier(jnp.sum(gram_t * gram_t, 1)), lax.optimization_barrier(jnp.sum(gram_s * gram_t, 1)))
    sq_s, sq_t, cross = lax.map(first, (teacher_blocks, student_blocks))
    alpha, beta, terms = coefficients(sq_s.reshape(TOTAL), sq_t.reshape(TOTAL), cross.reshape(TOTAL), TOTAL)
    loss = jnp.sum(terms) / TOTAL

    def second(col_acc, items):
        rows_t, rows_s, alpha_b, beta_b = items
        gram_s = jnp.dot(rows_s, student.T, preferred_element_type=jnp.float32)
        gram_t = jnp.dot(rows_t, teacher.T, preferred_element_type=jnp.float32)
        weights = (alpha_b[:, None] * gram_s - beta_b[:, None] * gram_t).astype(jnp.bfloat16)
        row_part = jnp.dot(weights, student, preferred_element_type=jnp.float32)
        col_acc = col_acc + jnp.dot(weights.T, rows_s, preferred_element_type=jnp.float32)
        return (col_acc, row_part)
    col_acc, row_parts = lax.scan(second, jnp.zeros((TOTAL, DS), jnp.float32), (teacher_blocks, student_blocks, alpha.reshape(count, block), beta.reshape(count, block)))
    student_grad = row_parts.reshape(TOTAL, DS) + col_acc
    return (loss, student_grad)
```

```python
import math

import jax
import jax.numpy as jnp
from jax import lax
from jax.sharding import PartitionSpec as P

DS = 768
AXES = ("blk", "inner")
GATHER_LIMIT = 24 * 2**20


EPSILON = 1e-06


def coefficients(sq_student, sq_teacher, cross, total):
    norm_student = jnp.sqrt(sq_student + EPSILON)
    norm_teacher = jnp.sqrt(sq_teacher + EPSILON)
    factor = 2.0 * math.sqrt(total * DS) / total
    cubed = norm_student * norm_student * norm_student
    alpha = factor * (EPSILON / norm_student + cross / norm_teacher) / cubed
    beta = factor / (norm_student * norm_teacher)
    terms = (
        sq_student / (norm_student * norm_student)
        + sq_teacher / (norm_teacher * norm_teacher)
        - 2.0 * cross / (norm_student * norm_teacher)
    )
    return (alpha, beta, terms)


def tile_grams(rows_t, rows_s, piece_t, piece_s):
    gram_s = jnp.einsum("rd,cd->rc", rows_s, piece_s, preferred_element_type=jnp.float32)
    gram_t = jnp.einsum("rd,cd->rc", rows_t, piece_t, preferred_element_type=jnp.float32)
    return (gram_s, gram_t)


def per_device_tiled(teacher, student):
    rows = teacher.shape[0]
    blocks = lax.axis_size("blk")
    inner = lax.axis_size("inner")
    total = rows * blocks * inner
    group_t, group_s = (
        lax.all_gather(teacher, "inner", axis=0, tiled=True),
        lax.all_gather(student, "inner", axis=0, tiled=True),
    )
    piece_t, piece_s = (
        lax.all_gather(teacher, "blk", axis=0, tiled=True),
        lax.all_gather(student, "blk", axis=0, tiled=True),
    )
    gram_s, gram_t = tile_grams(group_t, group_s, piece_t, piece_s)
    sq_s = jnp.sum(gram_s * gram_s, 1)
    sq_t = jnp.sum(gram_t * gram_t, 1)
    cross = jnp.sum(gram_s * gram_t, 1)
    sum_s, sum_t, sum_c = lax.psum((sq_s, sq_t, cross), "inner")
    alpha, beta, terms = coefficients(sum_s, sum_t, sum_c, total)
    loss = lax.psum(jnp.sum(terms), "blk") / total
    weights = (alpha[:, None] * gram_s - beta[:, None] * gram_t).astype(jnp.bfloat16)
    row_acc = jnp.dot(weights, piece_s, preferred_element_type=jnp.float32)
    col_term = jnp.einsum("rc,rd->cd", weights, group_s, preferred_element_type=jnp.float32)
    row_mine = lax.psum_scatter(row_acc, "inner", scatter_dimension=0, tiled=True)
    col_mine = lax.psum_scatter(col_term, "blk", scatter_dimension=0, tiled=True)
    return (loss, row_mine + col_mine)


def per_device(teacher, student):
    rows = teacher.shape[0]
    total = rows * lax.axis_size("blk") * lax.axis_size("inner")
    if total * (teacher.shape[1] + student.shape[1]) * 2 > GATHER_LIMIT:
        return per_device_tiled(teacher, student)
    all_t = lax.all_gather(teacher, AXES, axis=0, tiled=True)
    all_s = lax.all_gather(student, AXES, axis=0, tiled=True)
    gram_s, gram_t = tile_grams(teacher, student, all_t, all_s)
    sq_s = jnp.sum(gram_s * gram_s, 1)
    sq_t = jnp.sum(gram_t * gram_t, 1)
    cross = jnp.sum(gram_s * gram_t, 1)
    mine = jnp.stack(coefficients(sq_s, sq_t, cross, total))
    alpha, beta, terms = lax.all_gather(mine, AXES, axis=1, tiled=True)
    loss = jnp.sum(terms) / total
    row_w = mine[0][:, None] * gram_s - mine[1][:, None] * gram_t
    col_w = alpha[None, :] * gram_s - beta[None, :] * gram_t
    weights = jnp.concatenate([row_w, col_w]).astype(jnp.bfloat16)
    both = jnp.dot(weights, all_s, preferred_element_type=jnp.float32)
    return (loss, both[:rows] + both[rows:])


def solution(mesh):
    return jax.shard_map(
        per_device,
        mesh=mesh,
        in_specs=(P(AXES, None), P(AXES, None)),
        out_specs=(P(), P(AXES, None)),
        check_vma=False,
    )
```

```python
import math

import jax
import jax.numpy as jnp
from jax import lax
from jax.sharding import PartitionSpec as P

DS = 768
AXES = ("blk", "inner")


EPSILON = 1e-06


def coefficients(sq_student, sq_teacher, cross, total):
    norm_student = jnp.sqrt(sq_student + EPSILON)
    norm_teacher = jnp.sqrt(sq_teacher + EPSILON)
    factor = 2.0 * math.sqrt(total * DS) / total
    cubed = norm_student * norm_student * norm_student
    alpha = factor * (EPSILON / norm_student + cross / norm_teacher) / cubed
    beta = factor / (norm_student * norm_teacher)
    terms = (
        sq_student / (norm_student * norm_student)
        + sq_teacher / (norm_teacher * norm_teacher)
        - 2.0 * cross / (norm_student * norm_teacher)
    )
    return (alpha, beta, terms)


def span(masks):
    out = [0]
    for mask in masks:
        out += [mask ^ other for other in out]
    return out


def subgroups(blocks, inner):
    bits = [1 << b for b in range((inner - 1).bit_length())]
    bits += [inner << b for b in range(1, (blocks - 1).bit_length())]
    return (bits[0::2], bits[1::2] + [inner])


def send(value, mask, count):
    return lax.ppermute(value, AXES, [(i, i ^ mask) for i in range(count)])


def gather(own, masks, count):
    pieces = [own]
    for mask in masks:
        pieces += [send(piece, mask, count) for piece in pieces]
    return pieces


def tree_sum(values):
    while len(values) > 1:
        values = [values[i] + values[i + 1] for i in range(0, len(values), 2)]
    return values[0]


def group_sum(parts, masks, count):
    places = len(masks)
    values = [parts]
    for place, mask in enumerate(span(masks)):
        if place:
            got = send(parts, mask, count)
            order = [k ^ place for k in range(1 << places)]
            values.append(jnp.stack([got[:, k] for k in order], 1))
    return tree_sum(values)


def per_device(teacher, student):
    rows = teacher.shape[0]
    blocks = lax.axis_size("blk")
    inner = lax.axis_size("inner")
    count = blocks * inner
    total = rows * count
    row_masks, col_masks = subgroups(blocks, inner)
    n_row, n_col = 1 << len(row_masks), 1 << len(col_masks)

    row_t = gather(teacher, row_masks, count)
    col_t = gather(teacher, col_masks, count)
    row_s = gather(student, row_masks, count)
    col_s = gather(student, col_masks, count)
    row_t, col_t, row_s, col_s = map(jnp.concatenate, (row_t, col_t, row_s, col_s))

    gram_s = jnp.einsum("rd,cd->rc", row_s, col_s, preferred_element_type=jnp.float32)
    gram_t = jnp.einsum("rd,cd->rc", row_t, col_t, preferred_element_type=jnp.float32)
    products = (gram_s * gram_s, gram_t * gram_t, gram_s * gram_t)
    row_part = jnp.stack([jnp.sum(p, 1) for p in products]).reshape(3, n_row, rows)
    col_part = jnp.stack([jnp.sum(p, 0) for p in products]).reshape(3, n_col, rows)
    row_sum = group_sum(row_part, row_masks, count).reshape(3, -1)
    col_sum = group_sum(col_part, col_masks, count).reshape(3, -1)

    row_alpha, row_beta, _ = coefficients(*row_sum, total)
    col_alpha, col_beta, terms = coefficients(*col_sum, total)
    row_w = row_alpha[:, None] * gram_s - row_beta[:, None] * gram_t
    col_w = col_alpha[None, :] * gram_s - col_beta[None, :] * gram_t
    out = jnp.dot(row_w.astype(jnp.bfloat16), col_s, preferred_element_type=jnp.float32)
    out += jnp.dot(col_w.astype(jnp.bfloat16), col_s, preferred_element_type=jnp.float32)
    out = out.reshape(n_row, rows, -1)
    term = jnp.full((1, 128), jnp.sum(terms))

    grads, losses = [out[0]], [term]
    for place, mask in enumerate(span(row_masks)):
        if place:
            grads.append(send(out[place], mask, count))
            losses.append(send(term, mask, count))
    return (tree_sum(losses)[0, 0] / total, tree_sum(grads))


def solution(mesh):
    return jax.shard_map(
        per_device,
        mesh=mesh,
        in_specs=(P(AXES, None), P(AXES, None)),
        out_specs=(P(), P(AXES, None)),
        check_vma=False,
    )
```

```python
import math

import jax
import jax.numpy as jnp
from jax import lax
from jax.sharding import PartitionSpec as P

DS = 768
AXES = ("blk", "inner")


EPSILON = 1e-06


def coefficients(sq_student, sq_teacher, cross, total):
    norm_student = jnp.sqrt(sq_student + EPSILON)
    norm_teacher = jnp.sqrt(sq_teacher + EPSILON)
    factor = 2.0 * math.sqrt(total * DS) / total
    cubed = norm_student * norm_student * norm_student
    alpha = factor * (EPSILON / norm_student + cross / norm_teacher) / cubed
    beta = factor / (norm_student * norm_teacher)
    terms = (
        sq_student / (norm_student * norm_student)
        + sq_teacher / (norm_teacher * norm_teacher)
        - 2.0 * cross / (norm_student * norm_teacher)
    )
    return (alpha, beta, terms)


def span(masks):
    out = [0]
    for mask in masks:
        out += [mask ^ other for other in out]
    return out


def subgroups(blocks, inner):
    bits = [1 << b for b in range((inner - 1).bit_length())]
    bits += [inner << b for b in range(1, (blocks - 1).bit_length())]
    return (bits[0::2], bits[1::2] + [inner])


def send(value, mask, count):
    return lax.ppermute(value, AXES, [(i, i ^ mask) for i in range(count)])


def gather(own, masks, count):
    pieces = [own]
    for mask in masks:
        pieces += [send(piece, mask, count) for piece in pieces]
    return pieces


def after(value, other):
    return lax.optimization_barrier((value, other))[0]


def group_sum(parts, masks, count):
    for place, mask in enumerate(masks):
        got = send(parts, mask, count)
        shape = (3, -1, 2, 1 << place, got.shape[-1])
        got = jnp.flip(got.reshape(shape), 2).reshape(parts.shape)
        parts = parts + got
    return parts


def per_device(teacher, student):
    rows = teacher.shape[0]
    blocks = lax.axis_size("blk")
    inner = lax.axis_size("inner")
    count = blocks * inner
    total = rows * count
    row_masks, col_masks = subgroups(blocks, inner)
    n_row, n_col = 1 << len(row_masks), 1 << len(col_masks)

    row_t = gather(teacher, row_masks, count)
    col_t = gather(teacher, col_masks, count)
    student_late = after(student, (row_t[2], col_t[2]))
    row_s = gather(student_late, row_masks, count)
    col_s = gather(student_late, col_masks, count)
    row_t, col_t, row_s, col_s = map(jnp.concatenate, (row_t, col_t, row_s, col_s))

    gram_s = jnp.einsum("rd,cd->rc", row_s, col_s, preferred_element_type=jnp.float32)
    gram_t = jnp.einsum("rd,cd->rc", row_t, col_t, preferred_element_type=jnp.float32)
    products = (gram_s * gram_s, gram_t * gram_t, gram_s * gram_t)
    row_part = jnp.stack([jnp.sum(p, 1) for p in products]).reshape(3, n_row, rows)
    col_part = jnp.stack([jnp.sum(p, 0) for p in products]).reshape(3, n_col, rows)
    row_sum = group_sum(row_part, row_masks, count).reshape(3, -1)
    col_sum = group_sum(col_part, col_masks, count).reshape(3, -1)

    row_alpha, row_beta, _ = coefficients(*row_sum, total)
    col_alpha, col_beta, terms = coefficients(*col_sum, total)
    row_w = row_alpha[:, None] * gram_s - row_beta[:, None] * gram_t
    col_w = col_alpha[None, :] * gram_s - col_beta[None, :] * gram_t
    out = jnp.dot(row_w.astype(jnp.bfloat16), col_s, preferred_element_type=jnp.float32)
    out += jnp.dot(col_w.astype(jnp.bfloat16), col_s, preferred_element_type=jnp.float32)
    out = out.reshape(n_row, rows, -1)
    out = jnp.concatenate([out, jnp.full((n_row, 8, out.shape[2]), jnp.sum(terms))], 1)

    parts = [out[0]]
    for place, mask in enumerate(span(row_masks)):
        if place:
            parts.append(send(out[place], mask, count))
    while len(parts) > 1:
        parts = [parts[i] + parts[i + 1] for i in range(0, len(parts), 2)]
    return (parts[0][rows, 0] / total, parts[0][:rows])


def solution(mesh):
    return jax.shard_map(
        per_device,
        mesh=mesh,
        in_specs=(P(AXES, None), P(AXES, None)),
        out_specs=(P(), P(AXES, None)),
        check_vma=False,
    )
```

```python
import math

import jax
import jax.numpy as jnp
from jax import lax
from jax.sharding import PartitionSpec as P

DS = 768
AXES = ("blk", "inner")


EPSILON = 1e-06


def coefficients(sq_student, sq_teacher, cross, total):
    norm_student = jnp.sqrt(sq_student + EPSILON)
    norm_teacher = jnp.sqrt(sq_teacher + EPSILON)
    factor = 2.0 * math.sqrt(total * DS) / total
    cubed = norm_student * norm_student * norm_student
    alpha = factor * (EPSILON / norm_student + cross / norm_teacher) / cubed
    beta = factor / (norm_student * norm_teacher)
    terms = (
        sq_student / (norm_student * norm_student)
        + sq_teacher / (norm_teacher * norm_teacher)
        - 2.0 * cross / (norm_student * norm_teacher)
    )
    return (alpha, beta, terms)


def span(masks):
    out = [0]
    for mask in masks:
        out += [mask ^ other for other in out]
    return out


def subgroups(blocks, inner):
    bits = [1 << b for b in range((inner - 1).bit_length())]
    bits += [inner << b for b in range(1, (blocks - 1).bit_length())]
    return (bits[0::2], bits[1::2] + [inner])


def send(value, mask, count):
    return lax.ppermute(value, AXES, [(i, i ^ mask) for i in range(count)])


def after(value, other):
    return lax.optimization_barrier((value, other))[0]


def forward(pieces, masks, level, count):
    for place in range(1 << len(masks)):
        if place.bit_count() == level and place not in pieces:
            top = place.bit_length() - 1
            pieces[place] = send(pieces[place ^ (1 << top)], masks[top], count)


def gather(teacher, student, row_masks, col_masks, count):
    *plane_masks, core_mask = col_masks
    row_t, col_t = {0: teacher}, {0: teacher}
    row_s, col_s = {0: student}, {0: student}
    core_t, core_s = [], []
    sides = ((row_t, row_s, row_masks), (col_t, col_s, plane_masks))
    for side_t, _, masks in sides:
        for b, mask in enumerate(masks):
            side_t[1 << b] = send(teacher, mask, count)
    late = after(student, (row_t[2], col_t[2]))
    for _, side_s, masks in sides:
        for b, mask in enumerate(masks):
            if b:
                side_s[1 << b] = send(late, mask, count)
    late = after(student, (row_s[2], col_s[2]))
    for _, side_s, masks in sides:
        side_s[1] = send(late, masks[0], count)

    early = (row_s[2], col_s[2])
    for row, col, core in ((row_t, col_t, core_t), (row_s, col_s, core_s)):
        row[1], col[1] = after((row[1], col[1]), early)
        for level in range(1, len(row_masks) + 1):
            if level > 1:
                forward(row, row_masks, level, count)
                forward(col, plane_masks, level, count)
            ready = [p for p in range(1 << len(plane_masks)) if max(p.bit_count(), 1) == level]
            if ready:
                got = send(jnp.concatenate([col[p] for p in ready]), core_mask, count)
                core += zip(ready, jnp.split(got, len(ready)))
                if level == 1:
                    early = (early, got)
    out = []
    for row, col, core in ((row_t, col_t, core_t), (row_s, col_s, core_s)):
        col = [col[p] for p in sorted(col)] + [piece for _, piece in sorted(core, key=lambda c: c[0])]
        out.append((jnp.concatenate([row[p] for p in sorted(row)]), jnp.concatenate(col)))
    return out


def tree_sum(values):
    while len(values) > 1:
        values = [values[i] + values[i + 1] for i in range(0, len(values), 2)]
    return values[0]


def group_sum(parts, masks, count):
    for place, mask in enumerate(masks):
        got = send(parts, mask, count)
        shape = (3, -1, 2, 1 << place, got.shape[-1])
        got = jnp.flip(got.reshape(shape), 2).reshape(parts.shape)
        parts = parts + got
    return parts


def per_device(teacher, student):
    rows = teacher.shape[0]
    blocks = lax.axis_size("blk")
    inner = lax.axis_size("inner")
    count = blocks * inner
    total = rows * count
    row_masks, col_masks = subgroups(blocks, inner)
    n_row, n_col = 1 << len(row_masks), 1 << len(col_masks)

    (row_t, col_t), (row_s, col_s) = gather(teacher, student, row_masks, col_masks, count)

    gram_s = jnp.einsum("rd,cd->rc", row_s, col_s, preferred_element_type=jnp.float32)
    gram_t = jnp.einsum("rd,cd->rc", row_t, col_t, preferred_element_type=jnp.float32)
    products = (gram_s * gram_s, gram_t * gram_t, gram_s * gram_t)
    row_part = jnp.stack([jnp.sum(p, 1) for p in products]).reshape(3, n_row, rows)
    col_part = jnp.stack([jnp.sum(p, 0) for p in products]).reshape(3, n_col, rows)
    row_sum = group_sum(row_part, row_masks, count).reshape(3, -1)
    col_sum = group_sum(col_part, col_masks, count).reshape(3, -1)

    row_alpha, row_beta, _ = coefficients(*row_sum, total)
    col_alpha, col_beta, terms = coefficients(*col_sum, total)
    row_w = row_alpha[:, None] * gram_s - row_beta[:, None] * gram_t
    col_w = col_alpha[None, :] * gram_s - col_beta[None, :] * gram_t
    out = jnp.dot(row_w.astype(jnp.bfloat16), col_s, preferred_element_type=jnp.float32)
    out += jnp.dot(col_w.astype(jnp.bfloat16), col_s, preferred_element_type=jnp.float32)
    out = jnp.split(out, n_row)
    places = [(place, mask) for place, mask in enumerate(span(row_masks)) if place]
    grads = out[:1] + [send(out[place], mask, count) for place, mask in places]
    term = after(jnp.full((1, 128), jnp.sum(terms)), grads[2])
    losses = [term] + [send(term, mask, count) for _, mask in places]
    return (tree_sum(losses)[0, 0] / total, tree_sum(grads))


def solution(mesh):
    return jax.shard_map(
        per_device,
        mesh=mesh,
        in_specs=(P(AXES, None), P(AXES, None)),
        out_specs=(P(), P(AXES, None)),
        check_vma=False,
    )
```

```python
import math

import jax
import jax.numpy as jnp
from jax import lax
from jax.sharding import PartitionSpec as P

DS = 768
AXES = ("blk", "inner")


EPSILON = 1e-06


def coefficients(sq_student, sq_teacher, cross, total):
    norm_student = jnp.sqrt(sq_student + EPSILON)
    norm_teacher = jnp.sqrt(sq_teacher + EPSILON)
    factor = 2.0 * math.sqrt(total * DS) / total
    cubed = norm_student * norm_student * norm_student
    alpha = factor * (EPSILON / norm_student + cross / norm_teacher) / cubed
    beta = factor / (norm_student * norm_teacher)
    terms = (
        sq_student / (norm_student * norm_student)
        + sq_teacher / (norm_teacher * norm_teacher)
        - 2.0 * cross / (norm_student * norm_teacher)
    )
    return (alpha, beta, terms)


def span(masks):
    out = [0]
    for mask in masks:
        out += [mask ^ other for other in out]
    return out


def subgroups(blocks, inner):
    bits = [1 << b for b in range((inner - 1).bit_length())]
    bits += [inner << b for b in range(1, (blocks - 1).bit_length())]
    return (bits[0::2], bits[1::2] + [inner])


def send(value, mask, count):
    return lax.ppermute(value, AXES, [(i, i ^ mask) for i in range(count)])


def after(value, other):
    return lax.optimization_barrier((value, other))[0]


def forward(pieces, masks, level, count):
    for place in range(1 << len(masks)):
        if place.bit_count() == level and place not in pieces:
            top = place.bit_length() - 1
            pieces[place] = send(pieces[place ^ (1 << top)], masks[top], count)


def gather(teacher, student, row_masks, col_masks, count):
    *plane_masks, core_mask = col_masks
    row_t, col_t = {0: teacher}, {0: teacher}
    row_s, col_s = {0: student}, {0: student}
    core_t, core_s = [], []
    width = teacher.shape[1]
    both = jnp.concatenate([teacher, student], 1)
    row_t[1], col_t[1] = send(teacher, row_masks[0], count), send(teacher, plane_masks[0], count)
    for side_t, side_s, masks in ((row_t, row_s, row_masks), (col_t, col_s, plane_masks)):
        for b, mask in enumerate(masks):
            if b:
                got = send(both, mask, count)
                side_t[1 << b], side_s[1 << b] = got[:, :width], got[:, width:]
    col_s[1] = send(student, plane_masks[0], count)
    row_t[1], col_t[1], late = lax.optimization_barrier((row_t[1], col_t[1], student))
    row_s[1] = send(late, row_masks[0], count)
    early = (row_t[2], col_t[2], row_s[2], col_s[2])

    for row, col, core in ((row_t, col_t, core_t), (row_s, col_s, core_s)):
        row[1], col[1] = after((row[1], col[1]), early)
        for level in range(1, len(row_masks) + 1):
            if level > 1:
                forward(row, row_masks, level, count)
                forward(col, plane_masks, level, count)
            ready = [p for p in range(1 << len(plane_masks)) if max(p.bit_count(), 1) == level]
            if ready:
                got = send(jnp.concatenate([col[p] for p in ready]), core_mask, count)
                core += zip(ready, jnp.split(got, len(ready)))
                if level == 1:
                    early = got
    out = []
    for row, col, core in ((row_t, col_t, core_t), (row_s, col_s, core_s)):
        col = [col[p] for p in sorted(col)] + [piece for _, piece in sorted(core, key=lambda c: c[0])]
        out.append((jnp.concatenate([row[p] for p in sorted(row)]), jnp.concatenate(col)))
    return out


def tree_sum(values):
    while len(values) > 1:
        values = [values[i] + values[i + 1] for i in range(0, len(values), 2)]
    return values[0]


def add_partner(parts, masks, place, count):
    got = send(parts, masks[place], count)
    shape = (3, -1, 2, 1 << place, got.shape[-1])
    return parts + jnp.flip(got.reshape(shape), 2).reshape(parts.shape)


def per_device(teacher, student):
    rows = teacher.shape[0]
    blocks = lax.axis_size("blk")
    inner = lax.axis_size("inner")
    count = blocks * inner
    total = rows * count
    row_masks, col_masks = subgroups(blocks, inner)
    n_row, n_col = 1 << len(row_masks), 1 << len(col_masks)

    (row_t, col_t), (row_s, col_s) = gather(teacher, student, row_masks, col_masks, count)

    gram_s = jnp.einsum("rd,cd->rc", row_s, col_s, preferred_element_type=jnp.float32)
    gram_t = jnp.einsum("rd,cd->rc", row_t, col_t, preferred_element_type=jnp.float32)
    products = (gram_s * gram_s, gram_t * gram_t, gram_s * gram_t)
    row_part = jnp.stack([jnp.sum(p, 1) for p in products]).reshape(3, n_row, rows)
    col_part = jnp.stack([jnp.sum(p, 0) for p in products]).reshape(3, n_col, rows)
    for place in range(max(len(row_masks), len(col_masks))):
        if place < len(col_masks):
            col_part = add_partner(col_part, col_masks, place, count)
        if place < len(row_masks):
            row_part = add_partner(row_part, row_masks, place, count)
            row_part, col_part = lax.optimization_barrier((row_part, col_part))
    row_sum, col_sum = row_part.reshape(3, -1), col_part.reshape(3, -1)

    row_alpha, row_beta, _ = coefficients(*row_sum, total)
    col_alpha, col_beta, terms = coefficients(*col_sum, total)
    row_w = row_alpha[:, None] * gram_s - row_beta[:, None] * gram_t
    col_w = col_alpha[None, :] * gram_s - col_beta[None, :] * gram_t
    out = jnp.dot(row_w.astype(jnp.bfloat16), col_s, preferred_element_type=jnp.float32)
    out += jnp.dot(col_w.astype(jnp.bfloat16), col_s, preferred_element_type=jnp.float32)
    out = jnp.split(out, n_row)
    places = [(place, mask) for place, mask in enumerate(span(row_masks)) if place]
    grads = out[:1] + [send(out[place], mask, count) for place, mask in places]
    term = after(jnp.full((1, 128), jnp.sum(terms)), grads[2])
    losses = [term] + [send(term, mask, count) for _, mask in places]
    return (tree_sum(losses)[0, 0] / total, tree_sum(grads))


def solution(mesh):
    return jax.shard_map(
        per_device,
        mesh=mesh,
        in_specs=(P(AXES, None), P(AXES, None)),
        out_specs=(P(), P(AXES, None)),
        check_vma=False,
    )
```

```python
import math

import jax
import jax.numpy as jnp
from jax import lax
from jax.sharding import PartitionSpec as P

DS = 768
AXES = ("blk", "inner")


EPSILON = 1e-06


def coefficients(sq_student, sq_teacher, cross, total):
    norm_student = jnp.sqrt(sq_student + EPSILON)
    norm_teacher = jnp.sqrt(sq_teacher + EPSILON)
    factor = 2.0 * math.sqrt(total * DS) / total
    cubed = norm_student * norm_student * norm_student
    alpha = factor * (EPSILON / norm_student + cross / norm_teacher) / cubed
    beta = factor / (norm_student * norm_teacher)
    terms = (
        sq_student / (norm_student * norm_student)
        + sq_teacher / (norm_teacher * norm_teacher)
        - 2.0 * cross / (norm_student * norm_teacher)
    )
    return (alpha, beta, terms)


def span(masks):
    out = [0]
    for mask in masks:
        out += [mask ^ other for other in out]
    return out


def subgroups(blocks, inner):
    bits = [1 << b for b in range((inner - 1).bit_length())]
    bits += [inner << b for b in range(1, (blocks - 1).bit_length())]
    return (bits[0::2], bits[1::2] + [inner])


def send(value, mask, count):
    return lax.ppermute(value, AXES, [(i, i ^ mask) for i in range(count)])


def after(value, other):
    return lax.optimization_barrier((value, other))[0]


def forward(pieces, masks, level, count):
    for place in range(1 << len(masks)):
        if place.bit_count() == level and place not in pieces:
            top = place.bit_length() - 1
            pieces[place] = send(pieces[place ^ (1 << top)], masks[top], count)


def gather(teacher, student, row_masks, col_masks, count):
    *plane_masks, core_mask = col_masks
    row_t, col_t = {0: teacher}, {0: teacher}
    row_s, col_s = {0: student}, {0: student}
    core_t, core_s = [], []
    width = teacher.shape[1]
    core_s.append((0, send(student, core_mask, count)))
    both = after(jnp.concatenate([teacher, student], 1), core_s[0])
    row_t[1], col_t[1] = send(teacher, row_masks[0], count), send(teacher, plane_masks[0], count)
    for side_t, side_s, masks in ((row_t, row_s, row_masks), (col_t, col_s, plane_masks)):
        for b, mask in enumerate(masks):
            if b:
                got = send(both, mask, count)
                side_t[1 << b], side_s[1 << b] = got[:, :width], got[:, width:]
    col_s[1] = send(student, plane_masks[0], count)
    row_t[1], col_t[1], late = lax.optimization_barrier((row_t[1], col_t[1], student))
    row_s[1] = send(late, row_masks[0], count)
    early = (row_t[2], col_t[2], row_s[2], col_s[2])

    for row, col, core in ((row_t, col_t, core_t), (row_s, col_s, core_s)):
        row[1], col[1] = after((row[1], col[1]), early)
        for level in range(1, len(row_masks) + 1):
            if level > 1:
                forward(row, row_masks, level, count)
                forward(col, plane_masks, level, count)
            ready = [p for p in range(1 << len(plane_masks)) if max(p.bit_count(), 1) == level]
            ready = [p for p in ready if p or core is core_t]
            if ready:
                got = send(jnp.concatenate([col[p] for p in ready]), core_mask, count)
                core += zip(ready, jnp.split(got, len(ready)))
                if level == 1:
                    early = got
    out = []
    for row, col, core in ((row_t, col_t, core_t), (row_s, col_s, core_s)):
        col = [col[p] for p in sorted(col)] + [piece for _, piece in sorted(core, key=lambda c: c[0])]
        out.append((jnp.concatenate([row[p] for p in sorted(row)]), jnp.concatenate(col)))
    return out


def tree_sum(values):
    while len(values) > 1:
        values = [values[i] + values[i + 1] for i in range(0, len(values), 2)]
    return values[0]


def add_partner(parts, masks, place, count):
    got = send(parts, masks[place], count)
    shape = (3, -1, 2, 1 << place, got.shape[-1])
    return parts + jnp.flip(got.reshape(shape), 2).reshape(parts.shape)


def per_device(teacher, student):
    rows = teacher.shape[0]
    blocks = lax.axis_size("blk")
    inner = lax.axis_size("inner")
    count = blocks * inner
    total = rows * count
    row_masks, col_masks = subgroups(blocks, inner)
    n_row, n_col = 1 << len(row_masks), 1 << len(col_masks)

    (row_t, col_t), (row_s, col_s) = gather(teacher, student, row_masks, col_masks, count)

    gram_s = jnp.einsum("rd,cd->rc", row_s, col_s, preferred_element_type=jnp.float32)
    gram_t = jnp.einsum("rd,cd->rc", row_t, col_t, preferred_element_type=jnp.float32)
    products = (gram_s * gram_s, gram_t * gram_t, gram_s * gram_t)
    row_part = jnp.stack([jnp.sum(p, 1) for p in products]).reshape(3, n_row, rows)
    col_part = jnp.stack([jnp.sum(p, 0) for p in products]).reshape(3, n_col, rows)
    for place in range(max(len(row_masks), len(col_masks))):
        if place < len(col_masks):
            col_part = add_partner(col_part, col_masks, place, count)
        if place < len(row_masks):
            row_part = after(add_partner(row_part, row_masks, place, count), col_part)
    row_sum, col_sum = row_part.reshape(3, -1), col_part.reshape(3, -1)

    row_alpha, row_beta, _ = coefficients(*row_sum, total)
    col_alpha, col_beta, terms = coefficients(*col_sum, total)
    row_w = row_alpha[:, None] * gram_s - row_beta[:, None] * gram_t
    col_w = col_alpha[None, :] * gram_s - col_beta[None, :] * gram_t
    out = jnp.dot(row_w.astype(jnp.bfloat16), col_s, preferred_element_type=jnp.float32)
    out += jnp.dot(col_w.astype(jnp.bfloat16), col_s, preferred_element_type=jnp.float32)
    out = jnp.split(out, n_row)
    places = [(place, mask) for place, mask in enumerate(span(row_masks)) if place]
    grads = out[:1] + [send(out[place], mask, count) for place, mask in places]
    term = after(jnp.full((1, 128), jnp.sum(terms)), grads[2])
    losses = [term] + [send(term, mask, count) for _, mask in places]
    return (tree_sum(losses)[0, 0] / total, tree_sum(grads))


def solution(mesh):
    return jax.shard_map(
        per_device,
        mesh=mesh,
        in_specs=(P(AXES, None), P(AXES, None)),
        out_specs=(P(), P(AXES, None)),
        check_vma=False,
    )
```

```python
import functools
import math

import jax
import jax.numpy as jnp
from jax import lax
from jax.experimental import pallas as pl
from jax.experimental.pallas import tpu as pltpu
from jax.sharding import PartitionSpec as P

DS = 768
AXES = ("blk", "inner")
VMEM = 48 * 2**20
SHARE_SCALE = 8.0


EPSILON = 1e-06


def coefficients(sq_student, sq_teacher, cross, total):
    norm_student = jnp.sqrt(sq_student + EPSILON)
    norm_teacher = jnp.sqrt(sq_teacher + EPSILON)
    factor = 2.0 * math.sqrt(total * DS) / total
    cubed = norm_student * norm_student * norm_student
    alpha = factor * (EPSILON / norm_student + cross / norm_teacher) / cubed
    beta = factor / (norm_student * norm_teacher)
    terms = (
        sq_student / (norm_student * norm_student)
        + sq_teacher / (norm_teacher * norm_teacher)
        - 2.0 * cross / (norm_student * norm_teacher)
    )
    return (alpha, beta, terms)


def span(masks):
    out = [0]
    for mask in masks:
        out += [mask ^ other for other in out]
    return out


def subgroups(blocks, inner):
    bits = [1 << b for b in range((inner - 1).bit_length())]
    bits += [inner << b for b in range(1, (blocks - 1).bit_length())]
    return (bits[0::2], bits[1::2] + [inner])


def send(value, mask, count):
    return lax.ppermute(value, AXES, [(i, i ^ mask) for i in range(count)])


def after(value, other):
    return lax.optimization_barrier((value, other))[0]


def forward(pieces, masks, level, count):
    for place in range(1 << len(masks)):
        if place.bit_count() == level and place not in pieces:
            top = place.bit_length() - 1
            pieces[place] = send(pieces[place ^ (1 << top)], masks[top], count)


def gather(teacher, student, row_masks, col_masks, count):
    *plane_masks, core_mask = col_masks
    row_t, col_t = {0: teacher}, {0: teacher}
    row_s, col_s = {0: student}, {0: student}
    core_t, core_s = [], []
    width = teacher.shape[1]
    core_s.append((0, send(student, core_mask, count)))
    both = after(jnp.concatenate([teacher, student], 1), core_s[0])
    row_t[1], col_t[1] = send(teacher, row_masks[0], count), send(teacher, plane_masks[0], count)
    for side_t, side_s, masks in ((row_t, row_s, row_masks), (col_t, col_s, plane_masks)):
        for b, mask in enumerate(masks):
            if b:
                got = send(both, mask, count)
                side_t[1 << b], side_s[1 << b] = got[:, :width], got[:, width:]
    col_s[1] = send(after(student, core_s[0]), plane_masks[0], count)
    row_t[1], col_t[1], late = lax.optimization_barrier((row_t[1], col_t[1], student))
    row_s[1] = send(late, row_masks[0], count)
    early = (row_t[2], col_t[2], row_s[2], col_s[2])

    for row, col, core in ((row_t, col_t, core_t), (row_s, col_s, core_s)):
        row[1], col[1] = after((row[1], col[1]), early)
        for level in range(1, len(row_masks) + 1):
            if level > 1:
                forward(row, row_masks, level, count)
                forward(col, plane_masks, level, count)
            ready = [p for p in range(1 << len(plane_masks)) if max(p.bit_count(), 1) == level]
            ready = [p for p in ready if p or core is core_t]
            if ready:
                got = send(jnp.concatenate([col[p] for p in ready]), core_mask, count)
                core += zip(ready, jnp.split(got, len(ready)))
                if level == 1:
                    early = got
    out = []
    for row, col, core in ((row_t, col_t, core_t), (row_s, col_s, core_s)):
        col = [col[p] for p in sorted(col)] + [piece for _, piece in sorted(core, key=lambda c: c[0])]
        out.append((jnp.concatenate([row[p] for p in sorted(row)]), jnp.concatenate(col)))
    return out


def tree_sum(values):
    while len(values) > 1:
        values = [values[i] + values[i + 1] for i in range(0, len(values), 2)]
    return values[0]


def output_kernel(n_row, total, gram_s, gram_t, row_sum, col_sum, col_s, own, share, *pieces):
    row_alpha, row_beta, _ = coefficients(*(row_sum[k] for k in range(3)), total)
    col_alpha, col_beta, terms = coefficients(*(col_sum[k] for k in range(3)), total)
    row_ab = jnp.transpose(jnp.concatenate([row_alpha, row_beta] * 4))
    row_w = row_ab[:, 0:1] * gram_s[...] - row_ab[:, 1:2] * gram_t[...]
    col_w = col_alpha * gram_s[...] - col_beta * gram_t[...]
    out = jnp.dot(row_w.astype(jnp.bfloat16), col_s[...], preferred_element_type=jnp.float32)
    out += jnp.dot(col_w.astype(jnp.bfloat16), col_s[...], preferred_element_type=jnp.float32)

    rows, width = own.shape
    own[...] = out[:rows]
    term = jnp.sum(terms, axis=1, keepdims=True)
    share[...] = jnp.broadcast_to(term, share.shape)
    largest = jnp.max(jnp.max(jnp.abs(out), axis=0, keepdims=True), axis=1, keepdims=True)
    power = jnp.clip(jnp.floor(jnp.log2(largest)), -100.0, 100.0)
    term = term * SHARE_SCALE
    high = term.astype(jnp.bfloat16).astype(jnp.float32)
    middle = (term - high).astype(jnp.bfloat16).astype(jnp.float32)
    low = term - high - middle
    lane = lax.broadcasted_iota(jnp.int32, (rows, 128), 1)
    extra = jnp.where(lane == 0, power, jnp.where(lane == 1, high, jnp.where(lane == 2, middle, low)))
    scaled = out * jnp.exp2(13.0 - power)
    for k, piece in enumerate(pieces):
        piece[:, :width] = scaled[(k + 1) * rows : (k + 2) * rows]
        piece[:, width:] = extra


def final_kernel(total, own, share, *refs):
    *pieces, grad, loss = refs
    width = own.shape[1]
    grads, terms = [own[...]], [share[0:1, 0:1]]
    for piece in pieces:
        extra = piece[:, width:]
        grads.append(piece[:, :width] * jnp.exp2(extra[:, 0:1] - 13.0))
        terms.append((extra[0:1, 1:2] + extra[0:1, 2:3] + extra[0:1, 3:4]) * (1.0 / SHARE_SCALE))
    grad[...] = tree_sum(grads)
    loss[...] = tree_sum(terms) * (1.0 / total)


def add_partner(parts, masks, place, count):
    got = send(parts, masks[place], count)
    shape = (3, -1, 2, 1 << place, got.shape[-1])
    return parts + jnp.flip(got.reshape(shape), 2).reshape(parts.shape)


def per_device(teacher, student):
    rows = teacher.shape[0]
    blocks = lax.axis_size("blk")
    inner = lax.axis_size("inner")
    count = blocks * inner
    total = rows * count
    row_masks, col_masks = subgroups(blocks, inner)
    n_row, n_col = 1 << len(row_masks), 1 << len(col_masks)

    (row_t, col_t), (row_s, col_s) = gather(teacher, student, row_masks, col_masks, count)

    gram_s = jnp.einsum("rd,cd->rc", row_s, col_s, preferred_element_type=jnp.float32)
    gram_t = jnp.einsum("rd,cd->rc", row_t, col_t, preferred_element_type=jnp.float32)
    products = (gram_s * gram_s, gram_t * gram_t, gram_s * gram_t)
    row_part = jnp.stack([jnp.sum(p, 1) for p in products]).reshape(3, n_row, rows)
    col_part = jnp.stack([jnp.sum(p, 0) for p in products]).reshape(3, n_col, rows)
    for place in range(max(len(row_masks), len(col_masks))):
        if place < len(col_masks):
            col_part = add_partner(col_part, col_masks, place, count)
        if place < len(row_masks):
            row_part = after(add_partner(row_part, row_masks, place, count), col_part)
    row_sum, col_sum = row_part.reshape(3, 1, -1), col_part.reshape(3, 1, -1)

    width = student.shape[1]
    piece = jax.ShapeDtypeStruct((rows, width + 128), jnp.float32)
    own, share, *pieces = pl.pallas_call(
        functools.partial(output_kernel, n_row, total),
        out_shape=[
            jax.ShapeDtypeStruct((rows, width), jnp.float32),
            jax.ShapeDtypeStruct((8, 128), jnp.float32),
        ]
        + [piece] * (n_row - 1),
        compiler_params=pltpu.CompilerParams(vmem_limit_bytes=VMEM),
    )(gram_s, gram_t, row_sum, col_sum, col_s)
    got = [
        send(value.astype(jnp.float16), mask, count).astype(jnp.float32)
        for value, mask in zip(pieces, span(row_masks)[1:])
    ]
    grad, loss = pl.pallas_call(
        functools.partial(final_kernel, total),
        out_shape=[jax.ShapeDtypeStruct((rows, width), jnp.float32), jax.ShapeDtypeStruct((1, 1), jnp.float32)],
        compiler_params=pltpu.CompilerParams(vmem_limit_bytes=VMEM),
    )(own, share, *got)
    return (loss[0, 0], grad)


def solution(mesh):
    return jax.shard_map(
        per_device,
        mesh=mesh,
        in_specs=(P(AXES, None), P(AXES, None)),
        out_specs=(P(), P(AXES, None)),
        check_vma=False,
    )
```

```python
import functools
import math

import jax
import jax.numpy as jnp
from jax import lax
from jax.experimental import pallas as pl
from jax.experimental.pallas import tpu as pltpu
from jax.sharding import PartitionSpec as P

DS = 768
AXES = ("blk", "inner")
VMEM = 48 * 2**20
SHARE_SCALE = 8.0


EPSILON = 1e-06


def coefficients(sq_student, sq_teacher, cross, total):
    norm_student = jnp.sqrt(sq_student + EPSILON)
    norm_teacher = jnp.sqrt(sq_teacher + EPSILON)
    factor = 2.0 * math.sqrt(total * DS) / total
    cubed = norm_student * norm_student * norm_student
    alpha = factor * (EPSILON / norm_student + cross / norm_teacher) / cubed
    beta = factor / (norm_student * norm_teacher)
    terms = (
        sq_student / (norm_student * norm_student)
        + sq_teacher / (norm_teacher * norm_teacher)
        - 2.0 * cross / (norm_student * norm_teacher)
    )
    return (alpha, beta, terms)


def span(masks):
    out = [0]
    for mask in masks:
        out += [mask ^ other for other in out]
    return out


def subgroups(blocks, inner):
    bits = [1 << b for b in range((inner - 1).bit_length())]
    bits += [inner << b for b in range(1, (blocks - 1).bit_length())]
    return (bits[0::2], bits[1::2] + [inner])


def send(value, mask, count):
    return lax.ppermute(value, AXES, [(i, i ^ mask) for i in range(count)])


def after(value, other):
    return lax.optimization_barrier((value, other))[0]


def forward(pieces, masks, level, count):
    for place in range(1 << len(masks)):
        if place.bit_count() == level and place not in pieces:
            top = place.bit_length() - 1
            pieces[place] = send(pieces[place ^ (1 << top)], masks[top], count)


def gather(teacher, student, row_masks, col_masks, count):
    *plane_masks, core_mask = col_masks
    row_t, col_t = {0: teacher}, {0: teacher}
    row_s, col_s = {0: student}, {0: student}
    core_t, core_s = {}, {}
    width = teacher.shape[1]
    sides = ((row_t, row_s, row_masks), (col_t, col_s, plane_masks))

    def to_core(places):
        got = send(jnp.concatenate([col[p] for col, _, p in places], 1), core_mask, count)
        start = 0
        for col, core, p in places:
            end = start + col[p].shape[1]
            core[p] = got[:, start:end]
            start = end

    col_s[1], row_s[1] = send(student, plane_masks[0], count), send(student, row_masks[0], count)
    core_s[0] = send(student, core_mask, count)
    col_t[1], row_t[1] = send(teacher, plane_masks[0], count), send(teacher, row_masks[0], count)
    both = after(jnp.concatenate([teacher, student], 1), (row_s[1], col_s[1], core_s[0]))
    arrived = []
    for side_t, side_s, masks in sides:
        for b, mask in enumerate(masks):
            if b:
                got = send(both, mask, count)
                side_t[1 << b], side_s[1 << b] = got[:, :width], got[:, width:]
                arrived.append(got)
    others = [1 << b for b in range(1, len(plane_masks))]
    to_core([(col_t, core_t, p) for p in [0] + others] + [(col_s, core_s, p) for p in [1] + others])
    for level in range(2, len(row_masks) + 1):
        forward(row_s, row_masks, level, count)
        forward(col_s, plane_masks, level, count)
    row_t[1], col_t[1] = after((row_t[1], col_t[1]), arrived)
    rest = [p for p in range(1 << len(plane_masks)) if p.bit_count() > 1]
    to_core([(col_t, core_t, 1)] + [(col_s, core_s, p) for p in rest])
    for level in range(2, len(row_masks) + 1):
        forward(row_t, row_masks, level, count)
        forward(col_t, plane_masks, level, count)
    to_core([(col_t, core_t, p) for p in rest])
    out = []
    for row, col, core in ((row_t, col_t, core_t), (row_s, col_s, core_s)):
        col = [col[p] for p in sorted(col)] + [core[p] for p in sorted(core)]
        out.append((jnp.concatenate([row[p] for p in sorted(row)]), jnp.concatenate(col)))
    return out


def tree_sum(values):
    while len(values) > 1:
        values = [values[i] + values[i + 1] for i in range(0, len(values), 2)]
    return values[0]


def output_kernel(n_row, total, gram_s, gram_t, row_sum, col_sum, col_s, own, share, *pieces):
    row_alpha, row_beta, _ = coefficients(*(row_sum[k] for k in range(3)), total)
    col_alpha, col_beta, terms = coefficients(*(col_sum[k] for k in range(3)), total)
    row_ab = jnp.transpose(jnp.concatenate([row_alpha, row_beta] * 4))
    row_w = row_ab[:, 0:1] * gram_s[...] - row_ab[:, 1:2] * gram_t[...]
    col_w = col_alpha * gram_s[...] - col_beta * gram_t[...]
    out = jnp.dot(row_w.astype(jnp.bfloat16), col_s[...], preferred_element_type=jnp.float32)
    out += jnp.dot(col_w.astype(jnp.bfloat16), col_s[...], preferred_element_type=jnp.float32)

    rows, width = own.shape
    own[...] = out[:rows]
    term = jnp.sum(terms, axis=1, keepdims=True)
    share[...] = jnp.broadcast_to(term, share.shape)
    largest = jnp.max(jnp.max(jnp.abs(out), axis=0, keepdims=True), axis=1, keepdims=True)
    power = jnp.clip(jnp.floor(jnp.log2(largest)), -100.0, 100.0)
    term = term * SHARE_SCALE
    high = term.astype(jnp.bfloat16).astype(jnp.float32)
    middle = (term - high).astype(jnp.bfloat16).astype(jnp.float32)
    low = term - high - middle
    lane = lax.broadcasted_iota(jnp.int32, (rows, 128), 1)
    extra = jnp.where(lane == 0, power, jnp.where(lane == 1, high, jnp.where(lane == 2, middle, low)))
    scaled = out * jnp.exp2(13.0 - power)
    for k, piece in enumerate(pieces):
        piece[:, :width] = scaled[(k + 1) * rows : (k + 2) * rows]
        piece[:, width:] = extra


def final_kernel(total, own, share, *refs):
    *pieces, grad, loss = refs
    width = own.shape[1]
    grads, terms = [own[...]], [share[0:1, 0:1]]
    for piece in pieces:
        extra = piece[:, width:]
        grads.append(piece[:, :width] * jnp.exp2(extra[:, 0:1] - 13.0))
        terms.append((extra[0:1, 1:2] + extra[0:1, 2:3] + extra[0:1, 3:4]) * (1.0 / SHARE_SCALE))
    grad[...] = tree_sum(grads)
    loss[...] = tree_sum(terms) * (1.0 / total)


def add_partner(parts, masks, place, count):
    got = send(parts, masks[place], count)
    shape = (3, -1, 2, 1 << place, got.shape[-1])
    return parts + jnp.flip(got.reshape(shape), 2).reshape(parts.shape)


def per_device(teacher, student):
    rows = teacher.shape[0]
    blocks = lax.axis_size("blk")
    inner = lax.axis_size("inner")
    count = blocks * inner
    total = rows * count
    row_masks, col_masks = subgroups(blocks, inner)
    n_row, n_col = 1 << len(row_masks), 1 << len(col_masks)

    (row_t, col_t), (row_s, col_s) = gather(teacher, student, row_masks, col_masks, count)

    gram_s = jnp.einsum("rd,cd->rc", row_s, col_s, preferred_element_type=jnp.float32)
    gram_t = jnp.einsum("rd,cd->rc", row_t, col_t, preferred_element_type=jnp.float32)
    products = (gram_s * gram_s, gram_t * gram_t, gram_s * gram_t)
    row_part = jnp.stack([jnp.sum(p, 1) for p in products]).reshape(3, n_row, rows)
    col_part = jnp.stack([jnp.sum(p, 0) for p in products]).reshape(3, n_col, rows)
    for place in range(max(len(row_masks), len(col_masks))):
        if place < len(col_masks):
            col_part = add_partner(col_part, col_masks, place, count)
        if place < len(row_masks):
            row_part = after(add_partner(row_part, row_masks, place, count), col_part)
    row_sum, col_sum = row_part.reshape(3, 1, -1), col_part.reshape(3, 1, -1)

    width = student.shape[1]
    piece = jax.ShapeDtypeStruct((rows, width + 128), jnp.float32)
    own, share, *pieces = pl.pallas_call(
        functools.partial(output_kernel, n_row, total),
        out_shape=[
            jax.ShapeDtypeStruct((rows, width), jnp.float32),
            jax.ShapeDtypeStruct((8, 128), jnp.float32),
        ]
        + [piece] * (n_row - 1),
        compiler_params=pltpu.CompilerParams(vmem_limit_bytes=VMEM),
    )(gram_s, gram_t, row_sum, col_sum, col_s)
    got = [
        send(value.astype(jnp.float16), mask, count).astype(jnp.float32)
        for value, mask in zip(pieces, span(row_masks)[1:])
    ]
    grad, loss = pl.pallas_call(
        functools.partial(final_kernel, total),
        out_shape=[jax.ShapeDtypeStruct((rows, width), jnp.float32), jax.ShapeDtypeStruct((1, 1), jnp.float32)],
        compiler_params=pltpu.CompilerParams(vmem_limit_bytes=VMEM),
    )(own, share, *got)
    return (loss[0, 0], grad)


def solution(mesh):
    return jax.shard_map(
        per_device,
        mesh=mesh,
        in_specs=(P(AXES, None), P(AXES, None)),
        out_specs=(P(), P(AXES, None)),
        check_vma=False,
    )
```

```python
import functools
import math

import jax
import jax.numpy as jnp
from jax import lax
from jax.experimental import pallas as pl
from jax.experimental.pallas import tpu as pltpu
from jax.sharding import PartitionSpec as P

DS = 768
AXES = ("blk", "inner")
VMEM = 48 * 2**20
SHARE_SCALE = 8.0


EPSILON = 1e-06


def coefficients(sq_student, sq_teacher, cross, total):
    norm_student = jnp.sqrt(sq_student + EPSILON)
    norm_teacher = jnp.sqrt(sq_teacher + EPSILON)
    factor = 2.0 * math.sqrt(total * DS) / total
    cubed = norm_student * norm_student * norm_student
    alpha = factor * (EPSILON / norm_student + cross / norm_teacher) / cubed
    beta = factor / (norm_student * norm_teacher)
    terms = (
        sq_student / (norm_student * norm_student)
        + sq_teacher / (norm_teacher * norm_teacher)
        - 2.0 * cross / (norm_student * norm_teacher)
    )
    return (alpha, beta, terms)


def span(masks):
    out = [0]
    for mask in masks:
        out += [mask ^ other for other in out]
    return out


def subgroups(blocks, inner):
    bits = [1 << b for b in range((inner - 1).bit_length())]
    bits += [inner << b for b in range(1, (blocks - 1).bit_length())]
    return (bits[0::2], bits[1::2] + [inner])


def send(value, mask, count):
    return lax.ppermute(value, AXES, [(i, i ^ mask) for i in range(count)])


def after(value, other):
    return lax.optimization_barrier((value, other))[0]


def gather(own, row_masks, col_masks, count):
    *plane_masks, core_mask = col_masks
    row, col, core = {0: own}, {0: own}, []
    col[1] = send(own, plane_masks[0], count)
    row[1] = send(own, row_masks[0], count)
    core.append(send(own, core_mask, count))
    late = after(own, core[0])
    sides = ((row, row_masks), (col, plane_masks))
    for side, masks in sides:
        for b, mask in enumerate(masks):
            if b:
                side[1 << b] = send(late, mask, count)
    row[1], col[1] = after((row[1], col[1]), (row[2], col[2]))
    places = [0]
    for level in range(1, len(row_masks) + 1):
        for side, masks in sides:
            for place in range(1 << len(masks)):
                if place.bit_count() == level and place not in side:
                    top = place.bit_length() - 1
                    side[place] = send(side[place ^ (1 << top)], masks[top], count)
        ready = [p for p in range(1 << len(plane_masks)) if p.bit_count() == level]
        if ready:
            core.append(send(jnp.concatenate([col[p] for p in ready]), core_mask, count))
            places += ready
    return [row[p] for p in sorted(row)], [col[p] for p in places] + core, places


def tree_sum(values):
    while len(values) > 1:
        values = [values[i] + values[i + 1] for i in range(0, len(values), 2)]
    return values[0]


def join_kernel(teacher, student, own):
    own[:, : teacher.shape[1]] = teacher[...]
    own[:, teacher.shape[1] :] = student[...]


def put_sums(parts, row_part, col_part):
    pad = jnp.zeros((parts[0].shape[0], 128 - len(parts)), jnp.float32)
    by_row = jnp.transpose(jnp.concatenate([jnp.sum(p, 1, keepdims=True) for p in parts] + [pad], 1))
    for k, part in enumerate(parts):
        by_col = jnp.sum(part, 0, keepdims=True)
        for source, sums in ((by_row[k : k + 1], row_part), (by_col, col_part)):
            rows = sums.shape[2]
            for p in range(sums.shape[1]):
                sums[k, p : p + 1, :] = source[:, p * rows : (p + 1) * rows]


def gram_kernel(n_row, width, *refs):
    *pieces, gram_s, gram_t, row_part, col_part = refs
    grams = []
    for part in (slice(width, None), slice(0, width)):
        tops, sides = [jnp.concatenate([p[:, part] for p in group]) for group in (pieces[:n_row], pieces[n_row:])]
        grams.append(
            lax.dot_general(tops, sides, (((1,), (1,)), ((), ())), preferred_element_type=jnp.float32)
        )
    student, teacher = grams
    gram_s[...], gram_t[...] = grams
    put_sums([student * student, teacher * teacher, student * teacher], row_part, col_part)


def call(kernel, operands, outputs, flops=0):
    size = sum(math.prod(a.shape) * a.dtype.itemsize for a in [*operands, *jax.tree.leaves(outputs)])
    return pl.pallas_call(
        kernel,
        out_shape=outputs,
        compiler_params=pltpu.CompilerParams(vmem_limit_bytes=VMEM),
        cost_estimate=pl.CostEstimate(flops=flops, bytes_accessed=size, transcendentals=0),
    )(*operands)


def output_kernel(n_row, n_side, first, total, gram_s, gram_t, row_sum, col_sum, *refs):
    sides, (own, share, *pieces) = refs[:n_side], refs[n_side:]
    col_s = jnp.concatenate([side[:, first:] for side in sides])
    row_alpha, row_beta, _ = coefficients(row_sum[0], row_sum[1], row_sum[2], total)
    col_alpha, col_beta, terms = coefficients(col_sum[0], col_sum[1], col_sum[2], total)
    row_ab = jnp.transpose(jnp.concatenate([row_alpha, row_beta] * 4))
    row_w = row_ab[:, 0:1] * gram_s[...] - row_ab[:, 1:2] * gram_t[...]
    col_w = col_alpha * gram_s[...] - col_beta * gram_t[...]
    out = jnp.dot(row_w.astype(jnp.bfloat16), col_s, preferred_element_type=jnp.float32)
    out += jnp.dot(col_w.astype(jnp.bfloat16), col_s, preferred_element_type=jnp.float32)

    rows, width = own.shape
    own[...] = out[:rows]
    term = jnp.sum(terms, axis=1, keepdims=True)
    share[...] = jnp.broadcast_to(term, share.shape)
    largest = jnp.max(jnp.max(jnp.abs(out), axis=0, keepdims=True), axis=1, keepdims=True)
    power = jnp.clip(jnp.floor(jnp.log2(largest)), -100.0, 100.0)
    term = term * SHARE_SCALE
    high = term.astype(jnp.bfloat16).astype(jnp.float32)
    middle = (term - high).astype(jnp.bfloat16).astype(jnp.float32)
    low = term - high - middle
    lane = lax.broadcasted_iota(jnp.int32, (rows, 128), 1)
    extra = jnp.where(lane == 0, power, jnp.where(lane == 1, high, jnp.where(lane == 2, middle, low)))
    scaled = out * jnp.exp2(13.0 - power)
    for k, piece in enumerate(pieces):
        piece[:, :width] = scaled[(k + 1) * rows : (k + 2) * rows]
        piece[:, width:] = extra


def final_kernel(total, own, share, *refs):
    *pieces, grad, loss = refs
    width = own.shape[1]
    grads, terms = [own[...]], [share[0:1, 0:1]]
    for piece in pieces:
        extra = piece[:, width:]
        grads.append(piece[:, :width] * jnp.exp2(extra[:, 0:1] - 13.0))
        terms.append((extra[0:1, 1:2] + extra[0:1, 2:3] + extra[0:1, 3:4]) * (1.0 / SHARE_SCALE))
    grad[...] = tree_sum(grads)
    loss[...] = tree_sum(terms) * (1.0 / total)


def add_partner(parts, masks, place, count):
    got = send(parts, masks[place], count)
    shape = (3, -1, 2, 1 << place, got.shape[-1])
    return parts + jnp.flip(got.reshape(shape), 2).reshape(parts.shape)


def per_device(teacher, student):
    rows = teacher.shape[0]
    blocks = lax.axis_size("blk")
    inner = lax.axis_size("inner")
    count = blocks * inner
    total = rows * count
    row_masks, col_masks = subgroups(blocks, inner)
    n_row, n_col = 1 << len(row_masks), 1 << len(col_masks)

    depth = teacher.shape[1] + student.shape[1]
    own = call(join_kernel, [teacher, student], jax.ShapeDtypeStruct((rows, depth), teacher.dtype))
    row, col, places = gather(own, row_masks, col_masks, count)
    shape, width = (n_row * rows, n_col * rows), student.shape[1]

    def f32(*dims):
        return jax.ShapeDtypeStruct(dims, jnp.float32)

    gram_s, gram_t, row_part, col_part = call(
        functools.partial(gram_kernel, n_row, teacher.shape[1]),
        row + col,
        [f32(*shape), f32(*shape), f32(3, n_row, rows), f32(3, n_col, rows)],
        2 * math.prod(shape) * depth,
    )
    for place in range(max(len(row_masks), len(col_masks))):
        if place < len(col_masks):
            col_part = add_partner(col_part, col_masks, place, count)
        if place < len(row_masks):
            row_part = after(add_partner(row_part, row_masks, place, count), col_part)
    row_sum, col_sum = row_part.reshape(3, 1, -1), col_part.reshape(3, 1, -1)

    own, share, *pieces = call(
        functools.partial(output_kernel, n_row, len(col), teacher.shape[1], total),
        [gram_s, gram_t, row_sum, col_sum, *col],
        [f32(rows, width), f32(8, 128)] + [f32(rows, width + 128)] * (n_row - 1),
        4 * math.prod(shape) * width,
    )
    got = [
        send(value.astype(jnp.float16), mask, count).astype(jnp.float32)
        for value, mask in zip(pieces, span(row_masks)[1:])
    ]
    grad, loss = call(
        functools.partial(final_kernel, total), [own, share, *got], [f32(rows, width), f32(1, 1)]
    )
    return (loss[0, 0], grad)


def solution(mesh):
    return jax.shard_map(
        per_device,
        mesh=mesh,
        in_specs=(P(AXES, None), P(AXES, None)),
        out_specs=(P(), P(AXES, None)),
        check_vma=False,
    )
```

```python
import functools
import math

import jax
import jax.numpy as jnp
from jax import lax
from jax.experimental import pallas as pl
from jax.experimental.pallas import tpu as pltpu
from jax.sharding import PartitionSpec as P

DS = 768
AXES = ("blk", "inner")
VMEM = 48 * 2**20
SHARE_SCALE = 8.0


EPSILON = 1e-06


def coefficients(sq_student, sq_teacher, cross, total):
    norm_student = jnp.sqrt(sq_student + EPSILON)
    norm_teacher = jnp.sqrt(sq_teacher + EPSILON)
    factor = 2.0 * math.sqrt(total * DS) / total
    cubed = norm_student * norm_student * norm_student
    alpha = factor * (EPSILON / norm_student + cross / norm_teacher) / cubed
    beta = factor / (norm_student * norm_teacher)
    terms = (
        sq_student / (norm_student * norm_student)
        + sq_teacher / (norm_teacher * norm_teacher)
        - 2.0 * cross / (norm_student * norm_teacher)
    )
    return (alpha, beta, terms)


def span(masks):
    out = [0]
    for mask in masks:
        out += [mask ^ other for other in out]
    return out


def subgroups(blocks, inner):
    bits = [1 << b for b in range((inner - 1).bit_length())]
    bits += [inner << b for b in range(1, (blocks - 1).bit_length())]
    return (bits[0::2], bits[1::2] + [inner])


def send(value, mask, count):
    return lax.ppermute(value, AXES, [(i, i ^ mask) for i in range(count)])


def after(value, other):
    return lax.optimization_barrier((value, other))[0]


def gather(own, row_masks, col_masks, count):
    *plane_masks, core_mask = col_masks
    row, col, core = {0: own}, {0: own}, []
    col[1] = send(own, plane_masks[0], count)
    row[1] = send(own, row_masks[0], count)
    core.append(send(own, core_mask, count))
    late = after(own, core[0])
    sides = ((row, row_masks), (col, plane_masks))
    for side, masks in sides:
        for b, mask in enumerate(masks):
            if b:
                side[1 << b] = send(late, mask, count)
    row[1], col[1] = after((row[1], col[1]), (row[2], col[2]))
    places = [0]
    for level in range(1, len(row_masks) + 1):
        for side, masks in sides:
            for place in range(1 << len(masks)):
                if place.bit_count() == level and place not in side:
                    top = place.bit_length() - 1
                    side[place] = send(side[place ^ (1 << top)], masks[top], count)
        ready = [p for p in range(1 << len(plane_masks)) if p.bit_count() == level]
        if ready:
            core.append(send(jnp.concatenate([col[p] for p in ready]), core_mask, count))
            places += ready
    return [row[p] for p in sorted(row)], [col[p] for p in places] + core, places


def tree_sum(values):
    while len(values) > 1:
        values = [values[i] + values[i + 1] for i in range(0, len(values), 2)]
    return values[0]


def join_kernel(teacher, student, own, sems):
    width = teacher.shape[1]
    copies = [
        pltpu.make_async_copy(teacher, own.at[:, pl.ds(0, width)], sems.at[0]),
        pltpu.make_async_copy(student, own.at[:, pl.ds(width, student.shape[1])], sems.at[1]),
    ]
    for copy in copies:
        copy.start()
    for copy in copies:
        copy.wait()


def put_sums(parts, row_part, col_part):
    pad = jnp.zeros((parts[0].shape[0], 128 - len(parts)), jnp.float32)
    by_row = jnp.transpose(jnp.concatenate([jnp.sum(p, 1, keepdims=True) for p in parts] + [pad], 1))
    for k, part in enumerate(parts):
        by_col = jnp.sum(part, 0, keepdims=True)
        for source, sums in ((by_row[k : k + 1], row_part), (by_col, col_part)):
            rows = sums.shape[2]
            for p in range(sums.shape[1]):
                sums[k, p : p + 1, :] = source[:, p * rows : (p + 1) * rows]


def gram_kernel(n_row, width, *refs):
    *pieces, gram_s, gram_t, row_part, col_part = refs
    grams = []
    for part in (slice(width, None), slice(0, width)):
        tops, sides = [jnp.concatenate([p[:, part] for p in group]) for group in (pieces[:n_row], pieces[n_row:])]
        grams.append(
            lax.dot_general(tops, sides, (((1,), (1,)), ((), ())), preferred_element_type=jnp.float32)
        )
    student, teacher = grams
    gram_s[...], gram_t[...] = grams
    put_sums([student * student, teacher * teacher, student * teacher], row_part, col_part)


def call(kernel, operands, outputs, flops=0, vmem=VMEM, **options):
    size = sum(math.prod(a.shape) * a.dtype.itemsize for a in [*operands, *jax.tree.leaves(outputs)])
    return pl.pallas_call(
        kernel,
        out_shape=outputs,
        **options,
        compiler_params=pltpu.CompilerParams(vmem_limit_bytes=vmem),
        cost_estimate=pl.CostEstimate(flops=flops, bytes_accessed=size, transcendentals=0),
    )(*operands)


def output_kernel(n_row, n_side, first, total, gram_s, gram_t, row_sum, col_sum, *refs):
    sides, (own, share, *pieces) = refs[:n_side], refs[n_side:]
    col_s = jnp.concatenate([side[:, first:] for side in sides])
    row_alpha, row_beta, _ = coefficients(row_sum[0], row_sum[1], row_sum[2], total)
    col_alpha, col_beta, terms = coefficients(col_sum[0], col_sum[1], col_sum[2], total)
    row_ab = jnp.transpose(jnp.concatenate([row_alpha, row_beta] * 4))
    row_w = row_ab[:, 0:1] * gram_s[...] - row_ab[:, 1:2] * gram_t[...]
    col_w = col_alpha * gram_s[...] - col_beta * gram_t[...]
    out = jnp.dot(row_w.astype(jnp.bfloat16), col_s, preferred_element_type=jnp.float32)
    out += jnp.dot(col_w.astype(jnp.bfloat16), col_s, preferred_element_type=jnp.float32)

    rows, width = own.shape
    own[...] = out[:rows]
    term = jnp.sum(terms, axis=1, keepdims=True)
    share[...] = jnp.broadcast_to(term, share.shape)
    largest = jnp.max(jnp.max(jnp.abs(out), axis=0, keepdims=True), axis=1, keepdims=True)
    power = jnp.clip(jnp.floor(jnp.log2(largest)), -100.0, 100.0)
    term = term * SHARE_SCALE
    high = term.astype(jnp.bfloat16).astype(jnp.float32)
    middle = (term - high).astype(jnp.bfloat16).astype(jnp.float32)
    low = term - high - middle
    lane = lax.broadcasted_iota(jnp.int32, (rows, 128), 1)
    extra = jnp.where(lane == 0, power, jnp.where(lane == 1, high, jnp.where(lane == 2, middle, low)))
    scaled = out * jnp.exp2(13.0 - power)
    for k, piece in enumerate(pieces):
        piece[:, :width] = scaled[(k + 1) * rows : (k + 2) * rows]
        piece[:, width:] = extra


def final_kernel(total, own, share, *refs):
    *pieces, grad, loss = refs
    width = own.shape[1]
    grads, terms = [own[...]], [share[0:1, 0:1]]
    for piece in pieces:
        extra = piece[:, width:]
        grads.append(piece[:, :width] * jnp.exp2(extra[:, 0:1] - 13.0))
        terms.append((extra[0:1, 1:2] + extra[0:1, 2:3] + extra[0:1, 3:4]) * (1.0 / SHARE_SCALE))
    grad[...] = tree_sum(grads)
    loss[...] = tree_sum(terms) * (1.0 / total)


def group_sum(parts, masks, count):
    members = span(masks)
    spanned = set(members)
    heads = [i for i in range(count) if i == min(i ^ m for m in spanned)]
    groups = [[head ^ m for m in members] for head in heads]
    outgoing = jnp.stack([jnp.stack([parts[:, k ^ r] for k in range(len(members))], 1) for r in range(len(members))])
    place = lax.axis_index(AXES)
    for b, mask in enumerate(masks):
        bit = (place & mask) != 0
        shape = (-1, 2, 1 << b) + parts.shape
        flipped = jnp.flip(outgoing.reshape(shape), 1).reshape(outgoing.shape)
        outgoing = jnp.where(bit, flipped, outgoing)
    got = lax.all_to_all(outgoing, AXES, 0, 0, axis_index_groups=groups, tiled=True)
    return tree_sum([got[i] for i in range(len(members))])


def per_device(teacher, student):
    rows = teacher.shape[0]
    blocks = lax.axis_size("blk")
    inner = lax.axis_size("inner")
    count = blocks * inner
    total = rows * count
    row_masks, col_masks = subgroups(blocks, inner)
    n_row, n_col = 1 << len(row_masks), 1 << len(col_masks)

    depth = teacher.shape[1] + student.shape[1]
    own = call(
        join_kernel,
        [teacher, student],
        jax.ShapeDtypeStruct((rows, depth), teacher.dtype),
        in_specs=[pl.BlockSpec(memory_space=pl.ANY)] * 2,
        vmem=60 * 2**20,
        scratch_shapes=[pltpu.SemaphoreType.DMA((2,))],
    )
    row, col, places = gather(own, row_masks, col_masks, count)
    shape, width = (n_row * rows, n_col * rows), student.shape[1]

    def f32(*dims):
        return jax.ShapeDtypeStruct(dims, jnp.float32)

    gram_s, gram_t, row_part, col_part = call(
        functools.partial(gram_kernel, n_row, teacher.shape[1]),
        row + col,
        [f32(*shape), f32(*shape), f32(3, n_row, rows), f32(3, n_col, rows)],
        2 * math.prod(shape) * depth,
    )
    col_part = group_sum(col_part, col_masks, count)
    row_part = group_sum(row_part, row_masks, count)
    row_sum, col_sum = row_part.reshape(3, 1, -1), col_part.reshape(3, 1, -1)

    own, share, *pieces = call(
        functools.partial(output_kernel, n_row, len(col), teacher.shape[1], total),
        [gram_s, gram_t, row_sum, col_sum, *col],
        [f32(rows, width), f32(8, 128)] + [f32(rows, width + 128)] * (n_row - 1),
        4 * math.prod(shape) * width,
    )
    got = [
        send(value.astype(jnp.float16), mask, count).astype(jnp.float32)
        for value, mask in zip(pieces, span(row_masks)[1:])
    ]
    grad, loss = call(
        functools.partial(final_kernel, total), [own, share, *got], [f32(rows, width), f32(1, 1)]
    )
    return (loss[0, 0], grad)


def solution(mesh):
    return jax.shard_map(
        per_device,
        mesh=mesh,
        in_specs=(P(AXES, None), P(AXES, None)),
        out_specs=(P(), P(AXES, None)),
        check_vma=False,
    )
```

```python
import functools
import math

import jax
import jax.numpy as jnp
from jax import lax
from jax.experimental import pallas as pl
from jax.experimental.pallas import tpu as pltpu
from jax.sharding import PartitionSpec as P

DS = 768
AXES = ("blk", "inner")
VMEM = 48 * 2**20
SHARE_SCALE = 8.0


EPSILON = 1e-06


def coefficients(sq_student, sq_teacher, cross, total):
    norm_student = jnp.sqrt(sq_student + EPSILON)
    norm_teacher = jnp.sqrt(sq_teacher + EPSILON)
    factor = 2.0 * math.sqrt(total * DS) / total
    cubed = norm_student * norm_student * norm_student
    alpha = factor * (EPSILON / norm_student + cross / norm_teacher) / cubed
    beta = factor / (norm_student * norm_teacher)
    terms = (
        sq_student / (norm_student * norm_student)
        + sq_teacher / (norm_teacher * norm_teacher)
        - 2.0 * cross / (norm_student * norm_teacher)
    )
    return (alpha, beta, terms)


def span(masks):
    out = [0]
    for mask in masks:
        out += [mask ^ other for other in out]
    return out


def subgroups(blocks, inner):
    bits = [1 << b for b in range((inner - 1).bit_length())]
    bits += [inner << b for b in range(1, (blocks - 1).bit_length())]
    return (bits[0::2], bits[1::2] + [inner])


def send(value, mask, count):
    return lax.ppermute(value, AXES, [(i, i ^ mask) for i in range(count)])


def after(value, other):
    return lax.optimization_barrier((value, other))[0]


def gather(teacher, student, row_masks, col_masks, count):
    *plane_masks, core_mask = col_masks

    def join(pair):
        shape = (pair[0].shape[0], sum(value.shape[1] for value in pair))
        return call(join_kernel, pair, jax.ShapeDtypeStruct(shape, pair[0].dtype))

    col_t, row_t = send(teacher, plane_masks[0], count), send(teacher, row_masks[0], count)
    swapped = [send(value, core_mask, count) for value in (teacher, student)]
    late_t, late_s = after((teacher, student), swapped)
    own = join([late_t, late_s])
    row, col, core = {0: own}, {0: own}, [join(swapped)]
    sides = ((row, row_masks), (col, plane_masks))
    for side, masks in sides:
        for b, mask in enumerate(masks):
            if b:
                side[1 << b] = send(own, mask, count)
    col_s = send(late_s, plane_masks[0], count)
    row_t, col_t, late = lax.optimization_barrier((row_t, col_t, student))
    row_s = send(late, row_masks[0], count)
    pairs = (row_t, row_s), (col_t, col_s)
    row[1], col[1] = map(join, after(pairs, (row[2], col[2])))
    places = [0]
    for level in range(1, len(row_masks) + 1):
        for side, masks in sides:
            for place in range(1 << len(masks)):
                if place.bit_count() == level and place not in side:
                    top = place.bit_length() - 1
                    side[place] = send(side[place ^ (1 << top)], masks[top], count)
        ready = [p for p in range(1 << len(plane_masks)) if p.bit_count() == level]
        if ready:
            core.append(send(jnp.concatenate([col[p] for p in ready]), core_mask, count))
            places += ready
    return [row[p] for p in sorted(row)], [col[p] for p in places] + core, places


def tree_sum(values):
    while len(values) > 1:
        values = [values[i] + values[i + 1] for i in range(0, len(values), 2)]
    return values[0]


def join_kernel(left, right, both):
    both[:, : left.shape[1]] = left[...]
    both[:, left.shape[1] :] = right[...]


def put_sums(parts, row_part, col_part):
    pad = jnp.zeros((parts[0].shape[0], 128 - len(parts)), jnp.float32)
    by_row = jnp.transpose(jnp.concatenate([jnp.sum(p, 1, keepdims=True) for p in parts] + [pad], 1))
    for k, part in enumerate(parts):
        by_col = jnp.sum(part, 0, keepdims=True)
        for source, sums in ((by_row[k : k + 1], row_part), (by_col, col_part)):
            rows = sums.shape[2]
            for p in range(sums.shape[1]):
                sums[k, p : p + 1, :] = source[:, p * rows : (p + 1) * rows]


def gram_kernel(n_row, width, *refs):
    *pieces, gram_s, gram_t, row_part, col_part = refs
    grams = []
    for part in (slice(width, None), slice(0, width)):
        tops, sides = [jnp.concatenate([p[:, part] for p in group]) for group in (pieces[:n_row], pieces[n_row:])]
        grams.append(
            lax.dot_general(tops, sides, (((1,), (1,)), ((), ())), preferred_element_type=jnp.float32)
        )
    student, teacher = grams
    gram_s[...], gram_t[...] = grams
    put_sums([student * student, teacher * teacher, student * teacher], row_part, col_part)


def call(kernel, operands, outputs, flops=0, **options):
    size = sum(math.prod(a.shape) * a.dtype.itemsize for a in [*operands, *jax.tree.leaves(outputs)])
    return pl.pallas_call(
        kernel,
        out_shape=outputs,
        **options,
        compiler_params=pltpu.CompilerParams(vmem_limit_bytes=VMEM),
        cost_estimate=pl.CostEstimate(flops=flops, bytes_accessed=size, transcendentals=0),
    )(*operands)


def output_kernel(n_row, n_side, first, total, gram_s, gram_t, row_sum, col_sum, *refs):
    sides, (own, share, *pieces) = refs[:n_side], refs[n_side:]
    col_s = jnp.concatenate([side[:, first:] for side in sides])
    row_alpha, row_beta, _ = coefficients(row_sum[0], row_sum[1], row_sum[2], total)
    col_alpha, col_beta, terms = coefficients(col_sum[0], col_sum[1], col_sum[2], total)
    row_ab = jnp.transpose(jnp.concatenate([row_alpha, row_beta] * 4))
    row_w = row_ab[:, 0:1] * gram_s[...] - row_ab[:, 1:2] * gram_t[...]
    col_w = col_alpha * gram_s[...] - col_beta * gram_t[...]
    out = jnp.dot(row_w.astype(jnp.bfloat16), col_s, preferred_element_type=jnp.float32)
    out += jnp.dot(col_w.astype(jnp.bfloat16), col_s, preferred_element_type=jnp.float32)

    rows, width = own.shape
    own[...] = out[:rows]
    term = jnp.sum(terms, axis=1, keepdims=True)
    share[...] = jnp.broadcast_to(term, share.shape)
    largest = jnp.max(jnp.max(jnp.abs(out), axis=0, keepdims=True), axis=1, keepdims=True)
    power = jnp.clip(jnp.floor(jnp.log2(largest)), -100.0, 100.0)
    term = term * SHARE_SCALE
    high = term.astype(jnp.bfloat16).astype(jnp.float32)
    middle = (term - high).astype(jnp.bfloat16).astype(jnp.float32)
    low = term - high - middle
    lane = lax.broadcasted_iota(jnp.int32, (rows, 128), 1)
    extra = jnp.where(lane == 0, power, jnp.where(lane == 1, high, jnp.where(lane == 2, middle, low)))
    scaled = out * jnp.exp2(13.0 - power)
    for k, piece in enumerate(pieces):
        piece[:, :width] = scaled[(k + 1) * rows : (k + 2) * rows]
        piece[:, width:] = extra


def final_kernel(total, own, share, *refs):
    *pieces, grad, loss = refs
    width = own.shape[1]
    grads, terms = [own[...]], [share[0:1, 0:1]]
    for piece in pieces:
        extra = piece[:, width:]
        grads.append(piece[:, :width] * jnp.exp2(extra[:, 0:1] - 13.0))
        terms.append((extra[0:1, 1:2] + extra[0:1, 2:3] + extra[0:1, 3:4]) * (1.0 / SHARE_SCALE))
    grad[...] = tree_sum(grads)
    loss[...] = tree_sum(terms) * (1.0 / total)


def add_partner(parts, masks, place, count):
    got = send(parts, masks[place], count)
    shape = (3, -1, 2, 1 << place, got.shape[-1])
    return parts + jnp.flip(got.reshape(shape), 2).reshape(parts.shape)


def per_device(teacher, student):
    rows = teacher.shape[0]
    blocks = lax.axis_size("blk")
    inner = lax.axis_size("inner")
    count = blocks * inner
    total = rows * count
    row_masks, col_masks = subgroups(blocks, inner)
    n_row, n_col = 1 << len(row_masks), 1 << len(col_masks)

    depth = teacher.shape[1] + student.shape[1]
    row, col, places = gather(teacher, student, row_masks, col_masks, count)
    shape, width = (n_row * rows, n_col * rows), student.shape[1]

    def f32(*dims):
        return jax.ShapeDtypeStruct(dims, jnp.float32)

    gram_s, gram_t, row_part, col_part = call(
        functools.partial(gram_kernel, n_row, teacher.shape[1]),
        row + col,
        [f32(*shape), f32(*shape), f32(3, n_row, rows), f32(3, n_col, rows)],
        2 * math.prod(shape) * depth,
    )
    for place in range(max(len(row_masks), len(col_masks))):
        if place < len(col_masks):
            col_part = add_partner(col_part, col_masks, place, count)
        if place < len(row_masks):
            row_part = add_partner(row_part, row_masks, place, count)
        if place + 1 < len(row_masks):
            row_part, col_part = lax.optimization_barrier((row_part, col_part))
    row_sum, col_sum = row_part.reshape(3, 1, -1), col_part.reshape(3, 1, -1)

    own, share, *pieces = call(
        functools.partial(output_kernel, n_row, len(col), teacher.shape[1], total),
        [gram_s, gram_t, row_sum, col_sum, *col],
        [f32(rows, width), f32(8, 128)] + [f32(rows, width + 128)] * (n_row - 1),
        4 * math.prod(shape) * width,
    )
    got = [
        send(value.astype(jnp.float16), mask, count).astype(jnp.float32)
        for value, mask in zip(pieces, span(row_masks)[1:])
    ]
    grad, loss = call(
        functools.partial(final_kernel, total), [own, share, *got], [f32(rows, width), f32(1, 1)]
    )
    return (loss[0, 0], grad)


def solution(mesh):
    return jax.shard_map(
        per_device,
        mesh=mesh,
        in_specs=(P(AXES, None), P(AXES, None)),
        out_specs=(P(), P(AXES, None)),
        check_vma=False,
    )
```

```python
import functools
import math

import jax
import jax.numpy as jnp
from jax import lax
from jax.experimental import pallas as pl
from jax.experimental.pallas import tpu as pltpu
from jax.sharding import PartitionSpec as P

DS = 768
AXES = ("blk", "inner")
VMEM = 48 * 2**20
SHARE_SCALE = 8.0


EPSILON = 1e-06


def coefficients(sq_student, sq_teacher, cross, total):
    norm_student = jnp.sqrt(sq_student + EPSILON)
    norm_teacher = jnp.sqrt(sq_teacher + EPSILON)
    factor = 2.0 * math.sqrt(total * DS) / total
    cubed = norm_student * norm_student * norm_student
    alpha = factor * (EPSILON / norm_student + cross / norm_teacher) / cubed
    beta = factor / (norm_student * norm_teacher)
    terms = (
        sq_student / (norm_student * norm_student)
        + sq_teacher / (norm_teacher * norm_teacher)
        - 2.0 * cross / (norm_student * norm_teacher)
    )
    return (alpha, beta, terms)


def span(masks):
    out = [0]
    for mask in masks:
        out += [mask ^ other for other in out]
    return out


def subgroups(blocks, inner):
    bits = [1 << b for b in range((inner - 1).bit_length())]
    bits += [inner << b for b in range(1, (blocks - 1).bit_length())]
    return (bits[0::2], bits[1::2] + [inner])


def send(value, mask, count):
    return lax.ppermute(value, AXES, [(i, i ^ mask) for i in range(count)])


def after(value, other):
    return lax.optimization_barrier((value, other))[0]


def join(*values):
    shape = (values[0].shape[0], sum(value.shape[1] for value in values))
    return call(join_kernel, values, jax.ShapeDtypeStruct(shape, values[0].dtype))


def gather(teacher, student, row_masks, col_masks, count):
    *plane_masks, core_mask = col_masks
    row_t, row_s, col_t, col_s = {}, {}, {}, {}
    sides = ((row_t, row_s, row_masks), (col_t, col_s, plane_masks))

    def whole(value):
        return (value, 0, value.shape[1])

    def forward(side, masks, keep):
        for level in range(2, len(masks) + 1):
            for place in range(1 << len(masks)):
                if place.bit_count() == level and keep(place):
                    top = place.bit_length() - 1
                    side[place] = whole(send(side[place ^ (1 << top)][0], masks[top], count))

    for side_t, _, masks in reversed(sides):
        side_t[1] = whole(send(teacher, masks[0], count))
    for _, side_s, masks in reversed(sides):
        for b, mask in enumerate(masks):
            if b:
                side_s[1 << b] = whole(send(student, mask, count))
    own = join(teacher, student)
    late = after(teacher, (row_s[2][0], col_s[2][0], own))
    for side_t, _, masks in reversed(sides):
        side_t[0] = (own, 0, teacher.shape[1])
        for b, mask in enumerate(masks):
            if b:
                side_t[1 << b] = whole(send(late, mask, count))

    def long_way(side_s, masks, gate):
        forward(side_s, masks, lambda place: not place & 1)
        half = range(0, 1 << len(masks), 2)
        parts = [own[:, teacher.shape[1] :]] + [side_s[p][0] for p in half if p]
        side_s[0] = (own, teacher.shape[1], own.shape[1])
        got = send(after(join(*parts), gate), masks[0], count)
        for k, p in enumerate(half):
            side_s[p | 1] = (got, k * student.shape[1], (k + 1) * student.shape[1])

    first = (row_t[1][0], col_t[1][0])
    long_way(col_s, plane_masks, ())
    long_way(row_s, row_masks, first)
    row_t[1], col_t[1] = map(whole, after(first, (row_t[2][0], col_t[2][0])))
    for side_t, _, masks in reversed(sides):
        forward(side_t, masks, lambda place: True)

    core_t, core_s = {}, {}
    ones = [0] + [1 << b for b in range(len(plane_masks))]
    rest = [p for p in range(1 << len(plane_masks)) if p.bit_count() > 1]
    swaps = [
        [(col_t, core_t, p) for p in ones] + [(col_s, core_s, p) for p in col_s if not p & 1],
        [(col_t, core_t, p) for p in rest],
        [(col_s, core_s, p) for p in col_s if p & 1],
    ]
    for swap in swaps:
        arrays = list({id(side[p][0]): side[p][0] for side, _, p in swap}.values())
        got = send(join(*arrays) if len(arrays) > 1 else arrays[0], core_mask, count)
        starts = {id(array): sum(a.shape[1] for a in arrays[:k]) for k, array in enumerate(arrays)}
        for side, core, p in swap:
            array, start, stop = side[p]
            core[p] = (got, starts[id(array)] + start, starts[id(array)] + stop)
    places = sorted(col_t)
    return (
        [row_t[p] for p in sorted(row_t)],
        [row_s[p] for p in sorted(row_s)],
        [col_t[p] for p in places] + [core_t[p] for p in places],
        [col_s[p] for p in places] + [core_s[p] for p in places],
    )


def operands_of(*groups):
    arrays = []
    for array, _, _ in sum(groups, []):
        if not any(array is other for other in arrays):
            arrays.append(array)
    number = {id(array): k for k, array in enumerate(arrays)}
    return arrays, [[(number[id(array)], start, stop) for array, start, stop in group] for group in groups]


def load(refs, group):
    return jnp.concatenate([refs[k][:, start:stop] for k, start, stop in group])


def tree_sum(values):
    while len(values) > 1:
        values = [values[i] + values[i + 1] for i in range(0, len(values), 2)]
    return values[0]


def join_kernel(*refs):
    *parts, both = refs
    start = 0
    for part in parts:
        both[:, start : start + part.shape[1]] = part[...]
        start += part.shape[1]


def put_sums(parts, row_part, col_part):
    pad = jnp.zeros((parts[0].shape[0], 128 - len(parts)), jnp.float32)
    by_row = jnp.transpose(jnp.concatenate([jnp.sum(p, 1, keepdims=True) for p in parts] + [pad], 1))
    for k, part in enumerate(parts):
        by_col = jnp.sum(part, 0, keepdims=True)
        for source, sums in ((by_row[k : k + 1], row_part), (by_col, col_part)):
            rows = sums.shape[2]
            for p in range(sums.shape[1]):
                sums[k, p : p + 1, :] = source[:, p * rows : (p + 1) * rows]


def gram_kernel(groups, *refs):
    *arrays, gram_s, gram_t, row_part, col_part = refs
    row_t, row_s, col_t, col_s = [load(arrays, group) for group in groups]
    dims = (((1,), (1,)), ((), ()))
    student = lax.dot_general(row_s, col_s, dims, preferred_element_type=jnp.float32)
    teacher = lax.dot_general(row_t, col_t, dims, preferred_element_type=jnp.float32)
    gram_s[...], gram_t[...] = student, teacher
    put_sums([student * student, teacher * teacher, student * teacher], row_part, col_part)


def call(kernel, operands, outputs, flops=0, **options):
    size = sum(math.prod(a.shape) * a.dtype.itemsize for a in [*operands, *jax.tree.leaves(outputs)])
    return pl.pallas_call(
        kernel,
        out_shape=outputs,
        **options,
        compiler_params=pltpu.CompilerParams(vmem_limit_bytes=VMEM),
        cost_estimate=pl.CostEstimate(flops=flops, bytes_accessed=size, transcendentals=0),
    )(*operands)


def output_kernel(n_arrays, group, total, gram_s, gram_t, row_sum, col_sum, *refs):
    col_s = load(refs[:n_arrays], group)
    own, share, *pieces = refs[n_arrays:]
    row_alpha, row_beta, _ = coefficients(row_sum[0], row_sum[1], row_sum[2], total)
    col_alpha, col_beta, terms = coefficients(col_sum[0], col_sum[1], col_sum[2], total)
    row_ab = jnp.transpose(jnp.concatenate([row_alpha, row_beta] * 4))
    row_w = row_ab[:, 0:1] * gram_s[...] - row_ab[:, 1:2] * gram_t[...]
    col_w = col_alpha * gram_s[...] - col_beta * gram_t[...]
    out = jnp.dot(row_w.astype(jnp.bfloat16), col_s, preferred_element_type=jnp.float32)
    out += jnp.dot(col_w.astype(jnp.bfloat16), col_s, preferred_element_type=jnp.float32)

    rows, width = own.shape
    own[...] = out[:rows]
    term = jnp.sum(terms, axis=1, keepdims=True)
    share[...] = jnp.broadcast_to(term, share.shape)
    largest = jnp.max(jnp.max(jnp.abs(out), axis=0, keepdims=True), axis=1, keepdims=True)
    power = jnp.clip(jnp.floor(jnp.log2(largest)), -100.0, 100.0)
    term = term * SHARE_SCALE
    high = term.astype(jnp.bfloat16).astype(jnp.float32)
    middle = (term - high).astype(jnp.bfloat16).astype(jnp.float32)
    low = term - high - middle
    lane = lax.broadcasted_iota(jnp.int32, (rows, 128), 1)
    extra = jnp.where(lane == 0, power, jnp.where(lane == 1, high, jnp.where(lane == 2, middle, low)))
    scaled = out * jnp.exp2(13.0 - power)
    for k, piece in enumerate(pieces):
        piece[:, :width] = scaled[(k + 1) * rows : (k + 2) * rows]
        piece[:, width:] = extra


def final_kernel(total, own, share, *refs):
    *pieces, grad, loss = refs
    width = own.shape[1]
    grads, terms = [own[...]], [share[0:1, 0:1]]
    for piece in pieces:
        extra = piece[:, width:]
        grads.append(piece[:, :width] * jnp.exp2(extra[:, 0:1] - 13.0))
        terms.append((extra[0:1, 1:2] + extra[0:1, 2:3] + extra[0:1, 3:4]) * (1.0 / SHARE_SCALE))
    grad[...] = tree_sum(grads)
    loss[...] = tree_sum(terms) * (1.0 / total)


def add_partner(parts, masks, place, count):
    got = send(parts, masks[place], count)
    shape = (3, -1, 2, 1 << place, got.shape[-1])
    return parts + jnp.flip(got.reshape(shape), 2).reshape(parts.shape)


def per_device(teacher, student):
    rows = teacher.shape[0]
    blocks = lax.axis_size("blk")
    inner = lax.axis_size("inner")
    count = blocks * inner
    total = rows * count
    row_masks, col_masks = subgroups(blocks, inner)
    n_row, n_col = 1 << len(row_masks), 1 << len(col_masks)

    pieces = gather(teacher, student, row_masks, col_masks, count)
    shape, width = (n_row * rows, n_col * rows), student.shape[1]

    def f32(*dims):
        return jax.ShapeDtypeStruct(dims, jnp.float32)

    arrays, groups = operands_of(*pieces)
    gram_s, gram_t, row_part, col_part = call(
        functools.partial(gram_kernel, groups),
        arrays,
        [f32(*shape), f32(*shape), f32(3, n_row, rows), f32(3, n_col, rows)],
        2 * math.prod(shape) * (teacher.shape[1] + width),
    )
    for place in range(max(len(row_masks), len(col_masks))):
        if place < len(col_masks):
            col_part = add_partner(col_part, col_masks, place, count)
        if place < len(row_masks):
            row_part = add_partner(row_part, row_masks, place, count)
        if place < min(len(row_masks), len(col_masks)):
            row_part, col_part = lax.optimization_barrier((row_part, col_part))
    row_sum, col_sum = row_part.reshape(3, 1, -1), col_part.reshape(3, 1, -1)

    arrays, (group,) = operands_of(pieces[3])
    own, share, *pieces = call(
        functools.partial(output_kernel, len(arrays), group, total),
        [gram_s, gram_t, row_sum, col_sum, *arrays],
        [f32(rows, width), f32(8, 128)] + [f32(rows, width + 128)] * (n_row - 1),
        4 * math.prod(shape) * width,
    )
    got = [
        send(value.astype(jnp.float16), mask, count).astype(jnp.float32)
        for value, mask in zip(pieces, span(row_masks)[1:])
    ]
    grad, loss = call(
        functools.partial(final_kernel, total), [own, share, *got], [f32(rows, width), f32(1, 1)]
    )
    return (loss[0, 0], grad)


def solution(mesh):
    return jax.shard_map(
        per_device,
        mesh=mesh,
        in_specs=(P(AXES, None), P(AXES, None)),
        out_specs=(P(), P(AXES, None)),
        check_vma=False,
    )
```

```python
import functools
import math

import jax
import jax.numpy as jnp
from jax import lax
from jax.experimental import pallas as pl
from jax.experimental.pallas import tpu as pltpu
from jax.sharding import PartitionSpec as P

DS = 768
AXES = ("blk", "inner")
VMEM = 48 * 2**20
SHARE_SCALE = 8.0


EPSILON = 1e-06


def coefficients(sq_student, sq_teacher, cross, total):
    norm_student = jnp.sqrt(sq_student + EPSILON)
    norm_teacher = jnp.sqrt(sq_teacher + EPSILON)
    factor = 2.0 * math.sqrt(total * DS) / total
    cubed = norm_student * norm_student * norm_student
    alpha = factor * (EPSILON / norm_student + cross / norm_teacher) / cubed
    beta = factor / (norm_student * norm_teacher)
    terms = (
        sq_student / (norm_student * norm_student)
        + sq_teacher / (norm_teacher * norm_teacher)
        - 2.0 * cross / (norm_student * norm_teacher)
    )
    return (alpha, beta, terms)


def span(masks):
    out = [0]
    for mask in masks:
        out += [mask ^ other for other in out]
    return out


def subgroups(blocks, inner):
    bits = [1 << b for b in range((inner - 1).bit_length())]
    bits += [inner << b for b in range(1, (blocks - 1).bit_length())]
    return bits[0::2], bits[1::2], inner


def after(value, other):
    return lax.optimization_barrier((value, other))[0]


class Partners:
    def __init__(self, blocks, inner):
        self.count = blocks * inner
        self.rows, self.columns, self.core = subgroups(blocks, inner)

    def swap(self, value):
        return self.row(value, self.core)

    def row(self, value, mask):
        return lax.ppermute(value, AXES, [(i, i ^ mask) for i in range(self.count)])

    def step(self, value, b):
        pairs = []
        for i in range(self.count):
            masks = self.columns if i & self.core else self.rows
            if b < len(masks):
                pairs.append((i, i ^ masks[b]))
        return lax.ppermute(value, AXES, pairs)


def join(*values, axis=1):
    shape = list(values[0].shape)
    shape[axis] = sum(value.shape[axis] for value in values)
    kernel = functools.partial(join_kernel, axis)
    return call(kernel, values, jax.ShapeDtypeStruct(tuple(shape), values[0].dtype))


def gather(teacher, student, partners):
    levels = len(partners.rows)
    swapped = [partners.swap(value) for value in (teacher, student)]
    mine_t, mine_s = {0: join(teacher, swapped[0], axis=0)}, {0: join(student, swapped[1], axis=0)}
    for level in range(1, levels + 1):
        for mine in (mine_t, mine_s):
            for place in range(1, 1 << levels):
                if place.bit_count() == level:
                    top = place.bit_length() - 1
                    mine[place] = partners.step(mine[place ^ (1 << top)], top)

    other_t, other_s = {0: None}, {0: None}
    ones = [1 << b for b in range(levels)]
    rest = [place for place in range(1 << levels) if place.bit_count() > 1]
    groups = [
        [(mine_t, other_t, p) for p in ones] + [(mine_s, other_s, p) for p in ones[1:]],
        [(mine_s, other_s, 1)] + [(mine_t, other_t, p) for p in rest],
        [(mine_s, other_s, p) for p in rest],
    ]
    for group in groups:
        values = [mine[p] for mine, _, p in group]
        got, start = partners.swap(join(*values) if len(values) > 1 else values[0]), 0
        for (_, other, p), value in zip(group, values):
            other[p] = (got, start, start + value.shape[1])
            start += value.shape[1]
    places = range(1 << levels)
    mine = [[(side[p], 0, side[p].shape[1]) for p in places] for side in (mine_t, mine_s)]
    return mine, [[side[p] for p in places] for side in (other_t, other_s)]


def tile_rows(mine, other, n_row, core):
    if core == 0:
        return [(*mine[p], 0) for p in range(n_row)]
    return [(*mine[0], 0)] + [(*other[p], 1) for p in range(1, n_row)]


def tile_columns(mine, other, n_col, core):
    if core == 1:
        return [(*mine[p], half) for half in (0, 1) for p in range(n_col)]
    return [(*(other[p] if p else mine[0]), half if p else 1 - half) for half in (0, 1) for p in range(n_col)]


def operands_of(*groups):
    arrays = []
    for array, *_ in sum(groups, []):
        if not any(array is other for other in arrays):
            arrays.append(array)
    number = {id(array): k for k, array in enumerate(arrays)}
    return arrays, [[(number[id(array)], *place) for array, *place in group] for group in groups]


def load(refs, group):
    rows = refs[0].shape[0] // 2
    return jnp.concatenate([refs[k][half * rows : (half + 1) * rows, a:b] for k, a, b, half in group])


def by_core(body, choices):
    core = lax.rem(lax.axis_index("blk"), 2)
    for k, choice in enumerate(choices):
        pl.when(core == k)(functools.partial(body, choice))


def tree_sum(values):
    while len(values) > 1:
        values = [values[i] + values[i + 1] for i in range(0, len(values), 2)]
    return values[0]


def join_kernel(axis, *refs):
    *parts, both = refs
    start = 0
    for part in parts:
        stop = start + part.shape[axis]
        both[(slice(None),) * axis + (slice(start, stop),)] = part[...]
        start = stop


def put_sums(parts, row_part, col_part):
    pad = jnp.zeros((parts[0].shape[0], 128 - len(parts)), jnp.float32)
    by_row = jnp.transpose(jnp.concatenate([jnp.sum(p, 1, keepdims=True) for p in parts] + [pad], 1))
    for k, part in enumerate(parts):
        by_col = jnp.sum(part, 0, keepdims=True)
        for source, sums in ((by_row[k : k + 1], row_part), (by_col, col_part)):
            rows = sums.shape[2]
            for p in range(sums.shape[1]):
                sums[k, p : p + 1, :] = source[:, p * rows : (p + 1) * rows]


def gram_kernel(choices, *refs):
    *arrays, gram_s, gram_t, row_part, col_part = refs

    def multiply(groups):
        row_t, row_s, col_t, col_s = [load(arrays, group) for group in groups]
        dims = (((1,), (1,)), ((), ()))
        gram_s[...] = lax.dot_general(row_s, col_s, dims, preferred_element_type=jnp.float32)
        gram_t[...] = lax.dot_general(row_t, col_t, dims, preferred_element_type=jnp.float32)

    by_core(multiply, choices)
    student, teacher = gram_s[...], gram_t[...]
    put_sums([student * student, teacher * teacher, student * teacher], row_part, col_part)


def call(kernel, operands, outputs, flops=0, **options):
    size = sum(math.prod(a.shape) * a.dtype.itemsize for a in [*operands, *jax.tree.leaves(outputs)])
    return pl.pallas_call(
        kernel,
        out_shape=outputs,
        **options,
        compiler_params=pltpu.CompilerParams(vmem_limit_bytes=VMEM),
        cost_estimate=pl.CostEstimate(flops=flops, bytes_accessed=size, transcendentals=0),
    )(*operands)


def output_kernel(n_arrays, choices, total, gram_s, gram_t, row_sum, col_sum, *refs):
    *refs, students = refs
    own, share, *pieces = refs[n_arrays:]

    def fetch(group):
        students[...] = load(refs[:n_arrays], group)

    by_core(fetch, choices)
    col_s = students[...]
    row_alpha, row_beta, _ = coefficients(row_sum[0], row_sum[1], row_sum[2], total)
    col_alpha, col_beta, terms = coefficients(col_sum[0], col_sum[1], col_sum[2], total)
    row_ab = jnp.transpose(jnp.concatenate([row_alpha, row_beta] * 4))
    row_w = row_ab[:, 0:1] * gram_s[...] - row_ab[:, 1:2] * gram_t[...]
    col_w = col_alpha * gram_s[...] - col_beta * gram_t[...]
    out = jnp.dot(row_w.astype(jnp.bfloat16), col_s, preferred_element_type=jnp.float32)
    out += jnp.dot(col_w.astype(jnp.bfloat16), col_s, preferred_element_type=jnp.float32)

    rows, width = own.shape
    own[...] = out[:rows]
    term = jnp.sum(terms, axis=1, keepdims=True)
    share[...] = jnp.broadcast_to(term, share.shape)
    largest = jnp.max(jnp.max(jnp.abs(out), axis=0, keepdims=True), axis=1, keepdims=True)
    power = jnp.clip(jnp.floor(jnp.log2(largest)), -100.0, 100.0)
    term = term * SHARE_SCALE
    high = term.astype(jnp.bfloat16).astype(jnp.float32)
    middle = (term - high).astype(jnp.bfloat16).astype(jnp.float32)
    low = term - high - middle
    lane = lax.broadcasted_iota(jnp.int32, (rows, 128), 1)
    extra = jnp.where(lane == 0, power, jnp.where(lane == 1, high, jnp.where(lane == 2, middle, low)))
    scaled = out * jnp.exp2(13.0 - power)
    for k, piece in enumerate(pieces):
        piece[:, :width] = scaled[(k + 1) * rows : (k + 2) * rows]
        piece[:, width:] = extra


def final_kernel(total, own, share, *refs):
    *pieces, grad, loss = refs
    width = own.shape[1]
    grads, terms = [own[...]], [share[0:1, 0:1]]
    for piece in pieces:
        extra = piece[:, width:]
        grads.append(piece[:, :width] * jnp.exp2(extra[:, 0:1] - 13.0))
        terms.append((extra[0:1, 1:2] + extra[0:1, 2:3] + extra[0:1, 3:4]) * (1.0 / SHARE_SCALE))
    grad[...] = tree_sum(grads)
    loss[...] = tree_sum(terms) * (1.0 / total)


def exchange_sums(row_part, col_part, partners):
    n_row, n_col, rows = row_part.shape[1], col_part.shape[1], row_part.shape[2]
    got = partners.swap(jnp.concatenate([row_part, col_part], 1))
    all_rows = jnp.concatenate([row_part, got[:, :n_row]], 1)
    all_cols = col_part + got[:, n_row:]
    all_cols = jnp.pad(all_cols, ((0, 0), (0, 2 * n_row - n_col), (0, 0)))
    first = lax.axis_index("blk") % 2 == 0
    sums = jnp.where(first, all_rows, all_cols)
    for b in range(len(partners.rows)):
        got = partners.step(sums, b).reshape(3, -1, 2, 1 << b, rows)
        sums += jnp.flip(got, 2).reshape(sums.shape)
    got = partners.swap(sums)
    return (
        jnp.where(first, sums[:, :n_row], got[:, n_row:]),
        jnp.where(first, got[:, :n_col], sums[:, :n_col]),
    )


def per_device(teacher, student):
    rows = teacher.shape[0]
    partners = Partners(lax.axis_size("blk"), lax.axis_size("inner"))
    total = rows * partners.count
    n_row, n_col = 1 << len(partners.rows), 1 << len(partners.columns)
    shape, width = (n_row * rows, 2 * n_col * rows), student.shape[1]

    def f32(*dims):
        return jax.ShapeDtypeStruct(dims, jnp.float32)

    mine, other = gather(teacher, student, partners)
    tiles = []
    for core in (0, 1):
        tiles += [tile_rows(*pair, n_row, core) for pair in zip(mine, other)]
        tiles += [tile_columns(*pair, n_col, core) for pair in zip(mine, other)]
    arrays, groups = operands_of(*tiles)
    gram_s, gram_t, row_part, col_part = call(
        functools.partial(gram_kernel, [groups[:4], groups[4:]]),
        arrays,
        [f32(*shape), f32(*shape), f32(3, n_row, rows), f32(3, 2 * n_col, rows)],
        2 * math.prod(shape) * (teacher.shape[1] + width),
    )
    row_sum, col_sum = exchange_sums(row_part, col_part, partners)
    row_sum, col_sum = row_sum.reshape(3, 1, -1), col_sum.reshape(3, 1, -1)

    arrays, groups = operands_of(tiles[3], tiles[7])
    own, share, *pieces = call(
        functools.partial(output_kernel, len(arrays), groups, total),
        [gram_s, gram_t, row_sum, col_sum, *arrays],
        [f32(rows, width), f32(8, 128)] + [f32(rows, width + 128)] * (n_row - 1),
        4 * math.prod(shape) * width,
        scratch_shapes=[pltpu.VMEM((shape[1], width), student.dtype)],
    )
    got = [
        partners.row(value.astype(jnp.float16), mask).astype(jnp.float32)
        for value, mask in zip(pieces, span(partners.rows)[1:])
    ]
    grad, loss = call(
        functools.partial(final_kernel, total), [own, share, *got], [f32(rows, width), f32(1, 1)]
    )
    return (loss[0, 0], grad)


def solution(mesh):
    return jax.shard_map(
        per_device,
        mesh=mesh,
        in_specs=(P(AXES, None), P(AXES, None)),
        out_specs=(P(), P(AXES, None)),
        check_vma=False,
    )
```

```python
import functools
import math

import jax
import jax.numpy as jnp
from jax import lax
from jax.experimental import pallas as pl
from jax.experimental.pallas import tpu as pltpu
from jax.sharding import PartitionSpec as P

DS = 768
AXES = ("blk", "inner")
VMEM = 48 * 2**20
SHARE_SCALE = 8.0


EPSILON = 1e-06


def coefficients(sq_student, sq_teacher, cross, total):
    norm_student = jnp.sqrt(sq_student + EPSILON)
    norm_teacher = jnp.sqrt(sq_teacher + EPSILON)
    factor = 2.0 * math.sqrt(total * DS) / total
    cubed = norm_student * norm_student * norm_student
    alpha = factor * (EPSILON / norm_student + cross / norm_teacher) / cubed
    beta = factor / (norm_student * norm_teacher)
    terms = (
        sq_student / (norm_student * norm_student)
        + sq_teacher / (norm_teacher * norm_teacher)
        - 2.0 * cross / (norm_student * norm_teacher)
    )
    return (alpha, beta, terms)


def span(masks):
    out = [0]
    for mask in masks:
        out += [mask ^ other for other in out]
    return out


def subgroups(blocks, inner):
    bits = [1 << b for b in range((inner - 1).bit_length())]
    bits += [inner << b for b in range(1, (blocks - 1).bit_length())]
    return (bits[0::2], bits[1::2] + [inner])


def send(value, mask, count):
    return lax.ppermute(value, AXES, [(i, i ^ mask) for i in range(count)])


def after(value, other):
    return lax.optimization_barrier((value, other))[0]


def join(*values):
    shape = (values[0].shape[0], sum(value.shape[1] for value in values))
    return call(join_kernel, values, jax.ShapeDtypeStruct(shape, values[0].dtype))


def gather(teacher, student, row_masks, col_masks, count):
    *plane_masks, core_mask = col_masks
    row_t, row_s, col_t, col_s = {}, {}, {}, {}
    sides = ((row_t, row_s, row_masks), (col_t, col_s, plane_masks))

    def whole(value):
        return (value, 0, value.shape[1])

    def forward(side, masks, keep):
        for level in range(2, len(masks) + 1):
            for place in range(1 << len(masks)):
                if place.bit_count() == level and keep(place):
                    top = place.bit_length() - 1
                    side[place] = whole(send(side[place ^ (1 << top)][0], masks[top], count))

    for side_t, _, masks in reversed(sides):
        side_t[1] = whole(send(teacher, masks[0], count))
    for _, side_s, masks in reversed(sides):
        for b, mask in enumerate(masks):
            if b:
                side_s[1 << b] = whole(send(student, mask, count))
    own = join(teacher, student)
    late = after(teacher, (row_s[2][0], col_s[2][0], own))
    for side_t, _, masks in reversed(sides):
        side_t[0] = (own, 0, teacher.shape[1])
        for b, mask in enumerate(masks):
            if b:
                side_t[1 << b] = whole(send(late, mask, count))

    def long_way(side_s, masks, gate):
        forward(side_s, masks, lambda place: not place & 1)
        half = range(0, 1 << len(masks), 2)
        parts = [own[:, teacher.shape[1] :]] + [side_s[p][0] for p in half if p]
        side_s[0] = (own, teacher.shape[1], own.shape[1])
        got = send(after(join(*parts), gate), masks[0], count)
        for k, p in enumerate(half):
            side_s[p | 1] = (got, k * student.shape[1], (k + 1) * student.shape[1])

    first = (row_t[1][0], col_t[1][0])
    long_way(col_s, plane_masks, ())
    long_way(row_s, row_masks, first)
    row_t[1], col_t[1] = map(whole, after(first, (row_t[2][0], col_t[2][0])))
    for side_t, _, masks in reversed(sides):
        forward(side_t, masks, lambda place: True)

    core_t, core_s = {}, {}
    ones = [0] + [1 << b for b in range(len(plane_masks))]
    rest = [p for p in range(1 << len(plane_masks)) if p.bit_count() > 1]
    swaps = [
        [(col_t, core_t, p) for p in ones] + [(col_s, core_s, p) for p in col_s if not p & 1],
        [(col_t, core_t, p) for p in rest],
        [(col_s, core_s, p) for p in col_s if p & 1],
    ]
    for swap in swaps:
        arrays = list({id(side[p][0]): side[p][0] for side, _, p in swap}.values())
        got = send(join(*arrays) if len(arrays) > 1 else arrays[0], core_mask, count)
        starts = {id(array): sum(a.shape[1] for a in arrays[:k]) for k, array in enumerate(arrays)}
        for side, core, p in swap:
            array, start, stop = side[p]
            core[p] = (got, starts[id(array)] + start, starts[id(array)] + stop)
    places = sorted(col_t)
    return (
        [row_t[p] for p in sorted(row_t)],
        [row_s[p] for p in sorted(row_s)],
        [col_t[p] for p in places] + [core_t[p] for p in places],
        [col_s[p] for p in places] + [core_s[p] for p in places],
    )


def operands_of(*groups):
    arrays = []
    for array, _, _ in sum(groups, []):
        if not any(array is other for other in arrays):
            arrays.append(array)
    number = {id(array): k for k, array in enumerate(arrays)}
    return arrays, [[(number[id(array)], start, stop) for array, start, stop in group] for group in groups]


def load(refs, group):
    return jnp.concatenate([refs[k][:, start:stop] for k, start, stop in group])


def tree_sum(values):
    while len(values) > 1:
        values = [values[i] + values[i + 1] for i in range(0, len(values), 2)]
    return values[0]


def join_kernel(*refs):
    *parts, both = refs
    start = 0
    for part in parts:
        both[:, start : start + part.shape[1]] = part[...]
        start += part.shape[1]


def put_sums(parts, row_part, col_part):
    pad = jnp.zeros((parts[0].shape[0], 128 - len(parts)), jnp.float32)
    by_row = jnp.transpose(jnp.concatenate([jnp.sum(p, 1, keepdims=True) for p in parts] + [pad], 1))
    for k, part in enumerate(parts):
        by_col = jnp.sum(part, 0, keepdims=True)
        for source, sums in ((by_row[k : k + 1], row_part), (by_col, col_part)):
            rows = sums.shape[2]
            for p in range(sums.shape[1]):
                sums[k, p : p + 1, :] = source[:, p * rows : (p + 1) * rows]


def gram_kernel(groups, *refs):
    *arrays, gram_s, gram_t, row_part, col_part = refs
    row_t, row_s, col_t, col_s = [load(arrays, group) for group in groups]
    dims = (((1,), (1,)), ((), ()))
    student = lax.dot_general(row_s, col_s, dims, preferred_element_type=jnp.float32)
    teacher = lax.dot_general(row_t, col_t, dims, preferred_element_type=jnp.float32)
    gram_s[...], gram_t[...] = student, teacher
    put_sums([student * student, teacher * teacher, student * teacher], row_part, col_part)


def call(kernel, operands, outputs, flops=0, **options):
    size = sum(math.prod(a.shape) * a.dtype.itemsize for a in [*operands, *jax.tree.leaves(outputs)])
    return pl.pallas_call(
        kernel,
        out_shape=outputs,
        **options,
        compiler_params=pltpu.CompilerParams(vmem_limit_bytes=VMEM),
        cost_estimate=pl.CostEstimate(flops=flops, bytes_accessed=size, transcendentals=0),
    )(*operands)


def output_kernel(n_arrays, group, total, gram_s, gram_t, row_sum, col_sum, *refs):
    col_s = load(refs[:n_arrays], group)
    own, share, *pieces = refs[n_arrays:]
    row_alpha, row_beta, _ = coefficients(row_sum[0], row_sum[1], row_sum[2], total)
    col_alpha, col_beta, terms = coefficients(col_sum[0], col_sum[1], col_sum[2], total)
    row_ab = jnp.transpose(jnp.concatenate([row_alpha, row_beta] * 4))
    row_w = row_ab[:, 0:1] * gram_s[...] - row_ab[:, 1:2] * gram_t[...]
    col_w = col_alpha * gram_s[...] - col_beta * gram_t[...]
    out = jnp.dot(row_w.astype(jnp.bfloat16), col_s, preferred_element_type=jnp.float32)
    out += jnp.dot(col_w.astype(jnp.bfloat16), col_s, preferred_element_type=jnp.float32)

    rows, width = own.shape
    own[...] = out[:rows]
    term = jnp.sum(terms, axis=1, keepdims=True)
    share[...] = jnp.broadcast_to(term, share.shape)
    largest = jnp.max(jnp.max(jnp.abs(out), axis=0, keepdims=True), axis=1, keepdims=True)
    power = jnp.clip(jnp.floor(jnp.log2(largest)), -100.0, 100.0)
    term = term * SHARE_SCALE
    high = term.astype(jnp.bfloat16).astype(jnp.float32)
    middle = (term - high).astype(jnp.bfloat16).astype(jnp.float32)
    low = term - high - middle
    lane = lax.broadcasted_iota(jnp.int32, (rows, 128), 1)
    extra = jnp.where(lane == 0, power, jnp.where(lane == 1, high, jnp.where(lane == 2, middle, low)))
    scaled = out * jnp.exp2(13.0 - power)
    for k, piece in enumerate(pieces):
        piece[:, :width] = scaled[(k + 1) * rows : (k + 2) * rows]
        piece[:, width:] = extra


def final_kernel(total, own, share, *refs):
    *pieces, grad, loss = refs
    width = own.shape[1]
    grads, terms = [own[...]], [share[0:1, 0:1]]
    for piece in pieces:
        extra = piece[:, width:]
        grads.append(piece[:, :width] * jnp.exp2(extra[:, 0:1] - 13.0))
        terms.append((extra[0:1, 1:2] + extra[0:1, 2:3] + extra[0:1, 3:4]) * (1.0 / SHARE_SCALE))
    grad[...] = tree_sum(grads)
    loss[...] = tree_sum(terms) * (1.0 / total)


def exchange_sums(row_part, col_part, row_masks, col_masks, count):
    *plane_masks, core_mask = col_masks
    n_row, n_col, rows = row_part.shape[1], col_part.shape[1], row_part.shape[2]

    def other_core_first(cols):
        return jnp.roll(cols, n_col // 2, 1)

    got = send(jnp.concatenate([row_part, col_part], 1), core_mask, count)
    all_rows = jnp.concatenate([row_part, got[:, :n_row]], 1)
    all_cols = col_part + other_core_first(got[:, n_row:])
    all_cols = jnp.pad(all_cols, ((0, 0), (0, 2 * n_row - n_col), (0, 0)))
    first = (lax.axis_index("blk") & 1) == 0
    sums = jnp.where(first, all_rows, all_cols)
    for b in range(len(row_masks)):
        pairs = []
        for i in range(count):
            masks = plane_masks if i & core_mask else row_masks
            if b < len(masks):
                pairs.append((i, i ^ masks[b]))
        got = lax.ppermute(sums, AXES, pairs).reshape(3, -1, 2, 1 << b, rows)
        sums += jnp.flip(got, 2).reshape(sums.shape)
    got = send(sums, core_mask, count)
    return (
        jnp.where(first, sums[:, :n_row], got[:, n_row:]),
        jnp.where(first, other_core_first(got[:, :n_col]), sums[:, :n_col]),
    )


def per_device(teacher, student):
    rows = teacher.shape[0]
    blocks = lax.axis_size("blk")
    inner = lax.axis_size("inner")
    count = blocks * inner
    total = rows * count
    row_masks, col_masks = subgroups(blocks, inner)
    n_row, n_col = 1 << len(row_masks), 1 << len(col_masks)

    pieces = gather(teacher, student, row_masks, col_masks, count)
    shape, width = (n_row * rows, n_col * rows), student.shape[1]

    def f32(*dims):
        return jax.ShapeDtypeStruct(dims, jnp.float32)

    arrays, groups = operands_of(*pieces)
    gram_s, gram_t, row_part, col_part = call(
        functools.partial(gram_kernel, groups),
        arrays,
        [f32(*shape), f32(*shape), f32(3, n_row, rows), f32(3, n_col, rows)],
        2 * math.prod(shape) * (teacher.shape[1] + width),
    )
    row_part, col_part = exchange_sums(row_part, col_part, row_masks, col_masks, count)
    row_sum, col_sum = row_part.reshape(3, 1, -1), col_part.reshape(3, 1, -1)

    arrays, (group,) = operands_of(pieces[3])
    own, share, *pieces = call(
        functools.partial(output_kernel, len(arrays), group, total),
        [gram_s, gram_t, row_sum, col_sum, *arrays],
        [f32(rows, width), f32(8, 128)] + [f32(rows, width + 128)] * (n_row - 1),
        4 * math.prod(shape) * width,
    )
    got = [
        send(value.astype(jnp.float16), mask, count).astype(jnp.float32)
        for value, mask in zip(pieces, span(row_masks)[1:])
    ]
    grad, loss = call(
        functools.partial(final_kernel, total), [own, share, *got], [f32(rows, width), f32(1, 1)]
    )
    return (loss[0, 0], grad)


def solution(mesh):
    return jax.shard_map(
        per_device,
        mesh=mesh,
        in_specs=(P(AXES, None), P(AXES, None)),
        out_specs=(P(), P(AXES, None)),
        check_vma=False,
    )
```

```python
import functools
import math

import jax
import jax.numpy as jnp
from jax import lax
from jax.experimental import pallas as pl
from jax.experimental.pallas import tpu as pltpu
from jax.sharding import PartitionSpec as P

DS = 768
AXES = ("blk", "inner")
VMEM = 48 * 2**20
SHARE_SCALE = 8.0


EPSILON = 1e-06


def coefficients(sq_student, sq_teacher, cross, total):
    norm_student = jnp.sqrt(sq_student + EPSILON)
    norm_teacher = jnp.sqrt(sq_teacher + EPSILON)
    factor = 2.0 * math.sqrt(total * DS) / total
    cubed = norm_student * norm_student * norm_student
    alpha = factor * (EPSILON / norm_student + cross / norm_teacher) / cubed
    beta = factor / (norm_student * norm_teacher)
    terms = (
        sq_student / (norm_student * norm_student)
        + sq_teacher / (norm_teacher * norm_teacher)
        - 2.0 * cross / (norm_student * norm_teacher)
    )
    return (alpha, beta, terms)


def span(masks):
    out = [0]
    for mask in masks:
        out += [mask ^ other for other in out]
    return out


def subgroups(blocks, inner):
    bits = [1 << b for b in range((inner - 1).bit_length())]
    bits += [inner << b for b in range(1, (blocks - 1).bit_length())]
    return (bits[0::2], bits[1::2] + [inner])


def send(value, mask, count):
    return lax.ppermute(value, AXES, [(i, i ^ mask) for i in range(count)])


def after(value, other):
    return lax.optimization_barrier((value, other))[0]


def join(*values):
    shape = (values[0].shape[0], sum(value.shape[1] for value in values))
    return call(join_kernel, values, jax.ShapeDtypeStruct(shape, values[0].dtype))


def gather(teacher, student, row_masks, col_masks, count):
    *plane_masks, core_mask = col_masks
    row_t, row_s, col_t, col_s = {}, {}, {}, {}
    sides = ((row_t, row_s, row_masks), (col_t, col_s, plane_masks))

    def whole(value):
        return (value, 0, value.shape[1])

    def forward(side, masks, keep):
        for level in range(2, len(masks) + 1):
            for place in range(1 << len(masks)):
                if place.bit_count() == level and keep(place):
                    top = place.bit_length() - 1
                    side[place] = whole(send(side[place ^ (1 << top)][0], masks[top], count))

    for side_t, _, masks in reversed(sides):
        side_t[1] = whole(send(teacher, masks[0], count))
    swapped = [send(value, core_mask, count) for value in (teacher, student)]
    own = join(teacher, student)
    late_t, late_s = after((teacher, student), (*swapped, own))
    for side_t, side_s, masks in reversed(sides):
        side_t[0] = (own, 0, teacher.shape[1])
        for b, mask in enumerate(masks):
            if b:
                side_s[1 << b] = whole(send(late_s, mask, count))
                side_t[1 << b] = whole(send(late_t, mask, count))

    def long_way(side_s, masks, gate):
        forward(side_s, masks, lambda place: not place & 1)
        half = range(0, 1 << len(masks), 2)
        parts = [own[:, teacher.shape[1] :]] + [side_s[p][0] for p in half if p]
        side_s[0] = (own, teacher.shape[1], own.shape[1])
        got = send(after(join(*parts), gate), masks[0], count)
        for k, p in enumerate(half):
            side_s[p | 1] = (got, k * student.shape[1], (k + 1) * student.shape[1])

    first = (row_t[1][0], col_t[1][0])
    long_way(col_s, plane_masks, ())
    long_way(row_s, row_masks, first)
    row_t[1], col_t[1] = map(whole, after(first, (row_t[2][0], col_t[2][0])))
    for side_t, _, masks in reversed(sides):
        forward(side_t, masks, lambda place: True)

    core_t, core_s = {0: whole(swapped[0])}, {0: whole(swapped[1])}
    ones = [1 << b for b in range(len(plane_masks))]
    rest = [p for p in range(1 << len(plane_masks)) if p.bit_count() > 1]
    swaps = [
        [(col_t, core_t, p) for p in ones] + [(col_s, core_s, p) for p in col_s if p and not p & 1],
        [(col_t, core_t, p) for p in rest],
        [(col_s, core_s, p) for p in col_s if p & 1],
    ]
    for swap in swaps:
        arrays = list({id(side[p][0]): side[p][0] for side, _, p in swap}.values())
        got = send(join(*arrays) if len(arrays) > 1 else arrays[0], core_mask, count)
        starts = {id(array): sum(a.shape[1] for a in arrays[:k]) for k, array in enumerate(arrays)}
        for side, core, p in swap:
            array, start, stop = side[p]
            core[p] = (got, starts[id(array)] + start, starts[id(array)] + stop)
    places = sorted(col_t)
    return (
        [row_t[p] for p in sorted(row_t)],
        [row_s[p] for p in sorted(row_s)],
        [col_t[p] for p in places] + [core_t[p] for p in places],
        [col_s[p] for p in places] + [core_s[p] for p in places],
    )


def operands_of(*groups):
    arrays = []
    for array, _, _ in sum(groups, []):
        if not any(array is other for other in arrays):
            arrays.append(array)
    number = {id(array): k for k, array in enumerate(arrays)}
    return arrays, [[(number[id(array)], start, stop) for array, start, stop in group] for group in groups]


def load(refs, group):
    return jnp.concatenate([refs[k][:, start:stop] for k, start, stop in group])


def tree_sum(values):
    while len(values) > 1:
        values = [values[i] + values[i + 1] for i in range(0, len(values), 2)]
    return values[0]


def join_kernel(*refs):
    *parts, both = refs
    start = 0
    for part in parts:
        both[:, start : start + part.shape[1]] = part[...]
        start += part.shape[1]


def put_sums(parts, row_part, col_part):
    pad = jnp.zeros((parts[0].shape[0], 128 - len(parts)), jnp.float32)
    by_row = jnp.transpose(jnp.concatenate([jnp.sum(p, 1, keepdims=True) for p in parts] + [pad], 1))
    for k, part in enumerate(parts):
        by_col = jnp.sum(part, 0, keepdims=True)
        for source, sums in ((by_row[k : k + 1], row_part), (by_col, col_part)):
            rows = sums.shape[2]
            for p in range(sums.shape[1]):
                sums[k, p : p + 1, :] = source[:, p * rows : (p + 1) * rows]


def gram_kernel(groups, *refs):
    *arrays, gram_s, gram_t, row_part, col_part = refs
    row_t, row_s, col_t, col_s = [load(arrays, group) for group in groups]
    dims = (((1,), (1,)), ((), ()))
    student = lax.dot_general(row_s, col_s, dims, preferred_element_type=jnp.float32)
    teacher = lax.dot_general(row_t, col_t, dims, preferred_element_type=jnp.float32)
    gram_s[...], gram_t[...] = student, teacher
    put_sums([student * student, teacher * teacher, student * teacher], row_part, col_part)


def call(kernel, operands, outputs, flops=0, **options):
    size = sum(math.prod(a.shape) * a.dtype.itemsize for a in [*operands, *jax.tree.leaves(outputs)])
    return pl.pallas_call(
        kernel,
        out_shape=outputs,
        **options,
        compiler_params=pltpu.CompilerParams(vmem_limit_bytes=VMEM),
        cost_estimate=pl.CostEstimate(flops=flops, bytes_accessed=size, transcendentals=0),
    )(*operands)


def output_kernel(n_arrays, group, total, gram_s, gram_t, row_sum, col_sum, *refs):
    col_s = load(refs[:n_arrays], group)
    own, share, *pieces = refs[n_arrays:]
    row_alpha, row_beta, _ = coefficients(row_sum[0], row_sum[1], row_sum[2], total)
    col_alpha, col_beta, terms = coefficients(col_sum[0], col_sum[1], col_sum[2], total)
    row_ab = jnp.transpose(jnp.concatenate([row_alpha, row_beta] * 4))
    row_w = row_ab[:, 0:1] * gram_s[...] - row_ab[:, 1:2] * gram_t[...]
    col_w = col_alpha * gram_s[...] - col_beta * gram_t[...]
    out = jnp.dot(row_w.astype(jnp.bfloat16), col_s, preferred_element_type=jnp.float32)
    out += jnp.dot(col_w.astype(jnp.bfloat16), col_s, preferred_element_type=jnp.float32)

    rows, width = own.shape
    own[...] = out[:rows]
    term = jnp.sum(terms, axis=1, keepdims=True)
    share[...] = jnp.broadcast_to(term, share.shape)
    largest = jnp.max(jnp.max(jnp.abs(out), axis=0, keepdims=True), axis=1, keepdims=True)
    power = jnp.clip(jnp.floor(jnp.log2(largest)), -100.0, 100.0)
    term = term * SHARE_SCALE
    high = term.astype(jnp.bfloat16).astype(jnp.float32)
    middle = (term - high).astype(jnp.bfloat16).astype(jnp.float32)
    low = term - high - middle
    lane = lax.broadcasted_iota(jnp.int32, (rows, 128), 1)
    extra = jnp.where(lane == 0, power, jnp.where(lane == 1, high, jnp.where(lane == 2, middle, low)))
    scaled = out * jnp.exp2(13.0 - power)
    for k, piece in enumerate(pieces):
        piece[:, :width] = scaled[(k + 1) * rows : (k + 2) * rows]
        piece[:, width:] = extra


def final_kernel(total, own, share, *refs):
    *pieces, grad, loss = refs
    width = own.shape[1]
    grads, terms = [own[...]], [share[0:1, 0:1]]
    for piece in pieces:
        extra = piece[:, width:]
        grads.append(piece[:, :width] * jnp.exp2(extra[:, 0:1] - 13.0))
        terms.append((extra[0:1, 1:2] + extra[0:1, 2:3] + extra[0:1, 3:4]) * (1.0 / SHARE_SCALE))
    grad[...] = tree_sum(grads)
    loss[...] = tree_sum(terms) * (1.0 / total)


def exchange_sums(row_part, col_part, row_masks, col_masks, count):
    *plane_masks, core_mask = col_masks
    n_row, n_col, rows = row_part.shape[1], col_part.shape[1], row_part.shape[2]

    def other_core_first(cols):
        return jnp.roll(cols, n_col // 2, 1)

    got = send(jnp.concatenate([row_part, col_part], 1), core_mask, count)
    all_rows = jnp.concatenate([row_part, got[:, :n_row]], 1)
    all_cols = col_part + other_core_first(got[:, n_row:])
    all_cols = jnp.pad(all_cols, ((0, 0), (0, 2 * n_row - n_col), (0, 0)))
    first = (lax.axis_index("blk") & 1) == 0
    sums = jnp.where(first, all_rows, all_cols)
    for b in range(len(row_masks)):
        pairs = []
        for i in range(count):
            masks = plane_masks if i & core_mask else row_masks
            if b < len(masks):
                pairs.append((i, i ^ masks[b]))
        got = lax.ppermute(sums, AXES, pairs).reshape(3, -1, 2, 1 << b, rows)
        sums += jnp.flip(got, 2).reshape(sums.shape)
    got = send(sums, core_mask, count)
    return (
        jnp.where(first, sums[:, :n_row], got[:, n_row:]),
        jnp.where(first, other_core_first(got[:, :n_col]), sums[:, :n_col]),
    )


def per_device(teacher, student):
    rows = teacher.shape[0]
    blocks = lax.axis_size("blk")
    inner = lax.axis_size("inner")
    count = blocks * inner
    total = rows * count
    row_masks, col_masks = subgroups(blocks, inner)
    n_row, n_col = 1 << len(row_masks), 1 << len(col_masks)

    pieces = gather(teacher, student, row_masks, col_masks, count)
    shape, width = (n_row * rows, n_col * rows), student.shape[1]

    def f32(*dims):
        return jax.ShapeDtypeStruct(dims, jnp.float32)

    arrays, groups = operands_of(*pieces)
    gram_s, gram_t, row_part, col_part = call(
        functools.partial(gram_kernel, groups),
        arrays,
        [f32(*shape), f32(*shape), f32(3, n_row, rows), f32(3, n_col, rows)],
        2 * math.prod(shape) * (teacher.shape[1] + width),
    )
    row_part, col_part = exchange_sums(row_part, col_part, row_masks, col_masks, count)
    row_sum, col_sum = row_part.reshape(3, 1, -1), col_part.reshape(3, 1, -1)

    arrays, (group,) = operands_of(pieces[3])
    own, share, *pieces = call(
        functools.partial(output_kernel, len(arrays), group, total),
        [gram_s, gram_t, row_sum, col_sum, *arrays],
        [f32(rows, width), f32(8, 128)] + [f32(rows, width + 128)] * (n_row - 1),
        4 * math.prod(shape) * width,
    )
    got = [
        send(value.astype(jnp.float16), mask, count).astype(jnp.float32)
        for value, mask in zip(pieces, span(row_masks)[1:])
    ]
    grad, loss = call(
        functools.partial(final_kernel, total), [own, share, *got], [f32(rows, width), f32(1, 1)]
    )
    return (loss[0, 0], grad)


def solution(mesh):
    return jax.shard_map(
        per_device,
        mesh=mesh,
        in_specs=(P(AXES, None), P(AXES, None)),
        out_specs=(P(), P(AXES, None)),
        check_vma=False,
    )
```

```python
import functools
import math

import jax
import jax.numpy as jnp
from jax import lax
from jax.experimental import pallas as pl
from jax.experimental.pallas import tpu as pltpu
from jax.sharding import PartitionSpec as P

DS = 768
AXES = ("blk", "inner")
VMEM = 48 * 2**20
SHARE_SCALE = 8.0


EPSILON = 1e-06


def coefficients(sq_student, sq_teacher, cross, total):
    norm_student = jnp.sqrt(sq_student + EPSILON)
    norm_teacher = jnp.sqrt(sq_teacher + EPSILON)
    factor = 2.0 * math.sqrt(total * DS) / total
    cubed = norm_student * norm_student * norm_student
    alpha = factor * (EPSILON / norm_student + cross / norm_teacher) / cubed
    beta = factor / (norm_student * norm_teacher)
    terms = (
        sq_student / (norm_student * norm_student)
        + sq_teacher / (norm_teacher * norm_teacher)
        - 2.0 * cross / (norm_student * norm_teacher)
    )
    return (alpha, beta, terms)


def span(masks):
    out = [0]
    for mask in masks:
        out += [mask ^ other for other in out]
    return out


def subgroups(blocks, inner):
    bits = [1 << b for b in range((inner - 1).bit_length())]
    bits += [inner << b for b in range(1, (blocks - 1).bit_length())]
    return (bits[0::2], bits[1::2] + [inner])


def send(value, mask, count):
    return lax.ppermute(value, AXES, [(i, i ^ mask) for i in range(count)])


def after(value, other):
    return lax.optimization_barrier((value, other))[0]


def join(*values):
    shape = (values[0].shape[0], sum(value.shape[1] for value in values))
    return call(join_kernel, values, jax.ShapeDtypeStruct(shape, values[0].dtype))


def gather(teacher, student, row_masks, col_masks, count):
    *plane_masks, core_mask = col_masks
    row_t, row_s, col_t, col_s = {}, {}, {}, {}
    sides = ((row_t, row_s, row_masks), (col_t, col_s, plane_masks))

    def whole(value):
        return (value, 0, value.shape[1])

    def forward(side, masks, keep):
        for level in range(2, len(masks) + 1):
            for place in range(1 << len(masks)):
                if place.bit_count() == level and keep(place):
                    top = place.bit_length() - 1
                    side[place] = whole(send(side[place ^ (1 << top)][0], masks[top], count))

    for side_t, _, masks in reversed(sides):
        side_t[1] = whole(send(teacher, masks[0], count))
    swapped = [send(value, core_mask, count) for value in (teacher, student)]
    own = join(teacher, student)
    late_t, late_s = after((teacher, student), (*swapped, own))
    for side_t, side_s, masks in reversed(sides):
        side_t[0] = (own, 0, teacher.shape[1])
        for b, mask in enumerate(masks):
            if b:
                side_s[1 << b] = whole(send(late_s, mask, count))
                if side_t is col_t:
                    side_t[1 << b] = whole(send(late_t, mask, count))

    def long_way(side_s, masks, gate):
        forward(side_s, masks, lambda place: not place & 1)
        half = range(0, 1 << len(masks), 2)
        parts = [own[:, teacher.shape[1] :]] + [side_s[p][0] for p in half if p]
        side_s[0] = (own, teacher.shape[1], own.shape[1])
        got = send(after(join(*parts), gate), masks[0], count)
        for k, p in enumerate(half):
            side_s[p | 1] = (got, k * student.shape[1], (k + 1) * student.shape[1])

    first = (row_t[1][0], col_t[1][0])
    long_way(col_s, plane_masks, row_s[2][0])
    long_way(row_s, row_masks, first)
    row_t[1], col_t[1] = map(whole, after(first, col_t[2][0]))
    forward(col_t, plane_masks, lambda place: True)
    for b, mask in enumerate(row_masks):
        if b:
            parts = [row_t[p] for p in range(1 << b)]
            got, start = send(join(*(array[:, i:j] for array, i, j in parts)), mask, count), 0
            for p, (_, i, j) in enumerate(parts):
                row_t[p | 1 << b] = (got, start, start + j - i)
                start += j - i

    core_t, core_s = {0: whole(swapped[0])}, {0: whole(swapped[1])}
    ones = [1 << b for b in range(len(plane_masks))]
    rest = [p for p in range(1 << len(plane_masks)) if p.bit_count() > 1]
    swaps = [
        [(col_t, core_t, p) for p in ones] + [(col_s, core_s, p) for p in col_s if p and not p & 1],
        [(col_t, core_t, p) for p in rest],
        [(col_s, core_s, p) for p in col_s if p & 1],
    ]
    for swap in swaps:
        arrays = list({id(side[p][0]): side[p][0] for side, _, p in swap}.values())
        got = send(join(*arrays) if len(arrays) > 1 else arrays[0], core_mask, count)
        starts = {id(array): sum(a.shape[1] for a in arrays[:k]) for k, array in enumerate(arrays)}
        for side, core, p in swap:
            array, start, stop = side[p]
            core[p] = (got, starts[id(array)] + start, starts[id(array)] + stop)
    places = sorted(col_t)
    return (
        [row_t[p] for p in sorted(row_t)],
        [row_s[p] for p in sorted(row_s)],
        [col_t[p] for p in places] + [core_t[p] for p in places],
        [col_s[p] for p in places] + [core_s[p] for p in places],
    )


def operands_of(*groups):
    arrays = []
    for array, _, _ in sum(groups, []):
        if not any(array is other for other in arrays):
            arrays.append(array)
    number = {id(array): k for k, array in enumerate(arrays)}
    return arrays, [[(number[id(array)], start, stop) for array, start, stop in group] for group in groups]


def load(refs, group):
    return jnp.concatenate([refs[k][:, start:stop] for k, start, stop in group])


def tree_sum(values):
    while len(values) > 1:
        values = [values[i] + values[i + 1] for i in range(0, len(values), 2)]
    return values[0]


def join_kernel(*refs):
    *parts, both = refs
    start = 0
    for part in parts:
        both[:, start : start + part.shape[1]] = part[...]
        start += part.shape[1]


def put_sums(parts, row_part, col_part):
    pad = jnp.zeros((parts[0].shape[0], 128 - len(parts)), jnp.float32)
    by_row = jnp.transpose(jnp.concatenate([jnp.sum(p, 1, keepdims=True) for p in parts] + [pad], 1))
    for k, part in enumerate(parts):
        by_col = jnp.sum(part, 0, keepdims=True)
        for source, sums in ((by_row[k : k + 1], row_part), (by_col, col_part)):
            rows = sums.shape[2]
            for p in range(sums.shape[1]):
                sums[k, p : p + 1, :] = source[:, p * rows : (p + 1) * rows]


def gram_kernel(groups, *refs):
    *arrays, gram_s, gram_t, row_part, col_part = refs
    row_t, row_s, col_t, col_s = [load(arrays, group) for group in groups]
    dims = (((1,), (1,)), ((), ()))
    student = lax.dot_general(row_s, col_s, dims, preferred_element_type=jnp.float32)
    teacher = lax.dot_general(row_t, col_t, dims, preferred_element_type=jnp.float32)
    gram_s[...], gram_t[...] = student, teacher
    put_sums([student * student, teacher * teacher, student * teacher], row_part, col_part)


def call(kernel, operands, outputs, flops=0, **options):
    size = sum(math.prod(a.shape) * a.dtype.itemsize for a in [*operands, *jax.tree.leaves(outputs)])
    return pl.pallas_call(
        kernel,
        out_shape=outputs,
        **options,
        compiler_params=pltpu.CompilerParams(vmem_limit_bytes=VMEM),
        cost_estimate=pl.CostEstimate(flops=flops, bytes_accessed=size, transcendentals=0),
    )(*operands)


def output_kernel(n_arrays, group, total, gram_s, gram_t, row_sum, col_sum, *refs):
    col_s = load(refs[:n_arrays], group)
    own, share, *pieces = refs[n_arrays:]
    row_alpha, row_beta, _ = coefficients(row_sum[0], row_sum[1], row_sum[2], total)
    col_alpha, col_beta, terms = coefficients(col_sum[0], col_sum[1], col_sum[2], total)
    row_ab = jnp.transpose(jnp.concatenate([row_alpha, row_beta] * 4))
    row_w = row_ab[:, 0:1] * gram_s[...] - row_ab[:, 1:2] * gram_t[...]
    col_w = col_alpha * gram_s[...] - col_beta * gram_t[...]
    out = jnp.dot(row_w.astype(jnp.bfloat16), col_s, preferred_element_type=jnp.float32)
    out += jnp.dot(col_w.astype(jnp.bfloat16), col_s, preferred_element_type=jnp.float32)

    rows, width = own.shape
    own[...] = out[:rows]
    term = jnp.sum(terms, axis=1, keepdims=True)
    share[...] = jnp.broadcast_to(term, share.shape)
    largest = jnp.max(jnp.max(jnp.abs(out), axis=0, keepdims=True), axis=1, keepdims=True)
    power = jnp.clip(jnp.floor(jnp.log2(largest)), -100.0, 100.0)
    term = term * SHARE_SCALE
    high = term.astype(jnp.bfloat16).astype(jnp.float32)
    middle = (term - high).astype(jnp.bfloat16).astype(jnp.float32)
    low = term - high - middle
    lane = lax.broadcasted_iota(jnp.int32, (rows, 128), 1)
    extra = jnp.where(lane == 0, power, jnp.where(lane == 1, high, jnp.where(lane == 2, middle, low)))
    scaled = out * jnp.exp2(13.0 - power)
    for k, piece in enumerate(pieces):
        piece[:, :width] = scaled[(k + 1) * rows : (k + 2) * rows]
        piece[:, width:] = extra


def final_kernel(total, own, share, *refs):
    *pieces, grad, loss = refs
    width = own.shape[1]
    grads, terms = [own[...]], [share[0:1, 0:1]]
    for piece in pieces:
        extra = piece[:, width:]
        grads.append(piece[:, :width] * jnp.exp2(extra[:, 0:1] - 13.0))
        terms.append((extra[0:1, 1:2] + extra[0:1, 2:3] + extra[0:1, 3:4]) * (1.0 / SHARE_SCALE))
    grad[...] = tree_sum(grads)
    loss[...] = tree_sum(terms) * (1.0 / total)


def exchange_sums(row_part, col_part, row_masks, col_masks, count):
    *plane_masks, core_mask = col_masks
    n_row, n_col, rows = row_part.shape[1], col_part.shape[1], row_part.shape[2]

    def other_core_first(cols):
        return jnp.roll(cols, n_col // 2, 1)

    got = send(jnp.concatenate([row_part, col_part], 1), core_mask, count)
    all_rows = jnp.concatenate([row_part, got[:, :n_row]], 1)
    all_cols = col_part + other_core_first(got[:, n_row:])
    all_cols = jnp.pad(all_cols, ((0, 0), (0, 2 * n_row - n_col), (0, 0)))
    first = (lax.axis_index("blk") & 1) == 0
    sums = jnp.where(first, all_rows, all_cols)
    for b in range(len(row_masks)):
        pairs = []
        for i in range(count):
            masks = plane_masks if i & core_mask else row_masks
            if b < len(masks):
                pairs.append((i, i ^ masks[b]))
        got = lax.ppermute(sums, AXES, pairs).reshape(3, -1, 2, 1 << b, rows)
        sums += jnp.flip(got, 2).reshape(sums.shape)
    got = send(sums, core_mask, count)
    return (
        jnp.where(first, sums[:, :n_row], got[:, n_row:]),
        jnp.where(first, other_core_first(got[:, :n_col]), sums[:, :n_col]),
    )


def per_device(teacher, student):
    rows = teacher.shape[0]
    blocks = lax.axis_size("blk")
    inner = lax.axis_size("inner")
    count = blocks * inner
    total = rows * count
    row_masks, col_masks = subgroups(blocks, inner)
    n_row, n_col = 1 << len(row_masks), 1 << len(col_masks)

    pieces = gather(teacher, student, row_masks, col_masks, count)
    shape, width = (n_row * rows, n_col * rows), student.shape[1]

    def f32(*dims):
        return jax.ShapeDtypeStruct(dims, jnp.float32)

    arrays, groups = operands_of(*pieces)
    gram_s, gram_t, row_part, col_part = call(
        functools.partial(gram_kernel, groups),
        arrays,
        [f32(*shape), f32(*shape), f32(3, n_row, rows), f32(3, n_col, rows)],
        2 * math.prod(shape) * (teacher.shape[1] + width),
    )
    row_part, col_part = exchange_sums(row_part, col_part, row_masks, col_masks, count)
    row_sum, col_sum = row_part.reshape(3, 1, -1), col_part.reshape(3, 1, -1)

    arrays, (group,) = operands_of(pieces[3])
    own, share, *pieces = call(
        functools.partial(output_kernel, len(arrays), group, total),
        [gram_s, gram_t, row_sum, col_sum, *arrays],
        [f32(rows, width), f32(8, 128)] + [f32(rows, width + 128)] * (n_row - 1),
        4 * math.prod(shape) * width,
    )
    got = [
        send(value.astype(jnp.float16), mask, count).astype(jnp.float32)
        for value, mask in zip(pieces, span(row_masks)[1:])
    ]
    grad, loss = call(
        functools.partial(final_kernel, total), [own, share, *got], [f32(rows, width), f32(1, 1)]
    )
    return (loss[0, 0], grad)


def solution(mesh):
    return jax.shard_map(
        per_device,
        mesh=mesh,
        in_specs=(P(AXES, None), P(AXES, None)),
        out_specs=(P(), P(AXES, None)),
        check_vma=False,
    )
```

```python
import functools
import math

import jax
import jax.numpy as jnp
from jax import lax
from jax.experimental import pallas as pl
from jax.experimental.pallas import tpu as pltpu
from jax.sharding import PartitionSpec as P

DS = 768
AXES = ("blk", "inner")
VMEM = 48 * 2**20
SHARE_SCALE = 8.0


EPSILON = 1e-06


def coefficients(sq_student, sq_teacher, cross, total):
    norm_student = jnp.sqrt(sq_student + EPSILON)
    norm_teacher = jnp.sqrt(sq_teacher + EPSILON)
    factor = 2.0 * math.sqrt(total * DS) / total
    cubed = norm_student * norm_student * norm_student
    alpha = factor * (EPSILON / norm_student + cross / norm_teacher) / cubed
    beta = factor / (norm_student * norm_teacher)
    terms = (
        sq_student / (norm_student * norm_student)
        + sq_teacher / (norm_teacher * norm_teacher)
        - 2.0 * cross / (norm_student * norm_teacher)
    )
    return (alpha, beta, terms)


def span(masks):
    out = [0]
    for mask in masks:
        out += [mask ^ other for other in out]
    return out


def subgroups(blocks, inner):
    bits = [1 << b for b in range((inner - 1).bit_length())]
    bits += [inner << b for b in range(1, (blocks - 1).bit_length())]
    return (bits[0::2], bits[1::2] + [inner])


def send(value, mask, count):
    return lax.ppermute(value, AXES, [(i, i ^ mask) for i in range(count)])


def after(value, other):
    return lax.optimization_barrier((value, other))[0]


def join(*values):
    shape = (values[0].shape[0], sum(value.shape[1] for value in values))
    return call(join_kernel, values, jax.ShapeDtypeStruct(shape, values[0].dtype))


def gather(teacher, student, row_masks, col_masks, count):
    *plane_masks, core_mask = col_masks
    row_t, row_s, col_t, col_s = {}, {}, {}, {}
    sides = ((row_t, row_s, row_masks), (col_t, col_s, plane_masks))

    def whole(value):
        return (value, 0, value.shape[1])

    def forward(side, masks, keep):
        for level in range(2, len(masks) + 1):
            for place in range(1 << len(masks)):
                if place.bit_count() == level and keep(place):
                    top = place.bit_length() - 1
                    side[place] = whole(send(side[place ^ (1 << top)][0], masks[top], count))

    for side_t, _, masks in reversed(sides):
        side_t[1] = whole(send(teacher, masks[0], count))
    swapped = [send(value, core_mask, count) for value in (teacher, student)]
    own = join(teacher, student)
    late_t, late_s = after((teacher, student), swapped)
    for side_t, side_s, masks in reversed(sides):
        side_t[0] = (own, 0, teacher.shape[1])
        for b, mask in enumerate(masks):
            if b:
                side_s[1 << b] = whole(send(late_s, mask, count))
                if side_t is col_t:
                    side_t[1 << b] = whole(send(late_t, mask, count))

    def long_way(side_s, masks, gate):
        forward(side_s, masks, lambda place: not place & 1)
        half = range(0, 1 << len(masks), 2)
        parts = [own[:, teacher.shape[1] :]] + [side_s[p][0] for p in half if p]
        side_s[0] = (own, teacher.shape[1], own.shape[1])
        got = send(after(join(*parts), gate), masks[0], count)
        for k, p in enumerate(half):
            side_s[p | 1] = (got, k * student.shape[1], (k + 1) * student.shape[1])

    first = (row_t[1][0], col_t[1][0])
    long_way(col_s, plane_masks, row_s[2][0])
    long_way(row_s, row_masks, first)
    row_t[1], col_t[1] = map(whole, after(first, col_t[2][0]))
    forward(col_t, plane_masks, lambda place: True)
    for b, mask in enumerate(row_masks):
        if b:
            parts = [row_t[p] for p in range(1 << b)]
            got, start = send(join(*(array[:, i:j] for array, i, j in parts)), mask, count), 0
            for p, (_, i, j) in enumerate(parts):
                row_t[p | 1 << b] = (got, start, start + j - i)
                start += j - i

    core_t, core_s = {0: whole(swapped[0])}, {0: whole(swapped[1])}
    ones = [1 << b for b in range(len(plane_masks))]
    rest = [p for p in range(1 << len(plane_masks)) if p.bit_count() > 1]
    swaps = [
        [(col_t, core_t, p) for p in ones] + [(col_s, core_s, p) for p in col_s if p and not p & 1],
        [(col_t, core_t, p) for p in rest],
        [(col_s, core_s, p) for p in col_s if p & 1],
    ]
    for swap in swaps:
        arrays = list({id(side[p][0]): side[p][0] for side, _, p in swap}.values())
        got = send(join(*arrays) if len(arrays) > 1 else arrays[0], core_mask, count)
        starts = {id(array): sum(a.shape[1] for a in arrays[:k]) for k, array in enumerate(arrays)}
        for side, core, p in swap:
            array, start, stop = side[p]
            core[p] = (got, starts[id(array)] + start, starts[id(array)] + stop)
    places = sorted(col_t)
    return (
        [row_t[p] for p in sorted(row_t)],
        [row_s[p] for p in sorted(row_s)],
        [col_t[p] for p in places] + [core_t[p] for p in places],
        [col_s[p] for p in places] + [core_s[p] for p in places],
    )


def operands_of(*groups):
    arrays = []
    for array, _, _ in sum(groups, []):
        if not any(array is other for other in arrays):
            arrays.append(array)
    number = {id(array): k for k, array in enumerate(arrays)}
    return arrays, [[(number[id(array)], start, stop) for array, start, stop in group] for group in groups]


def load(refs, group):
    return jnp.concatenate([refs[k][:, start:stop] for k, start, stop in group])


def tree_sum(values):
    while len(values) > 1:
        values = [values[i] + values[i + 1] for i in range(0, len(values), 2)]
    return values[0]


def join_kernel(*refs):
    *parts, both = refs
    start = 0
    for part in parts:
        both[:, start : start + part.shape[1]] = part[...]
        start += part.shape[1]


def put_sums(parts, row_part, col_part):
    pad = jnp.zeros((parts[0].shape[0], 128 - len(parts)), jnp.float32)
    by_row = jnp.transpose(jnp.concatenate([jnp.sum(p, 1, keepdims=True) for p in parts] + [pad], 1))
    for k, part in enumerate(parts):
        by_col = jnp.sum(part, 0, keepdims=True)
        for source, sums in ((by_row[k : k + 1], row_part), (by_col, col_part)):
            rows = sums.shape[2]
            for p in range(sums.shape[1]):
                sums[k, p : p + 1, :] = source[:, p * rows : (p + 1) * rows]


def gram_kernel(groups, *refs):
    *arrays, gram_s, gram_t, row_part, col_part = refs
    row_t, row_s, col_t, col_s = [load(arrays, group) for group in groups]
    dims = (((1,), (1,)), ((), ()))
    student = lax.dot_general(row_s, col_s, dims, preferred_element_type=jnp.float32)
    teacher = lax.dot_general(row_t, col_t, dims, preferred_element_type=jnp.float32)
    gram_s[...], gram_t[...] = student, teacher
    put_sums([student * student, teacher * teacher, student * teacher], row_part, col_part)


def call(kernel, operands, outputs, flops=0, **options):
    size = sum(math.prod(a.shape) * a.dtype.itemsize for a in [*operands, *jax.tree.leaves(outputs)])
    return pl.pallas_call(
        kernel,
        out_shape=outputs,
        **options,
        compiler_params=pltpu.CompilerParams(vmem_limit_bytes=VMEM),
        cost_estimate=pl.CostEstimate(flops=flops, bytes_accessed=size, transcendentals=0),
    )(*operands)


def output_kernel(n_arrays, group, total, gram_s, gram_t, row_sum, col_sum, *refs):
    col_s = load(refs[:n_arrays], group)
    own, share, *pieces = refs[n_arrays:]
    row_alpha, row_beta, _ = coefficients(row_sum[0], row_sum[1], row_sum[2], total)
    col_alpha, col_beta, terms = coefficients(col_sum[0], col_sum[1], col_sum[2], total)
    row_ab = jnp.transpose(jnp.concatenate([row_alpha, row_beta] * 4))
    row_w = row_ab[:, 0:1] * gram_s[...] - row_ab[:, 1:2] * gram_t[...]
    col_w = col_alpha * gram_s[...] - col_beta * gram_t[...]
    out = jnp.dot(row_w.astype(jnp.bfloat16), col_s, preferred_element_type=jnp.float32)
    out += jnp.dot(col_w.astype(jnp.bfloat16), col_s, preferred_element_type=jnp.float32)

    rows, width = own.shape
    own[...] = out[:rows]
    term = jnp.sum(terms, axis=1, keepdims=True)
    share[...] = jnp.broadcast_to(term, share.shape)
    largest = jnp.max(jnp.max(jnp.abs(out), axis=0, keepdims=True), axis=1, keepdims=True)
    power = jnp.clip(jnp.floor(jnp.log2(largest)), -100.0, 100.0)
    term = term * SHARE_SCALE
    high = term.astype(jnp.bfloat16).astype(jnp.float32)
    middle = (term - high).astype(jnp.bfloat16).astype(jnp.float32)
    low = term - high - middle
    lane = lax.broadcasted_iota(jnp.int32, (rows, 128), 1)
    extra = jnp.where(lane == 0, power, jnp.where(lane == 1, high, jnp.where(lane == 2, middle, low)))
    scaled = out * jnp.exp2(13.0 - power)
    for k, piece in enumerate(pieces):
        piece[:, :width] = scaled[(k + 1) * rows : (k + 2) * rows]
        piece[:, width:] = extra


def final_kernel(total, own, share, *refs):
    *pieces, grad, loss = refs
    width = own.shape[1]
    grads, terms = [own[...]], [share[0:1, 0:1]]
    for piece in pieces:
        extra = piece[:, width:]
        grads.append(piece[:, :width] * jnp.exp2(extra[:, 0:1] - 13.0))
        terms.append((extra[0:1, 1:2] + extra[0:1, 2:3] + extra[0:1, 3:4]) * (1.0 / SHARE_SCALE))
    grad[...] = tree_sum(grads)
    loss[...] = tree_sum(terms) * (1.0 / total)


def exchange_sums(row_part, col_part, row_masks, col_masks, count):
    *plane_masks, core_mask = col_masks
    n_row, n_col, rows = row_part.shape[1], col_part.shape[1], row_part.shape[2]

    def other_core_first(cols):
        return jnp.roll(cols, n_col // 2, 1)

    got = send(jnp.concatenate([row_part, col_part], 1), core_mask, count)
    all_rows = jnp.concatenate([row_part, got[:, :n_row]], 1)
    all_cols = col_part + other_core_first(got[:, n_row:])
    all_cols = jnp.pad(all_cols, ((0, 0), (0, 2 * n_row - n_col), (0, 0)))
    first = (lax.axis_index("blk") & 1) == 0
    sums = jnp.where(first, all_rows, all_cols)
    for b in range(len(row_masks)):
        pairs = []
        for i in range(count):
            masks = plane_masks if i & core_mask else row_masks
            if b < len(masks):
                pairs.append((i, i ^ masks[b]))
        got = lax.ppermute(sums, AXES, pairs).reshape(3, -1, 2, 1 << b, rows)
        sums += jnp.flip(got, 2).reshape(sums.shape)
    got = send(sums, core_mask, count)
    return (
        jnp.where(first, sums[:, :n_row], got[:, n_row:]),
        jnp.where(first, other_core_first(got[:, :n_col]), sums[:, :n_col]),
    )


def per_device(teacher, student):
    rows = teacher.shape[0]
    blocks = lax.axis_size("blk")
    inner = lax.axis_size("inner")
    count = blocks * inner
    total = rows * count
    row_masks, col_masks = subgroups(blocks, inner)
    n_row, n_col = 1 << len(row_masks), 1 << len(col_masks)

    pieces = gather(teacher, student, row_masks, col_masks, count)
    shape, width = (n_row * rows, n_col * rows), student.shape[1]

    def f32(*dims):
        return jax.ShapeDtypeStruct(dims, jnp.float32)

    arrays, groups = operands_of(*pieces)
    gram_s, gram_t, row_part, col_part = call(
        functools.partial(gram_kernel, groups),
        arrays,
        [f32(*shape), f32(*shape), f32(3, n_row, rows), f32(3, n_col, rows)],
        2 * math.prod(shape) * (teacher.shape[1] + width),
    )
    row_part, col_part = exchange_sums(row_part, col_part, row_masks, col_masks, count)
    row_sum, col_sum = row_part.reshape(3, 1, -1), col_part.reshape(3, 1, -1)

    arrays, (group,) = operands_of(pieces[3])
    own, share, *pieces = call(
        functools.partial(output_kernel, len(arrays), group, total),
        [gram_s, gram_t, row_sum, col_sum, *arrays],
        [f32(rows, width), f32(8, 128)] + [f32(rows, width + 128)] * (n_row - 1),
        4 * math.prod(shape) * width,
    )
    got = [
        send(value.astype(jnp.float16), mask, count).astype(jnp.float32)
        for value, mask in zip(pieces, span(row_masks)[1:])
    ]
    grad, loss = call(
        functools.partial(final_kernel, total), [own, share, *got], [f32(rows, width), f32(1, 1)]
    )
    return (loss[0, 0], grad)


def solution(mesh):
    return jax.shard_map(
        per_device,
        mesh=mesh,
        in_specs=(P(AXES, None), P(AXES, None)),
        out_specs=(P(), P(AXES, None)),
        check_vma=False,
    )
```

```python
import functools
import math

import jax
import jax.numpy as jnp
from jax import lax
from jax.experimental import pallas as pl
from jax.experimental.pallas import tpu as pltpu
from jax.sharding import PartitionSpec as P

DS = 768
AXES = ("blk", "inner")
VMEM = 48 * 2**20
SHARE_SCALE = 8.0


EPSILON = 1e-06


def coefficients(sq_student, sq_teacher, cross, total):
    norm_student = jnp.sqrt(sq_student + EPSILON)
    norm_teacher = jnp.sqrt(sq_teacher + EPSILON)
    factor = 2.0 * math.sqrt(total * DS) / total
    cubed = norm_student * norm_student * norm_student
    alpha = factor * (EPSILON / norm_student + cross / norm_teacher) / cubed
    beta = factor / (norm_student * norm_teacher)
    terms = (
        sq_student / (norm_student * norm_student)
        + sq_teacher / (norm_teacher * norm_teacher)
        - 2.0 * cross / (norm_student * norm_teacher)
    )
    return (alpha, beta, terms)


def span(masks):
    out = [0]
    for mask in masks:
        out += [mask ^ other for other in out]
    return out


def subgroups(blocks, inner):
    bits = [1 << b for b in range((inner - 1).bit_length())]
    bits += [inner << b for b in range(1, (blocks - 1).bit_length())]
    return (bits[0::2], bits[1::2] + [inner])


def send(value, mask, count):
    return lax.ppermute(value, AXES, [(i, i ^ mask) for i in range(count)])


def after(value, other):
    return lax.optimization_barrier((value, other))[0]


def join(*values):
    shape = (values[0].shape[0], sum(value.shape[1] for value in values))
    return call(join_kernel, values, jax.ShapeDtypeStruct(shape, values[0].dtype))


def gather(teacher, student, row_masks, col_masks, count):
    *plane_masks, core_mask = col_masks
    row_t, row_s, col_t, col_s = {}, {}, {}, {}
    sides = ((row_t, row_s, row_masks), (col_t, col_s, plane_masks))

    def whole(value):
        return (value, 0, value.shape[1])

    def forward(side, masks, keep):
        for level in range(2, len(masks) + 1):
            for place in range(1 << len(masks)):
                if place.bit_count() == level and keep(place):
                    top = place.bit_length() - 1
                    side[place] = whole(send(side[place ^ (1 << top)][0], masks[top], count))

    for side_t, _, masks in reversed(sides):
        side_t[1] = whole(send(teacher, masks[0], count))
    swapped = [send(value, core_mask, count) for value in (teacher, student)]
    own = join(teacher, student)
    late_t, late_s = after((teacher, student), swapped)
    for side_t, side_s, masks in reversed(sides):
        side_t[0] = (own, 0, teacher.shape[1])
        for b, mask in enumerate(masks):
            if b:
                side_s[1 << b] = whole(send(late_s, mask, count))
                if side_t is col_t:
                    side_t[1 << b] = whole(send(late_t, mask, count))

    def long_way(side_s, masks, gate):
        forward(side_s, masks, lambda place: not place & 1)
        half = range(0, 1 << len(masks), 2)
        parts = [own[:, teacher.shape[1] :]] + [side_s[p][0] for p in half if p]
        side_s[0] = (own, teacher.shape[1], own.shape[1])
        got = send(after(join(*parts), gate), masks[0], count)
        for k, p in enumerate(half):
            side_s[p | 1] = (got, k * student.shape[1], (k + 1) * student.shape[1])

    first = (row_t[1][0], col_t[1][0])
    long_way(col_s, plane_masks, row_s[2][0])
    long_way(row_s, row_masks, first)
    row_t[1], col_t[1] = map(whole, after(first, col_t[2][0]))
    forward(col_t, plane_masks, lambda place: True)
    for b, mask in enumerate(row_masks):
        if b:
            parts = [row_t[p] for p in range(1 << b)]
            value = after(join(*(array[:, i:j] for array, i, j in parts)), row_s[2][0])
            got, start = send(value, mask, count), 0
            for p, (_, i, j) in enumerate(parts):
                row_t[p | 1 << b] = (got, start, start + j - i)
                start += j - i

    core_t, core_s = {0: whole(swapped[0])}, {0: whole(swapped[1])}
    ones = [1 << b for b in range(len(plane_masks))]
    rest = [p for p in range(1 << len(plane_masks)) if p.bit_count() > 1]
    swaps = [
        [(col_t, core_t, p) for p in ones] + [(col_s, core_s, p) for p in col_s if p and not p & 1],
        [(col_t, core_t, p) for p in rest],
        [(col_s, core_s, p) for p in col_s if p & 1],
    ]
    for swap in swaps:
        arrays = list({id(side[p][0]): side[p][0] for side, _, p in swap}.values())
        value = join(*arrays) if len(arrays) > 1 else arrays[0]
        if swap is swaps[1]:
            value = after(value, col_s[1][0])
        if swap is swaps[2]:
            value = after(value, row_t[max(row_t)][0])
        got = send(value, core_mask, count)
        starts = {id(array): sum(a.shape[1] for a in arrays[:k]) for k, array in enumerate(arrays)}
        for side, core, p in swap:
            array, start, stop = side[p]
            core[p] = (got, starts[id(array)] + start, starts[id(array)] + stop)
    places = sorted(col_t)
    return (
        [row_t[p] for p in sorted(row_t)],
        [row_s[p] for p in sorted(row_s)],
        [col_t[p] for p in places] + [core_t[p] for p in places],
        [col_s[p] for p in places] + [core_s[p] for p in places],
    )


def operands_of(*groups):
    arrays = []
    for array, _, _ in sum(groups, []):
        if not any(array is other for other in arrays):
            arrays.append(array)
    number = {id(array): k for k, array in enumerate(arrays)}
    return arrays, [[(number[id(array)], start, stop) for array, start, stop in group] for group in groups]


def load(refs, group):
    return jnp.concatenate([refs[k][:, start:stop] for k, start, stop in group])


def tree_sum(values):
    while len(values) > 1:
        values = [values[i] + values[i + 1] for i in range(0, len(values), 2)]
    return values[0]


def join_kernel(*refs):
    *parts, both = refs
    start = 0
    for part in parts:
        both[:, start : start + part.shape[1]] = part[...]
        start += part.shape[1]


def put_sums(parts, row_part, col_part):
    pad = jnp.zeros((parts[0].shape[0], 128 - len(parts)), jnp.float32)
    by_row = jnp.transpose(jnp.concatenate([jnp.sum(p, 1, keepdims=True) for p in parts] + [pad], 1))
    for k, part in enumerate(parts):
        by_col = jnp.sum(part, 0, keepdims=True)
        for source, sums in ((by_row[k : k + 1], row_part), (by_col, col_part)):
            rows = sums.shape[2]
            for p in range(sums.shape[1]):
                sums[k, p : p + 1, :] = source[:, p * rows : (p + 1) * rows]


def gram_kernel(groups, *refs):
    *arrays, gram_s, gram_t, row_part, col_part = refs
    row_t, row_s, col_t, col_s = [load(arrays, group) for group in groups]
    dims = (((1,), (1,)), ((), ()))
    student = lax.dot_general(row_s, col_s, dims, preferred_element_type=jnp.float32)
    teacher = lax.dot_general(row_t, col_t, dims, preferred_element_type=jnp.float32)
    gram_s[...], gram_t[...] = student, teacher
    put_sums([student * student, teacher * teacher, student * teacher], row_part, col_part)


def call(kernel, operands, outputs, flops=0, **options):
    size = sum(math.prod(a.shape) * a.dtype.itemsize for a in [*operands, *jax.tree.leaves(outputs)])
    return pl.pallas_call(
        kernel,
        out_shape=outputs,
        **options,
        compiler_params=pltpu.CompilerParams(vmem_limit_bytes=VMEM),
        cost_estimate=pl.CostEstimate(flops=flops, bytes_accessed=size, transcendentals=0),
    )(*operands)


def output_kernel(n_arrays, group, total, gram_s, gram_t, row_sum, col_sum, *refs):
    col_s = load(refs[:n_arrays], group)
    own, share, *pieces = refs[n_arrays:]
    row_alpha, row_beta, _ = coefficients(row_sum[0], row_sum[1], row_sum[2], total)
    col_alpha, col_beta, terms = coefficients(col_sum[0], col_sum[1], col_sum[2], total)
    row_ab = jnp.transpose(jnp.concatenate([row_alpha, row_beta] * 4))
    row_w = row_ab[:, 0:1] * gram_s[...] - row_ab[:, 1:2] * gram_t[...]
    col_w = col_alpha * gram_s[...] - col_beta * gram_t[...]
    out = jnp.dot(row_w.astype(jnp.bfloat16), col_s, preferred_element_type=jnp.float32)
    out += jnp.dot(col_w.astype(jnp.bfloat16), col_s, preferred_element_type=jnp.float32)

    rows, width = own.shape
    own[...] = out[:rows]
    term = jnp.sum(terms, axis=1, keepdims=True)
    share[...] = jnp.broadcast_to(term, share.shape)
    largest = jnp.max(jnp.max(jnp.abs(out), axis=0, keepdims=True), axis=1, keepdims=True)
    power = jnp.clip(jnp.floor(jnp.log2(largest)), -100.0, 100.0)
    term = term * SHARE_SCALE
    high = term.astype(jnp.bfloat16).astype(jnp.float32)
    middle = (term - high).astype(jnp.bfloat16).astype(jnp.float32)
    low = term - high - middle
    lane = lax.broadcasted_iota(jnp.int32, (rows, 128), 1)
    extra = jnp.where(lane == 0, power, jnp.where(lane == 1, high, jnp.where(lane == 2, middle, low)))
    scaled = out * jnp.exp2(13.0 - power)
    for k, piece in enumerate(pieces):
        piece[:, :width] = scaled[(k + 1) * rows : (k + 2) * rows]
        piece[:, width:] = extra


def final_kernel(total, own, share, *refs):
    *pieces, grad, loss = refs
    width = own.shape[1]
    grads, terms = [own[...]], [share[0:1, 0:1]]
    for piece in pieces:
        extra = piece[:, width:]
        grads.append(piece[:, :width] * jnp.exp2(extra[:, 0:1] - 13.0))
        terms.append((extra[0:1, 1:2] + extra[0:1, 2:3] + extra[0:1, 3:4]) * (1.0 / SHARE_SCALE))
    grad[...] = tree_sum(grads)
    loss[...] = tree_sum(terms) * (1.0 / total)


def exchange_sums(row_part, col_part, row_masks, col_masks, count):
    *plane_masks, core_mask = col_masks
    n_row, n_col, rows = row_part.shape[1], col_part.shape[1], row_part.shape[2]

    def other_core_first(cols):
        return jnp.roll(cols, n_col // 2, 1)

    got = send(jnp.concatenate([row_part, col_part], 1), core_mask, count)
    all_rows = jnp.concatenate([row_part, got[:, :n_row]], 1)
    all_cols = col_part + other_core_first(got[:, n_row:])
    all_cols = jnp.pad(all_cols, ((0, 0), (0, 2 * n_row - n_col), (0, 0)))
    first = (lax.axis_index("blk") & 1) == 0
    sums = jnp.where(first, all_rows, all_cols)
    for b in range(len(row_masks)):
        pairs = []
        for i in range(count):
            masks = plane_masks if i & core_mask else row_masks
            if b < len(masks):
                pairs.append((i, i ^ masks[b]))
        got = lax.ppermute(sums, AXES, pairs).reshape(3, -1, 2, 1 << b, rows)
        sums += jnp.flip(got, 2).reshape(sums.shape)
    got = send(sums, core_mask, count)
    return (
        jnp.where(first, sums[:, :n_row], got[:, n_row:]),
        jnp.where(first, other_core_first(got[:, :n_col]), sums[:, :n_col]),
    )


def per_device(teacher, student):
    rows = teacher.shape[0]
    blocks = lax.axis_size("blk")
    inner = lax.axis_size("inner")
    count = blocks * inner
    total = rows * count
    row_masks, col_masks = subgroups(blocks, inner)
    n_row, n_col = 1 << len(row_masks), 1 << len(col_masks)

    pieces = gather(teacher, student, row_masks, col_masks, count)
    shape, width = (n_row * rows, n_col * rows), student.shape[1]

    def f32(*dims):
        return jax.ShapeDtypeStruct(dims, jnp.float32)

    arrays, groups = operands_of(*pieces)
    gram_s, gram_t, row_part, col_part = call(
        functools.partial(gram_kernel, groups),
        arrays,
        [f32(*shape), f32(*shape), f32(3, n_row, rows), f32(3, n_col, rows)],
        2 * math.prod(shape) * (teacher.shape[1] + width),
    )
    row_part, col_part = exchange_sums(row_part, col_part, row_masks, col_masks, count)
    row_sum, col_sum = row_part.reshape(3, 1, -1), col_part.reshape(3, 1, -1)

    arrays, (group,) = operands_of(pieces[3])
    own, share, *pieces = call(
        functools.partial(output_kernel, len(arrays), group, total),
        [gram_s, gram_t, row_sum, col_sum, *arrays],
        [f32(rows, width), f32(8, 128)] + [f32(rows, width + 128)] * (n_row - 1),
        4 * math.prod(shape) * width,
    )
    got = [
        send(value.astype(jnp.float16), mask, count).astype(jnp.float32)
        for value, mask in zip(pieces, span(row_masks)[1:])
    ]
    grad, loss = call(
        functools.partial(final_kernel, total), [own, share, *got], [f32(rows, width), f32(1, 1)]
    )
    return (loss[0, 0], grad)


def solution(mesh):
    return jax.shard_map(
        per_device,
        mesh=mesh,
        in_specs=(P(AXES, None), P(AXES, None)),
        out_specs=(P(), P(AXES, None)),
        check_vma=False,
    )
```

```python
import functools
import math

import jax
import jax.numpy as jnp
from jax import lax
from jax.experimental import pallas as pl
from jax.experimental.pallas import tpu as pltpu
from jax.sharding import PartitionSpec as P

DS = 768
AXES = ("blk", "inner")
VMEM = 48 * 2**20
SHARE_SCALE = 8.0
EXTRA = 16


EPSILON = 1e-06


def coefficients(sq_student, sq_teacher, cross, total):
    norm_student = jnp.sqrt(sq_student + EPSILON)
    norm_teacher = jnp.sqrt(sq_teacher + EPSILON)
    factor = 2.0 * math.sqrt(total * DS) / total
    cubed = norm_student * norm_student * norm_student
    alpha = factor * (EPSILON / norm_student + cross / norm_teacher) / cubed
    beta = factor / (norm_student * norm_teacher)
    terms = (
        sq_student / (norm_student * norm_student)
        + sq_teacher / (norm_teacher * norm_teacher)
        - 2.0 * cross / (norm_student * norm_teacher)
    )
    return (alpha, beta, terms)


def span(masks):
    out = [0]
    for mask in masks:
        out += [mask ^ other for other in out]
    return out


def subgroups(blocks, inner):
    bits = [1 << b for b in range((inner - 1).bit_length())]
    bits += [inner << b for b in range(1, (blocks - 1).bit_length())]
    return (bits[0::2], bits[1::2] + [inner])


def send(value, mask, count):
    return lax.ppermute(value, AXES, [(i, i ^ mask) for i in range(count)])


def after(value, other):
    return lax.optimization_barrier((value, other))[0]


def join(*values):
    shape = (values[0].shape[0], sum(value.shape[1] for value in values))
    return call(join_kernel, values, jax.ShapeDtypeStruct(shape, values[0].dtype))


def gather(teacher, student, row_masks, col_masks, count):
    *plane_masks, core_mask = col_masks
    row_t, row_s, col_t, col_s = {}, {}, {}, {}
    sides = ((row_t, row_s, row_masks), (col_t, col_s, plane_masks))

    def whole(value):
        return (value, 0, value.shape[1])

    def forward(side, masks, keep):
        for level in range(2, len(masks) + 1):
            for place in range(1 << len(masks)):
                if place.bit_count() == level and keep(place):
                    top = place.bit_length() - 1
                    side[place] = whole(send(side[place ^ (1 << top)][0], masks[top], count))

    for side_t, _, masks in reversed(sides):
        side_t[1] = whole(send(teacher, masks[0], count))
    swapped = [send(value, core_mask, count) for value in (teacher, student)]
    own = join(teacher, student)
    late_t, late_s = after((teacher, student), swapped)
    for side_t, side_s, masks in reversed(sides):
        side_t[0] = (own, 0, teacher.shape[1])
        for b, mask in enumerate(masks):
            if b:
                side_s[1 << b] = whole(send(late_s, mask, count))
                if side_t is col_t:
                    side_t[1 << b] = whole(send(late_t, mask, count))

    def long_way(side_s, masks, gate):
        forward(side_s, masks, lambda place: not place & 1)
        half = range(0, 1 << len(masks), 2)
        parts = [own[:, teacher.shape[1] :]] + [side_s[p][0] for p in half if p]
        side_s[0] = (own, teacher.shape[1], own.shape[1])
        got = send(after(join(*parts), gate), masks[0], count)
        for k, p in enumerate(half):
            side_s[p | 1] = (got, k * student.shape[1], (k + 1) * student.shape[1])

    first = (row_t[1][0], col_t[1][0])
    long_way(col_s, plane_masks, row_s[2][0])
    long_way(row_s, row_masks, first)
    row_t[1], col_t[1] = map(whole, after(first, col_t[2][0]))
    forward(col_t, plane_masks, lambda place: True)
    for b, mask in enumerate(row_masks):
        if b:
            parts = [row_t[p] for p in range(1 << b)]
            got, start = send(join(*(array[:, i:j] for array, i, j in parts)), mask, count), 0
            for p, (_, i, j) in enumerate(parts):
                row_t[p | 1 << b] = (got, start, start + j - i)
                start += j - i

    core_t, core_s = {0: whole(swapped[0])}, {0: whole(swapped[1])}
    ones = [1 << b for b in range(len(plane_masks))]
    rest = [p for p in range(1 << len(plane_masks)) if p.bit_count() > 1]
    swaps = [
        [(col_t, core_t, p) for p in ones] + [(col_s, core_s, p) for p in col_s if p and not p & 1],
        [(col_t, core_t, p) for p in rest],
        [(col_s, core_s, p) for p in col_s if p & 1],
    ]
    for swap in swaps:
        arrays = list({id(side[p][0]): side[p][0] for side, _, p in swap}.values())
        got = send(join(*arrays) if len(arrays) > 1 else arrays[0], core_mask, count)
        starts = {id(array): sum(a.shape[1] for a in arrays[:k]) for k, array in enumerate(arrays)}
        for side, core, p in swap:
            array, start, stop = side[p]
            core[p] = (got, starts[id(array)] + start, starts[id(array)] + stop)
    places = sorted(col_t)
    return (
        [row_t[p] for p in sorted(row_t)],
        [row_s[p] for p in sorted(row_s)],
        [col_t[p] for p in places] + [core_t[p] for p in places],
        [col_s[p] for p in places] + [core_s[p] for p in places],
    )


def operands_of(*groups):
    arrays = []
    for array, _, _ in sum(groups, []):
        if not any(array is other for other in arrays):
            arrays.append(array)
    number = {id(array): k for k, array in enumerate(arrays)}
    return arrays, [[(number[id(array)], start, stop) for array, start, stop in group] for group in groups]


def load(refs, group):
    return jnp.concatenate([refs[k][:, start:stop] for k, start, stop in group])


def tree_sum(values):
    while len(values) > 1:
        values = [values[i] + values[i + 1] for i in range(0, len(values), 2)]
    return values[0]


def join_kernel(*refs):
    *parts, both = refs
    start = 0
    for part in parts:
        both[:, start : start + part.shape[1]] = part[...]
        start += part.shape[1]


def put_sums(parts, row_part, col_part):
    pad = jnp.zeros((parts[0].shape[0], 128 - len(parts)), jnp.float32)
    by_row = jnp.transpose(jnp.concatenate([jnp.sum(p, 1, keepdims=True) for p in parts] + [pad], 1))
    for k, part in enumerate(parts):
        by_col = jnp.sum(part, 0, keepdims=True)
        for source, sums in ((by_row[k : k + 1], row_part), (by_col, col_part)):
            rows = sums.shape[2]
            for p in range(sums.shape[1]):
                sums[k, p : p + 1, :] = source[:, p * rows : (p + 1) * rows]


def gram_kernel(groups, *refs):
    *arrays, gram_s, gram_t, row_part, col_part = refs
    row_t, row_s, col_t, col_s = [load(arrays, group) for group in groups]
    dims = (((1,), (1,)), ((), ()))
    student = lax.dot_general(row_s, col_s, dims, preferred_element_type=jnp.float32)
    teacher = lax.dot_general(row_t, col_t, dims, preferred_element_type=jnp.float32)
    gram_s[...], gram_t[...] = student, teacher
    put_sums([student * student, teacher * teacher, student * teacher], row_part, col_part)


def call(kernel, operands, outputs, flops=0, **options):
    size = sum(math.prod(a.shape) * a.dtype.itemsize for a in [*operands, *jax.tree.leaves(outputs)])
    return pl.pallas_call(
        kernel,
        out_shape=outputs,
        **options,
        compiler_params=pltpu.CompilerParams(vmem_limit_bytes=VMEM),
        cost_estimate=pl.CostEstimate(flops=flops, bytes_accessed=size, transcendentals=0),
    )(*operands)


def output_kernel(n_arrays, group, total, gram_s, gram_t, row_sum, col_sum, *refs):
    col_s = load(refs[:n_arrays], group)
    own, share, *pieces = refs[n_arrays:]
    row_alpha, row_beta, _ = coefficients(row_sum[0], row_sum[1], row_sum[2], total)
    col_alpha, col_beta, terms = coefficients(col_sum[0], col_sum[1], col_sum[2], total)
    row_ab = jnp.transpose(jnp.concatenate([row_alpha, row_beta] * 4))
    row_w = row_ab[:, 0:1] * gram_s[...] - row_ab[:, 1:2] * gram_t[...]
    col_w = col_alpha * gram_s[...] - col_beta * gram_t[...]
    out = jnp.dot(row_w.astype(jnp.bfloat16), col_s, preferred_element_type=jnp.float32)
    out += jnp.dot(col_w.astype(jnp.bfloat16), col_s, preferred_element_type=jnp.float32)

    rows, width = own.shape
    own[...] = out[:rows]
    term = jnp.sum(terms, axis=1, keepdims=True)
    share[...] = jnp.broadcast_to(term, share.shape)
    largest = jnp.max(jnp.max(jnp.abs(out), axis=0, keepdims=True), axis=1, keepdims=True)
    power = jnp.clip(jnp.floor(jnp.log2(jnp.maximum(largest, 1e-30))), -100.0, 100.0)
    term = term * SHARE_SCALE
    high = term.astype(jnp.bfloat16).astype(jnp.float32)
    middle = (term - high).astype(jnp.bfloat16).astype(jnp.float32)
    low = term - high - middle
    lane = lax.broadcasted_iota(jnp.int32, (EXTRA, 128), 1)
    extra = jnp.where(lane == 0, power, jnp.where(lane == 1, high, jnp.where(lane == 2, middle, low)))
    scaled = out * jnp.exp2(13.0 - power)
    for k, piece in enumerate(pieces):
        for c in range(width // 128):
            block = scaled[(k + 1) * rows : (k + 2) * rows, c * 128 : (c + 1) * 128]
            piece[c * rows : (c + 1) * rows, :] = block
        piece[width // 128 * rows :, :] = extra


def final_kernel(total, own, share, *refs):
    *pieces, grad, loss = refs
    width = own.shape[1]
    grads, terms = [own[...]], [share[0:1, 0:1]]
    rows = own.shape[0]
    for piece in pieces:
        extra = piece[width // 128 * rows :, :]
        blocks = [piece[c * rows : (c + 1) * rows, :] for c in range(width // 128)]
        grads.append(jnp.concatenate(blocks, 1) * jnp.exp2(extra[0:1, 0:1] - 13.0))
        terms.append((extra[0:1, 1:2] + extra[0:1, 2:3] + extra[0:1, 3:4]) * (1.0 / SHARE_SCALE))
    grad[...] = tree_sum(grads)
    loss[...] = tree_sum(terms) * (1.0 / total)


def exchange_sums(row_part, col_part, row_masks, col_masks, count):
    *plane_masks, core_mask = col_masks
    n_row, n_col, rows = row_part.shape[1], col_part.shape[1], row_part.shape[2]

    def other_core_first(cols):
        return jnp.roll(cols, n_col // 2, 1)

    got = send(jnp.concatenate([row_part, col_part], 1), core_mask, count)
    all_rows = jnp.concatenate([row_part, got[:, :n_row]], 1)
    all_cols = col_part + other_core_first(got[:, n_row:])
    all_cols = jnp.pad(all_cols, ((0, 0), (0, 2 * n_row - n_col), (0, 0)))
    first = (lax.axis_index("blk") & 1) == 0
    sums = jnp.where(first, all_rows, all_cols)
    for b in range(len(row_masks)):
        pairs = []
        for i in range(count):
            masks = plane_masks if i & core_mask else row_masks
            if b < len(masks):
                pairs.append((i, i ^ masks[b]))
        got = lax.ppermute(sums, AXES, pairs).reshape(3, -1, 2, 1 << b, rows)
        sums += jnp.flip(got, 2).reshape(sums.shape)
    got = send(sums, core_mask, count)
    return (
        jnp.where(first, sums[:, :n_row], got[:, n_row:]),
        jnp.where(first, other_core_first(got[:, :n_col]), sums[:, :n_col]),
    )


def per_device(teacher, student):
    rows = teacher.shape[0]
    blocks = lax.axis_size("blk")
    inner = lax.axis_size("inner")
    count = blocks * inner
    total = rows * count
    row_masks, col_masks = subgroups(blocks, inner)
    n_row, n_col = 1 << len(row_masks), 1 << len(col_masks)

    pieces = gather(teacher, student, row_masks, col_masks, count)
    shape, width = (n_row * rows, n_col * rows), student.shape[1]

    def f32(*dims):
        return jax.ShapeDtypeStruct(dims, jnp.float32)

    arrays, groups = operands_of(*pieces)
    gram_s, gram_t, row_part, col_part = call(
        functools.partial(gram_kernel, groups),
        arrays,
        [f32(*shape), f32(*shape), f32(3, n_row, rows), f32(3, n_col, rows)],
        2 * math.prod(shape) * (teacher.shape[1] + width),
    )
    row_part, col_part = exchange_sums(row_part, col_part, row_masks, col_masks, count)
    row_sum, col_sum = row_part.reshape(3, 1, -1), col_part.reshape(3, 1, -1)

    arrays, (group,) = operands_of(pieces[3])
    own, share, *pieces = call(
        functools.partial(output_kernel, len(arrays), group, total),
        [gram_s, gram_t, row_sum, col_sum, *arrays],
        [f32(rows, width), f32(8, 128)] + [f32(width // 128 * rows + EXTRA, 128)] * (n_row - 1),
        4 * math.prod(shape) * width,
    )
    got = [
        send(value.astype(jnp.float16), mask, count).astype(jnp.float32)
        for value, mask in zip(pieces, span(row_masks)[1:])
    ]
    grad, loss = call(
        functools.partial(final_kernel, total), [own, share, *got], [f32(rows, width), f32(1, 1)]
    )
    return (loss[0, 0], grad)


def solution(mesh):
    return jax.shard_map(
        per_device,
        mesh=mesh,
        in_specs=(P(AXES, None), P(AXES, None)),
        out_specs=(P(), P(AXES, None)),
        check_vma=False,
    )
```

```python
import functools
import math

import jax
import jax.numpy as jnp
from jax import lax
from jax.experimental import pallas as pl
from jax.experimental.pallas import tpu as pltpu
from jax.sharding import PartitionSpec as P

DS = 768
AXES = ("blk", "inner")
VMEM = 48 * 2**20
SHARE_SCALE = 8.0
EXTRA = 16


EPSILON = 1e-06


def coefficients(sq_student, sq_teacher, cross, total):
    norm_student = jnp.sqrt(sq_student + EPSILON)
    norm_teacher = jnp.sqrt(sq_teacher + EPSILON)
    factor = 2.0 * math.sqrt(total * DS) / total
    cubed = norm_student * norm_student * norm_student
    alpha = factor * (EPSILON / norm_student + cross / norm_teacher) / cubed
    beta = factor / (norm_student * norm_teacher)
    terms = (
        sq_student / (norm_student * norm_student)
        + sq_teacher / (norm_teacher * norm_teacher)
        - 2.0 * cross / (norm_student * norm_teacher)
    )
    return (alpha, beta, terms)


def span(masks):
    out = [0]
    for mask in masks:
        out += [mask ^ other for other in out]
    return out


def subgroups(blocks, inner):
    bits = [1 << b for b in range((inner - 1).bit_length())]
    bits += [inner << b for b in range(1, (blocks - 1).bit_length())]
    return (bits[0::2], bits[1::2] + [inner])


def send(value, mask, count):
    return lax.ppermute(value, AXES, [(i, i ^ mask) for i in range(count)])


def after(value, other):
    return lax.optimization_barrier((value, other))[0]


def join(*values):
    shape = (values[0].shape[0], sum(value.shape[1] for value in values))
    return call(join_kernel, values, jax.ShapeDtypeStruct(shape, values[0].dtype))


def gather(teacher, student, row_masks, col_masks, count):
    *plane_masks, core_mask = col_masks
    row_t, row_s, col_t, col_s = {}, {}, {}, {}
    sides = ((row_t, row_s, row_masks), (col_t, col_s, plane_masks))

    def whole(value):
        return (value, 0, value.shape[1])

    def forward(side, masks, keep):
        for level in range(2, len(masks) + 1):
            for place in range(1 << len(masks)):
                if place.bit_count() == level and keep(place):
                    top = place.bit_length() - 1
                    side[place] = whole(send(side[place ^ (1 << top)][0], masks[top], count))

    col_t[1] = whole(send(teacher, plane_masks[0], count))
    swapped = [send(value, core_mask, count) for value in (teacher, student)]
    own = join(teacher, student)
    late_t, late_s = after((teacher, student), swapped)
    row_t[1] = whole(send(after(teacher, swapped[1]), row_masks[0], count))
    for side_t, side_s, masks in reversed(sides):
        side_t[0] = (own, 0, teacher.shape[1])
        for b, mask in enumerate(masks):
            if b:
                side_s[1 << b] = whole(send(late_s, mask, count))
                if side_t is col_t:
                    side_t[1 << b] = whole(send(late_t, mask, count))

    def long_way(side_s, masks, gate):
        forward(side_s, masks, lambda place: not place & 1)
        half = range(0, 1 << len(masks), 2)
        parts = [own[:, teacher.shape[1] :]] + [side_s[p][0] for p in half if p]
        side_s[0] = (own, teacher.shape[1], own.shape[1])
        got = send(after(join(*parts), gate), masks[0], count)
        for k, p in enumerate(half):
            side_s[p | 1] = (got, k * student.shape[1], (k + 1) * student.shape[1])

    first = (row_t[1][0], col_t[1][0])
    long_way(col_s, plane_masks, row_s[2][0])
    long_way(row_s, row_masks, first)
    row_t[1], col_t[1] = map(whole, after(first, col_t[2][0]))
    forward(col_t, plane_masks, lambda place: True)
    for b, mask in enumerate(row_masks):
        if b:
            parts = [row_t[p] for p in range(1 << b)]
            got, start = send(join(*(array[:, i:j] for array, i, j in parts)), mask, count), 0
            for p, (_, i, j) in enumerate(parts):
                row_t[p | 1 << b] = (got, start, start + j - i)
                start += j - i

    core_t, core_s = {0: whole(swapped[0])}, {0: whole(swapped[1])}
    ones = [1 << b for b in range(len(plane_masks))]
    rest = [p for p in range(1 << len(plane_masks)) if p.bit_count() > 1]
    swaps = [
        [(col_t, core_t, p) for p in ones] + [(col_s, core_s, p) for p in col_s if p and not p & 1],
        [(col_t, core_t, p) for p in rest],
        [(col_s, core_s, p) for p in col_s if p & 1],
    ]
    for swap in swaps:
        arrays = list({id(side[p][0]): side[p][0] for side, _, p in swap}.values())
        got = send(join(*arrays) if len(arrays) > 1 else arrays[0], core_mask, count)
        starts = {id(array): sum(a.shape[1] for a in arrays[:k]) for k, array in enumerate(arrays)}
        for side, core, p in swap:
            array, start, stop = side[p]
            core[p] = (got, starts[id(array)] + start, starts[id(array)] + stop)
    places = sorted(col_t)
    return (
        [row_t[p] for p in sorted(row_t)],
        [row_s[p] for p in sorted(row_s)],
        [col_t[p] for p in places] + [core_t[p] for p in places],
        [col_s[p] for p in places] + [core_s[p] for p in places],
    )


def operands_of(*groups):
    arrays = []
    for array, _, _ in sum(groups, []):
        if not any(array is other for other in arrays):
            arrays.append(array)
    number = {id(array): k for k, array in enumerate(arrays)}
    return arrays, [[(number[id(array)], start, stop) for array, start, stop in group] for group in groups]


def load(refs, group):
    return jnp.concatenate([refs[k][:, start:stop] for k, start, stop in group])


def tree_sum(values):
    while len(values) > 1:
        values = [values[i] + values[i + 1] for i in range(0, len(values), 2)]
    return values[0]


def join_kernel(*refs):
    *parts, both = refs
    start = 0
    for part in parts:
        both[:, start : start + part.shape[1]] = part[...]
        start += part.shape[1]


def put_sums(parts, row_part, col_part):
    pad = jnp.zeros((parts[0].shape[0], 128 - len(parts)), jnp.float32)
    by_row = jnp.transpose(jnp.concatenate([jnp.sum(p, 1, keepdims=True) for p in parts] + [pad], 1))
    for k, part in enumerate(parts):
        by_col = jnp.sum(part, 0, keepdims=True)
        for source, sums in ((by_row[k : k + 1], row_part), (by_col, col_part)):
            rows = sums.shape[2]
            for p in range(sums.shape[1]):
                sums[k, p : p + 1, :] = source[:, p * rows : (p + 1) * rows]


def gram_kernel(groups, *refs):
    *arrays, gram_s, gram_t, row_part, col_part = refs
    row_t, row_s, col_t, col_s = [load(arrays, group) for group in groups]
    dims = (((1,), (1,)), ((), ()))
    student = lax.dot_general(row_s, col_s, dims, preferred_element_type=jnp.float32)
    teacher = lax.dot_general(row_t, col_t, dims, preferred_element_type=jnp.float32)
    gram_s[...], gram_t[...] = student, teacher
    put_sums([student * student, teacher * teacher, student * teacher], row_part, col_part)


def call(kernel, operands, outputs, flops=0, **options):
    size = sum(math.prod(a.shape) * a.dtype.itemsize for a in [*operands, *jax.tree.leaves(outputs)])
    return pl.pallas_call(
        kernel,
        out_shape=outputs,
        **options,
        compiler_params=pltpu.CompilerParams(vmem_limit_bytes=VMEM),
        cost_estimate=pl.CostEstimate(flops=flops, bytes_accessed=size, transcendentals=0),
    )(*operands)


def output_kernel(n_arrays, group, total, gram_s, gram_t, row_sum, col_sum, *refs):
    col_s = load(refs[:n_arrays], group)
    own, share, *pieces = refs[n_arrays:]
    row_alpha, row_beta, _ = coefficients(row_sum[0], row_sum[1], row_sum[2], total)
    col_alpha, col_beta, terms = coefficients(col_sum[0], col_sum[1], col_sum[2], total)
    row_ab = jnp.transpose(jnp.concatenate([row_alpha, row_beta] * 4))
    row_w = row_ab[:, 0:1] * gram_s[...] - row_ab[:, 1:2] * gram_t[...]
    col_w = col_alpha * gram_s[...] - col_beta * gram_t[...]
    out = jnp.dot(row_w.astype(jnp.bfloat16), col_s, preferred_element_type=jnp.float32)
    out += jnp.dot(col_w.astype(jnp.bfloat16), col_s, preferred_element_type=jnp.float32)

    rows, width = own.shape
    own[...] = out[:rows]
    term = jnp.sum(terms, axis=1, keepdims=True)
    share[...] = jnp.broadcast_to(term, share.shape)
    largest = jnp.max(jnp.max(jnp.abs(out), axis=0, keepdims=True), axis=1, keepdims=True)
    power = jnp.clip(jnp.floor(jnp.log2(jnp.maximum(largest, 1e-30))), -100.0, 100.0)
    term = term * SHARE_SCALE
    high = term.astype(jnp.bfloat16).astype(jnp.float32)
    middle = (term - high).astype(jnp.bfloat16).astype(jnp.float32)
    low = term - high - middle
    lane = lax.broadcasted_iota(jnp.int32, (EXTRA, 128), 1)
    extra = jnp.where(lane == 0, power, jnp.where(lane == 1, high, jnp.where(lane == 2, middle, low)))
    scaled = out * jnp.exp2(13.0 - power)
    for k, piece in enumerate(pieces):
        for c in range(width // 128):
            block = scaled[(k + 1) * rows : (k + 2) * rows, c * 128 : (c + 1) * 128]
            piece[c * rows : (c + 1) * rows, :] = block
        piece[width // 128 * rows :, :] = extra


def final_kernel(total, own, share, *refs):
    *pieces, grad, loss = refs
    width = own.shape[1]
    grads, terms = [own[...]], [share[0:1, 0:1]]
    rows = own.shape[0]
    for piece in pieces:
        extra = piece[width // 128 * rows :, :]
        blocks = [piece[c * rows : (c + 1) * rows, :] for c in range(width // 128)]
        grads.append(jnp.concatenate(blocks, 1) * jnp.exp2(extra[0:1, 0:1] - 13.0))
        terms.append((extra[0:1, 1:2] + extra[0:1, 2:3] + extra[0:1, 3:4]) * (1.0 / SHARE_SCALE))
    grad[...] = tree_sum(grads)
    loss[...] = tree_sum(terms) * (1.0 / total)


def exchange_sums(row_part, col_part, row_masks, col_masks, count):
    *plane_masks, core_mask = col_masks
    n_row, n_col, rows = row_part.shape[1], col_part.shape[1], row_part.shape[2]

    def other_core_first(cols):
        return jnp.roll(cols, n_col // 2, 1)

    got = send(jnp.concatenate([row_part, col_part], 1), core_mask, count)
    all_rows = jnp.concatenate([row_part, got[:, :n_row]], 1)
    all_cols = col_part + other_core_first(got[:, n_row:])
    all_cols = jnp.pad(all_cols, ((0, 0), (0, 2 * n_row - n_col), (0, 0)))
    first = (lax.axis_index("blk") & 1) == 0
    sums = jnp.where(first, all_rows, all_cols)
    for b in range(len(row_masks)):
        pairs = []
        for i in range(count):
            masks = plane_masks if i & core_mask else row_masks
            if b < len(masks):
                pairs.append((i, i ^ masks[b]))
        got = lax.ppermute(sums, AXES, pairs).reshape(3, -1, 2, 1 << b, rows)
        sums += jnp.flip(got, 2).reshape(sums.shape)
    got = send(sums, core_mask, count)
    return (
        jnp.where(first, sums[:, :n_row], got[:, n_row:]),
        jnp.where(first, other_core_first(got[:, :n_col]), sums[:, :n_col]),
    )


def per_device(teacher, student):
    rows = teacher.shape[0]
    blocks = lax.axis_size("blk")
    inner = lax.axis_size("inner")
    count = blocks * inner
    total = rows * count
    row_masks, col_masks = subgroups(blocks, inner)
    n_row, n_col = 1 << len(row_masks), 1 << len(col_masks)

    pieces = gather(teacher, student, row_masks, col_masks, count)
    shape, width = (n_row * rows, n_col * rows), student.shape[1]

    def f32(*dims):
        return jax.ShapeDtypeStruct(dims, jnp.float32)

    arrays, groups = operands_of(*pieces)
    gram_s, gram_t, row_part, col_part = call(
        functools.partial(gram_kernel, groups),
        arrays,
        [f32(*shape), f32(*shape), f32(3, n_row, rows), f32(3, n_col, rows)],
        2 * math.prod(shape) * (teacher.shape[1] + width),
    )
    row_part, col_part = exchange_sums(row_part, col_part, row_masks, col_masks, count)
    row_sum, col_sum = row_part.reshape(3, 1, -1), col_part.reshape(3, 1, -1)

    arrays, (group,) = operands_of(pieces[3])
    own, share, *pieces = call(
        functools.partial(output_kernel, len(arrays), group, total),
        [gram_s, gram_t, row_sum, col_sum, *arrays],
        [f32(rows, width), f32(8, 128)] + [f32(width // 128 * rows + EXTRA, 128)] * (n_row - 1),
        4 * math.prod(shape) * width,
    )
    got = [
        send(value.astype(jnp.float16), mask, count).astype(jnp.float32)
        for value, mask in zip(pieces, span(row_masks)[1:])
    ]
    grad, loss = call(
        functools.partial(final_kernel, total), [own, share, *got], [f32(rows, width), f32(1, 1)]
    )
    return (loss[0, 0], grad)


def solution(mesh):
    return jax.shard_map(
        per_device,
        mesh=mesh,
        in_specs=(P(AXES, None), P(AXES, None)),
        out_specs=(P(), P(AXES, None)),
        check_vma=False,
    )
```

```python
import functools
import math

import jax
import jax.numpy as jnp
from jax import lax
from jax.experimental import pallas as pl
from jax.experimental.pallas import tpu as pltpu
from jax.sharding import PartitionSpec as P

DS = 768
AXES = ("blk", "inner")
VMEM = 48 * 2**20
SHARE_SCALE = 8.0
EXTRA = 16


EPSILON = 1e-06


def coefficients(sq_student, sq_teacher, cross, total):
    norm_student = jnp.sqrt(sq_student + EPSILON)
    norm_teacher = jnp.sqrt(sq_teacher + EPSILON)
    factor = 2.0 * math.sqrt(total * DS) / total
    cubed = norm_student * norm_student * norm_student
    alpha = factor * (EPSILON / norm_student + cross / norm_teacher) / cubed
    beta = factor / (norm_student * norm_teacher)
    terms = (
        sq_student / (norm_student * norm_student)
        + sq_teacher / (norm_teacher * norm_teacher)
        - 2.0 * cross / (norm_student * norm_teacher)
    )
    return (alpha, beta, terms)


def span(masks):
    out = [0]
    for mask in masks:
        out += [mask ^ other for other in out]
    return out


def subgroups(blocks, inner):
    bits = [1 << b for b in range((inner - 1).bit_length())]
    bits += [inner << b for b in range(1, (blocks - 1).bit_length())]
    return (bits[0::2], bits[1::2] + [inner])


def send(value, mask, count):
    return lax.ppermute(value, AXES, [(i, i ^ mask) for i in range(count)])


def after(value, other):
    return lax.optimization_barrier((value, other))[0]


def join(*values):
    shape = (values[0].shape[0], sum(value.shape[1] for value in values))
    return call(join_kernel, values, jax.ShapeDtypeStruct(shape, values[0].dtype))


def gather(teacher, student, row_masks, col_masks, count):
    *plane_masks, core_mask = col_masks
    row_t, row_s, col_t, col_s = {}, {}, {}, {}
    sides = ((row_t, row_s, row_masks), (col_t, col_s, plane_masks))

    def whole(value):
        return (value, 0, value.shape[1])

    def forward(side, masks, keep):
        for level in range(2, len(masks) + 1):
            for place in range(1 << len(masks)):
                if place.bit_count() == level and keep(place):
                    top = place.bit_length() - 1
                    side[place] = whole(send(side[place ^ (1 << top)][0], masks[top], count))

    for side_t, _, masks in reversed(sides):
        side_t[1] = whole(send(teacher, masks[0], count))
    swapped = [send(value, core_mask, count) for value in (teacher, student)]
    own = join(teacher, student)
    late_t, late_s = after((teacher, student), swapped)
    for side_t, side_s, masks in reversed(sides):
        side_t[0] = (own, 0, teacher.shape[1])
        for b, mask in enumerate(masks):
            if b:
                side_s[1 << b] = whole(send(late_s, mask, count))
                if side_t is col_t:
                    side_t[1 << b] = whole(send(late_t, mask, count))

    def long_way(side_s, masks, gate):
        forward(side_s, masks, lambda place: not place & 1)
        half = range(0, 1 << len(masks), 2)
        parts = [own[:, teacher.shape[1] :]] + [side_s[p][0] for p in half if p]
        side_s[0] = (own, teacher.shape[1], own.shape[1])
        got = send(after(join(*parts), gate), masks[0], count)
        for k, p in enumerate(half):
            side_s[p | 1] = (got, k * student.shape[1], (k + 1) * student.shape[1])

    first = (row_t[1][0], col_t[1][0])
    long_way(col_s, plane_masks, row_s[2][0])
    long_way(row_s, row_masks, first)
    row_t[1], col_t[1] = map(whole, after(first, col_t[2][0]))
    forward(col_t, plane_masks, lambda place: True)
    for b, mask in enumerate(row_masks):
        if b:
            parts = [row_t[p] for p in range(1 << b)]
            got, start = send(join(*(array[:, i:j] for array, i, j in parts)), mask, count), 0
            for p, (_, i, j) in enumerate(parts):
                row_t[p | 1 << b] = (got, start, start + j - i)
                start += j - i

    core_t, core_s = {0: whole(swapped[0])}, {0: whole(swapped[1])}
    ones = [1 << b for b in range(len(plane_masks))]
    rest = [p for p in range(1 << len(plane_masks)) if p.bit_count() > 1]
    swaps = [
        [(col_t, core_t, p) for p in ones] + [(col_s, core_s, p) for p in col_s if p and not p & 1],
        [(col_t, core_t, p) for p in rest],
        [(col_s, core_s, p) for p in col_s if p & 1],
    ]
    for swap in swaps:
        arrays = list({id(side[p][0]): side[p][0] for side, _, p in swap}.values())
        got = send(join(*arrays) if len(arrays) > 1 else arrays[0], core_mask, count)
        starts = {id(array): sum(a.shape[1] for a in arrays[:k]) for k, array in enumerate(arrays)}
        for side, core, p in swap:
            array, start, stop = side[p]
            core[p] = (got, starts[id(array)] + start, starts[id(array)] + stop)
    places = sorted(col_t)
    return (
        [row_t[p] for p in sorted(row_t)],
        [row_s[p] for p in sorted(row_s)],
        [col_t[p] for p in places] + [core_t[p] for p in places],
        [col_s[p] for p in places] + [core_s[p] for p in places],
    )


def operands_of(*groups):
    arrays = []
    for array, _, _ in sum(groups, []):
        if not any(array is other for other in arrays):
            arrays.append(array)
    number = {id(array): k for k, array in enumerate(arrays)}
    return arrays, [[(number[id(array)], start, stop) for array, start, stop in group] for group in groups]


def load(refs, group):
    return jnp.concatenate([refs[k][:, start:stop] for k, start, stop in group])


def tree_sum(values):
    while len(values) > 1:
        values = [values[i] + values[i + 1] for i in range(0, len(values), 2)]
    return values[0]


def join_kernel(*refs):
    *parts, both = refs
    start = 0
    for part in parts:
        both[:, start : start + part.shape[1]] = part[...]
        start += part.shape[1]


def put_sums(parts, row_part, col_part):
    pad = jnp.zeros((parts[0].shape[0], 128 - len(parts)), jnp.float32)
    by_row = jnp.transpose(jnp.concatenate([jnp.sum(p, 1, keepdims=True) for p in parts] + [pad], 1))
    for k, part in enumerate(parts):
        by_col = jnp.sum(part, 0, keepdims=True)
        for source, sums in ((by_row[k : k + 1], row_part), (by_col, col_part)):
            rows = sums.shape[2]
            for p in range(sums.shape[1]):
                sums[k, p : p + 1, :] = source[:, p * rows : (p + 1) * rows]


def gram_kernel(groups, *refs):
    *arrays, gram_s, gram_t, row_part, col_part = refs
    row_t, row_s, col_t, col_s = [load(arrays, group) for group in groups]
    dims = (((1,), (1,)), ((), ()))
    student = lax.dot_general(row_s, col_s, dims, preferred_element_type=jnp.float32)
    teacher = lax.dot_general(row_t, col_t, dims, preferred_element_type=jnp.float32)
    gram_s[...], gram_t[...] = student, teacher
    put_sums([student * student, teacher * teacher, student * teacher], row_part, col_part)


def call(kernel, operands, outputs, flops=0, **options):
    size = sum(math.prod(a.shape) * a.dtype.itemsize for a in [*operands, *jax.tree.leaves(outputs)])
    return pl.pallas_call(
        kernel,
        out_shape=outputs,
        **options,
        compiler_params=pltpu.CompilerParams(vmem_limit_bytes=VMEM),
        cost_estimate=pl.CostEstimate(flops=flops, bytes_accessed=size, transcendentals=0),
    )(*operands)


def output_kernel(n_arrays, group, total, gram_s, gram_t, row_sum, col_sum, *refs):
    col_s = load(refs[:n_arrays], group)
    own, share, *pieces = refs[n_arrays:]
    row_alpha, row_beta, _ = coefficients(row_sum[0], row_sum[1], row_sum[2], total)
    col_alpha, col_beta, terms = coefficients(col_sum[0], col_sum[1], col_sum[2], total)
    row_ab = jnp.transpose(jnp.concatenate([row_alpha, row_beta] * 4))
    row_w = row_ab[:, 0:1] * gram_s[...] - row_ab[:, 1:2] * gram_t[...]
    col_w = col_alpha * gram_s[...] - col_beta * gram_t[...]
    out = jnp.dot(row_w.astype(jnp.bfloat16), col_s, preferred_element_type=jnp.float32)
    out += jnp.dot(col_w.astype(jnp.bfloat16), col_s, preferred_element_type=jnp.float32)

    rows, width = own.shape
    own[...] = out[:rows]
    term = jnp.sum(terms, axis=1, keepdims=True)
    share[...] = jnp.broadcast_to(term, share.shape)
    largest = jnp.max(jnp.max(jnp.abs(out), axis=0, keepdims=True), axis=1, keepdims=True)
    power = jnp.clip(jnp.floor(jnp.log2(jnp.maximum(largest, 1e-30))), -100.0, 100.0)
    term = term * SHARE_SCALE
    high = term.astype(jnp.bfloat16).astype(jnp.float32)
    middle = (term - high).astype(jnp.bfloat16).astype(jnp.float32)
    low = term - high - middle
    lane = lax.broadcasted_iota(jnp.int32, (EXTRA, 128), 1)
    extra = jnp.where(lane == 0, power, jnp.where(lane == 1, high, jnp.where(lane == 2, middle, low)))
    scaled = out * jnp.exp2(13.0 - power)
    for k, piece in enumerate(pieces):
        for c in range(width // 128):
            block = scaled[(k + 1) * rows : (k + 2) * rows, c * 128 : (c + 1) * 128]
            piece[c * rows : (c + 1) * rows, :] = block
        piece[width // 128 * rows :, :] = extra


def final_kernel(order, total, own, share, *refs):
    *pieces, grad, loss = refs
    width = own.shape[1]
    grads, terms = [own[...]], [share[0:1, 0:1]]
    rows = own.shape[0]
    for piece in [pieces[order.index(k)] for k in range(len(pieces))]:
        extra = piece[width // 128 * rows :, :]
        blocks = [piece[c * rows : (c + 1) * rows, :] for c in range(width // 128)]
        grads.append(jnp.concatenate(blocks, 1) * jnp.exp2(extra[0:1, 0:1] - 13.0))
        terms.append((extra[0:1, 1:2] + extra[0:1, 2:3] + extra[0:1, 3:4]) * (1.0 / SHARE_SCALE))
    grad[...] = tree_sum(grads)
    loss[...] = tree_sum(terms) * (1.0 / total)


def exchange_sums(row_part, col_part, row_masks, col_masks, count):
    *plane_masks, core_mask = col_masks
    n_row, n_col, rows = row_part.shape[1], col_part.shape[1], row_part.shape[2]

    def other_core_first(cols):
        return jnp.roll(cols, n_col // 2, 1)

    got = send(jnp.concatenate([row_part, col_part], 1), core_mask, count)
    all_rows = jnp.concatenate([row_part, got[:, :n_row]], 1)
    all_cols = col_part + other_core_first(got[:, n_row:])
    all_cols = jnp.pad(all_cols, ((0, 0), (0, 2 * n_row - n_col), (0, 0)))
    first = (lax.axis_index("blk") & 1) == 0
    sums = jnp.where(first, all_rows, all_cols)
    for b in range(len(row_masks)):
        pairs = []
        for i in range(count):
            masks = plane_masks if i & core_mask else row_masks
            if b < len(masks):
                pairs.append((i, i ^ masks[b]))
        got = lax.ppermute(sums, AXES, pairs).reshape(3, -1, 2, 1 << b, rows)
        sums += jnp.flip(got, 2).reshape(sums.shape)
    got = send(sums, core_mask, count)
    return (
        jnp.where(first, sums[:, :n_row], got[:, n_row:]),
        jnp.where(first, other_core_first(got[:, :n_col]), sums[:, :n_col]),
    )


def per_device(teacher, student):
    rows = teacher.shape[0]
    blocks = lax.axis_size("blk")
    inner = lax.axis_size("inner")
    count = blocks * inner
    total = rows * count
    row_masks, col_masks = subgroups(blocks, inner)
    n_row, n_col = 1 << len(row_masks), 1 << len(col_masks)

    pieces = gather(teacher, student, row_masks, col_masks, count)
    shape, width = (n_row * rows, n_col * rows), student.shape[1]

    def f32(*dims):
        return jax.ShapeDtypeStruct(dims, jnp.float32)

    arrays, groups = operands_of(*pieces)
    gram_s, gram_t, row_part, col_part = call(
        functools.partial(gram_kernel, groups),
        arrays,
        [f32(*shape), f32(*shape), f32(3, n_row, rows), f32(3, n_col, rows)],
        2 * math.prod(shape) * (teacher.shape[1] + width),
    )
    row_part, col_part = exchange_sums(row_part, col_part, row_masks, col_masks, count)
    row_sum, col_sum = row_part.reshape(3, 1, -1), col_part.reshape(3, 1, -1)

    arrays, (group,) = operands_of(pieces[3])
    own, share, *pieces = call(
        functools.partial(output_kernel, len(arrays), group, total),
        [gram_s, gram_t, row_sum, col_sum, *arrays],
        [f32(rows, width), f32(8, 128)] + [f32(width // 128 * rows + EXTRA, 128)] * (n_row - 1),
        4 * math.prod(shape) * width,
    )
    order = sorted(range(n_row - 1), key=lambda k: ((k + 1).bit_count(), -k))
    masks = span(row_masks)[1:]
    got = [send(pieces[k].astype(jnp.float16), masks[k], count).astype(jnp.float32) for k in order]
    grad, loss = call(
        functools.partial(final_kernel, order, total), [own, share, *got], [f32(rows, width), f32(1, 1)]
    )
    return (loss[0, 0], grad)


def solution(mesh):
    return jax.shard_map(
        per_device,
        mesh=mesh,
        in_specs=(P(AXES, None), P(AXES, None)),
        out_specs=(P(), P(AXES, None)),
        check_vma=False,
    )
```

```python
import functools
import math

import jax
import jax.numpy as jnp
from jax import lax
from jax.experimental import pallas as pl
from jax.experimental.pallas import tpu as pltpu
from jax.sharding import PartitionSpec as P

DS = 768
AXES = ("blk", "inner")
VMEM = 48 * 2**20
SHARE_SCALE = 8.0
EXTRA = 16


EPSILON = 1e-06


def coefficients(sq_student, sq_teacher, cross, total):
    norm_student = jnp.sqrt(sq_student + EPSILON)
    norm_teacher = jnp.sqrt(sq_teacher + EPSILON)
    factor = 2.0 * math.sqrt(total * DS) / total
    cubed = norm_student * norm_student * norm_student
    alpha = factor * (EPSILON / norm_student + cross / norm_teacher) / cubed
    beta = factor / (norm_student * norm_teacher)
    terms = (
        sq_student / (norm_student * norm_student)
        + sq_teacher / (norm_teacher * norm_teacher)
        - 2.0 * cross / (norm_student * norm_teacher)
    )
    return (alpha, beta, terms)


def span(masks):
    out = [0]
    for mask in masks:
        out += [mask ^ other for other in out]
    return out


def subgroups(blocks, inner):
    bits = [1 << b for b in range((inner - 1).bit_length())]
    bits += [inner << b for b in range(1, (blocks - 1).bit_length())]
    return (bits[0::2], bits[1::2] + [inner])


def send(value, mask, count):
    return lax.ppermute(value, AXES, [(i, i ^ mask) for i in range(count)])


def after(value, other):
    return lax.optimization_barrier((value, other))[0]


def join(*values):
    shape = (values[0].shape[0], sum(value.shape[1] for value in values))
    return call(join_kernel, values, jax.ShapeDtypeStruct(shape, values[0].dtype))


def gather(teacher, student, row_masks, col_masks, count):
    *plane_masks, core_mask = col_masks
    row_t, row_s, col_t, col_s = {}, {}, {}, {}
    sides = ((row_t, row_s, row_masks), (col_t, col_s, plane_masks))

    def whole(value):
        return (value, 0, value.shape[1])

    def forward(side, masks, keep):
        for level in range(2, len(masks) + 1):
            for place in range(1 << len(masks)):
                if place.bit_count() == level and keep(place):
                    top = place.bit_length() - 1
                    side[place] = whole(send(side[place ^ (1 << top)][0], masks[top], count))

    for side_t, _, masks in reversed(sides):
        side_t[1] = whole(send(teacher, masks[0], count))
    swapped = [send(value, core_mask, count) for value in (teacher, student)]
    own = join(teacher, student)
    late_t, late_s = after((teacher, student), swapped)
    for side_t, side_s, masks in reversed(sides):
        side_t[0] = (own, 0, teacher.shape[1])
        for b, mask in enumerate(masks):
            if b:
                side_s[1 << b] = whole(send(late_s, mask, count))
                if side_t is col_t:
                    side_t[1 << b] = whole(send(late_t, mask, count))

    def long_way(side_s, masks, gate):
        forward(side_s, masks, lambda place: not place & 1)
        half = range(0, 1 << len(masks), 2)
        parts = [own[:, teacher.shape[1] :]] + [side_s[p][0] for p in half if p]
        side_s[0] = (own, teacher.shape[1], own.shape[1])
        got = send(after(join(*parts), gate), masks[0], count)
        for k, p in enumerate(half):
            side_s[p | 1] = (got, k * student.shape[1], (k + 1) * student.shape[1])

    first = (row_t[1][0], col_t[1][0])
    long_way(col_s, plane_masks, row_s[2][0])
    long_way(row_s, row_masks, first)
    row_t[1], col_t[1] = map(whole, after(first, col_t[2][0]))
    forward(col_t, plane_masks, lambda place: True)
    for b, mask in enumerate(row_masks):
        if b:
            parts = [row_t[p] for p in range(1 << b)]
            got, start = send(join(*(array[:, i:j] for array, i, j in parts)), mask, count), 0
            for p, (_, i, j) in enumerate(parts):
                row_t[p | 1 << b] = (got, start, start + j - i)
                start += j - i

    core_t, core_s = {0: whole(swapped[0])}, {0: whole(swapped[1])}
    ones = [1 << b for b in range(len(plane_masks))]
    rest = [p for p in range(1 << len(plane_masks)) if p.bit_count() > 1]
    swaps = [
        [(col_t, core_t, p) for p in ones] + [(col_s, core_s, p) for p in col_s if p and not p & 1],
        [(col_t, core_t, p) for p in rest],
        [(col_s, core_s, p) for p in col_s if p & 1],
    ]
    for swap in swaps:
        arrays = list({id(side[p][0]): side[p][0] for side, _, p in swap}.values())
        got = send(join(*arrays) if len(arrays) > 1 else arrays[0], core_mask, count)
        starts = {id(array): sum(a.shape[1] for a in arrays[:k]) for k, array in enumerate(arrays)}
        for side, core, p in swap:
            array, start, stop = side[p]
            core[p] = (got, starts[id(array)] + start, starts[id(array)] + stop)
    places = sorted(col_t)
    return (
        [row_t[p] for p in sorted(row_t)],
        [row_s[p] for p in sorted(row_s)],
        [col_t[p] for p in places] + [core_t[p] for p in places],
        [col_s[p] for p in places] + [core_s[p] for p in places],
    )


def operands_of(*groups):
    arrays = []
    for array, _, _ in sum(groups, []):
        if not any(array is other for other in arrays):
            arrays.append(array)
    number = {id(array): k for k, array in enumerate(arrays)}
    return arrays, [[(number[id(array)], start, stop) for array, start, stop in group] for group in groups]


def load(refs, group):
    return jnp.concatenate([refs[k][:, start:stop] for k, start, stop in group])


def tree_sum(values):
    while len(values) > 1:
        values = [values[i] + values[i + 1] for i in range(0, len(values), 2)]
    return values[0]


def join_kernel(*refs):
    *parts, both = refs
    start = 0
    for part in parts:
        both[:, start : start + part.shape[1]] = part[...]
        start += part.shape[1]


def put_sums(parts, row_part, col_part):
    pad = jnp.zeros((parts[0].shape[0], 128 - len(parts)), jnp.float32)
    by_row = jnp.transpose(jnp.concatenate([jnp.sum(p, 1, keepdims=True) for p in parts] + [pad], 1))
    for k, part in enumerate(parts):
        by_col = jnp.sum(part, 0, keepdims=True)
        for source, sums in ((by_row[k : k + 1], row_part), (by_col, col_part)):
            rows = sums.shape[2]
            for p in range(sums.shape[1]):
                sums[k, p : p + 1, :] = source[:, p * rows : (p + 1) * rows]


def gram_kernel(groups, *refs):
    *arrays, gram_s, gram_t, row_part, col_part = refs
    row_t, row_s, col_t, col_s = [load(arrays, group) for group in groups]
    dims = (((1,), (1,)), ((), ()))
    student = lax.dot_general(row_s, col_s, dims, preferred_element_type=jnp.float32)
    teacher = lax.dot_general(row_t, col_t, dims, preferred_element_type=jnp.float32)
    gram_s[...], gram_t[...] = student, teacher
    put_sums([student * student, teacher * teacher, student * teacher], row_part, col_part)


def call(kernel, operands, outputs, flops=0, **options):
    size = sum(math.prod(a.shape) * a.dtype.itemsize for a in [*operands, *jax.tree.leaves(outputs)])
    return pl.pallas_call(
        kernel,
        out_shape=outputs,
        **options,
        compiler_params=pltpu.CompilerParams(vmem_limit_bytes=VMEM),
        cost_estimate=pl.CostEstimate(flops=flops, bytes_accessed=size, transcendentals=0),
    )(*operands)


def output_kernel(n_arrays, group, total, gram_s, gram_t, row_sum, col_sum, *refs):
    col_s = load(refs[:n_arrays], group)
    own, share, *pieces = refs[n_arrays:]
    row_alpha, row_beta, _ = coefficients(row_sum[0], row_sum[1], row_sum[2], total)
    col_alpha, col_beta, terms = coefficients(col_sum[0], col_sum[1], col_sum[2], total)
    row_ab = jnp.transpose(jnp.concatenate([row_alpha, row_beta] * 4))
    row_w = row_ab[:, 0:1] * gram_s[...] - row_ab[:, 1:2] * gram_t[...]
    col_w = col_alpha * gram_s[...] - col_beta * gram_t[...]
    out = jnp.dot(row_w.astype(jnp.bfloat16), col_s, preferred_element_type=jnp.float32)
    out += jnp.dot(col_w.astype(jnp.bfloat16), col_s, preferred_element_type=jnp.float32)

    rows, width = own.shape
    own[...] = out[:rows]
    term = jnp.sum(terms, axis=1, keepdims=True)
    share[...] = jnp.broadcast_to(term, share.shape)
    largest = jnp.max(jnp.max(jnp.abs(out), axis=0, keepdims=True), axis=1, keepdims=True)
    power = jnp.clip(jnp.floor(jnp.log2(jnp.maximum(largest, 1e-30))), -100.0, 100.0)
    term = term * SHARE_SCALE
    high = term.astype(jnp.bfloat16).astype(jnp.float32)
    middle = (term - high).astype(jnp.bfloat16).astype(jnp.float32)
    low = term - high - middle
    lane = lax.broadcasted_iota(jnp.int32, (EXTRA, 128), 1)
    extra = jnp.where(lane == 0, power, jnp.where(lane == 1, high, jnp.where(lane == 2, middle, low)))
    scaled = out * jnp.exp2(13.0 - power)
    for k, piece in enumerate(pieces):
        for c in range(width // 128):
            block = scaled[(k + 1) * rows : (k + 2) * rows, c * 128 : (c + 1) * 128]
            piece[c * rows : (c + 1) * rows, :] = block
        piece[width // 128 * rows :, :] = extra


def final_kernel(order, total, own, share, *refs):
    *pieces, grad, loss = refs
    width = own.shape[1]
    grads, terms = [own[...]], [share[0:1, 0:1]]
    rows = own.shape[0]
    for piece in [pieces[order.index(k)] for k in range(len(pieces))]:
        extra = piece[width // 128 * rows :, :]
        blocks = [piece[c * rows : (c + 1) * rows, :] for c in range(width // 128)]
        grads.append(jnp.concatenate(blocks, 1) * jnp.exp2(extra[0:1, 0:1] - 13.0))
        terms.append((extra[0:1, 1:2] + extra[0:1, 2:3] + extra[0:1, 3:4]) * (1.0 / SHARE_SCALE))
    grad[...] = tree_sum(grads)
    loss[...] = tree_sum(terms) * (1.0 / total)


def exchange_sums(row_part, col_part, row_masks, col_masks, count):
    *plane_masks, core_mask = col_masks
    n_row, n_col, rows = row_part.shape[1], col_part.shape[1], row_part.shape[2]

    def other_core_first(cols):
        return jnp.roll(cols, n_col // 2, 1)

    got = send(jnp.concatenate([row_part, col_part], 1), core_mask, count)
    all_rows = jnp.concatenate([row_part, got[:, :n_row]], 1)
    all_cols = col_part + other_core_first(got[:, n_row:])
    all_cols = jnp.pad(all_cols, ((0, 0), (0, 2 * n_row - n_col), (0, 0)))
    first = (lax.axis_index("blk") & 1) == 0
    sums = jnp.where(first, all_rows, all_cols)
    for b in range(len(row_masks)):
        pairs = []
        for i in range(count):
            masks = plane_masks if i & core_mask else row_masks
            if b < len(masks):
                pairs.append((i, i ^ masks[b]))
        got = lax.ppermute(sums, AXES, pairs).reshape(3, -1, 2, 1 << b, rows)
        sums += jnp.flip(got, 2).reshape(sums.shape)
    got = send(sums, core_mask, count)
    return (
        jnp.where(first, sums[:, :n_row], got[:, n_row:]),
        jnp.where(first, other_core_first(got[:, :n_col]), sums[:, :n_col]),
    )


def per_device(teacher, student):
    rows = teacher.shape[0]
    blocks = lax.axis_size("blk")
    inner = lax.axis_size("inner")
    count = blocks * inner
    total = rows * count
    row_masks, col_masks = subgroups(blocks, inner)
    n_row, n_col = 1 << len(row_masks), 1 << len(col_masks)

    pieces = gather(teacher, student, row_masks, col_masks, count)
    shape, width = (n_row * rows, n_col * rows), student.shape[1]

    def f32(*dims):
        return jax.ShapeDtypeStruct(dims, jnp.float32)

    arrays, groups = operands_of(*pieces)
    gram_s, gram_t, row_part, col_part = call(
        functools.partial(gram_kernel, groups),
        arrays,
        [f32(*shape), f32(*shape), f32(3, n_row, rows), f32(3, n_col, rows)],
        2 * math.prod(shape) * (teacher.shape[1] + width),
    )
    row_part, col_part = exchange_sums(row_part, col_part, row_masks, col_masks, count)
    row_sum, col_sum = row_part.reshape(3, 1, -1), col_part.reshape(3, 1, -1)

    arrays, (group,) = operands_of(pieces[3])
    own, share, *pieces = call(
        functools.partial(output_kernel, len(arrays), group, total),
        [gram_s, gram_t, row_sum, col_sum, *arrays],
        [f32(rows, width), f32(8, 128)] + [f32(width // 128 * rows + EXTRA, 128)] * (n_row - 1),
        4 * math.prod(shape) * width,
    )
    order = sorted(range(n_row - 1), key=lambda k: (-(k + 1).bit_count(), -k))
    masks = span(row_masks)[1:]
    got = [send(pieces[k].astype(jnp.float16), masks[k], count).astype(jnp.float32) for k in order]
    grad, loss = call(
        functools.partial(final_kernel, order, total), [own, share, *got], [f32(rows, width), f32(1, 1)]
    )
    return (loss[0, 0], grad)


def solution(mesh):
    return jax.shard_map(
        per_device,
        mesh=mesh,
        in_specs=(P(AXES, None), P(AXES, None)),
        out_specs=(P(), P(AXES, None)),
        check_vma=False,
    )
```

```python
import functools
import math

import jax
import jax.numpy as jnp
from jax import lax
from jax.experimental import pallas as pl
from jax.experimental.pallas import tpu as pltpu
from jax.sharding import PartitionSpec as P

DS = 768
AXES = ("blk", "inner")
VMEM = 48 * 2**20
SHARE_SCALE = 8.0
EXTRA = 16


EPSILON = 1e-06


def coefficients(sq_student, sq_teacher, cross, total):
    norm_student = jnp.sqrt(sq_student + EPSILON)
    norm_teacher = jnp.sqrt(sq_teacher + EPSILON)
    factor = 2.0 * math.sqrt(total * DS) / total
    cubed = norm_student * norm_student * norm_student
    alpha = factor * (EPSILON / norm_student + cross / norm_teacher) / cubed
    beta = factor / (norm_student * norm_teacher)
    terms = (
        sq_student / (norm_student * norm_student)
        + sq_teacher / (norm_teacher * norm_teacher)
        - 2.0 * cross / (norm_student * norm_teacher)
    )
    return (alpha, beta, terms)


def span(masks):
    out = [0]
    for mask in masks:
        out += [mask ^ other for other in out]
    return out


def subgroups(blocks, inner):
    bits = [1 << b for b in range((inner - 1).bit_length())]
    bits += [inner << b for b in range(1, (blocks - 1).bit_length())]
    return (bits[0::2], bits[1::2] + [inner])


def send(value, mask, count):
    return lax.ppermute(value, AXES, [(i, i ^ mask) for i in range(count)])


def after(value, other):
    return lax.optimization_barrier((value, other))[0]


def join(*values):
    shape = (values[0].shape[0], sum(value.shape[1] for value in values))
    return call(join_kernel, values, jax.ShapeDtypeStruct(shape, values[0].dtype))


def gather(teacher, student, row_masks, col_masks, count):
    *plane_masks, core_mask = col_masks
    row_t, row_s, col_t, col_s = {}, {}, {}, {}
    sides = ((row_t, row_s, row_masks), (col_t, col_s, plane_masks))

    def whole(value):
        return (value, 0, value.shape[1])

    def forward(side, masks, keep):
        for level in range(2, len(masks) + 1):
            for place in range(1 << len(masks)):
                if place.bit_count() == level and keep(place):
                    top = place.bit_length() - 1
                    side[place] = whole(send(side[place ^ (1 << top)][0], masks[top], count))

    for side_t, _, masks in reversed(sides):
        side_t[1] = whole(send(teacher, masks[0], count))
    swapped = [send(value, core_mask, count) for value in (teacher, student)]
    own = join(teacher, student)
    late_t, late_s = after((teacher, student), swapped)
    for side_t, side_s, masks in reversed(sides):
        side_t[0] = (own, 0, teacher.shape[1])
        for b, mask in enumerate(masks):
            if b:
                side_s[1 << b] = whole(send(late_s, mask, count))
                if side_t is col_t:
                    side_t[1 << b] = whole(send(late_t, mask, count))

    def long_way(side_s, masks, gate):
        forward(side_s, masks, lambda place: not place & 1)
        half = range(0, 1 << len(masks), 2)
        parts = [own[:, teacher.shape[1] :]] + [side_s[p][0] for p in half if p]
        side_s[0] = (own, teacher.shape[1], own.shape[1])
        got = send(after(join(*parts), gate), masks[0], count)
        for k, p in enumerate(half):
            side_s[p | 1] = (got, k * student.shape[1], (k + 1) * student.shape[1])

    first = (row_t[1][0], col_t[1][0])
    long_way(col_s, plane_masks, row_s[2][0])
    long_way(row_s, row_masks, first)
    row_t[1], col_t[1] = map(whole, after(first, col_t[2][0]))
    forward(col_t, plane_masks, lambda place: True)
    for b, mask in enumerate(row_masks):
        if b:
            parts = [row_t[p] for p in range(1 << b)]
            got, start = send(join(*(array[:, i:j] for array, i, j in parts)), mask, count), 0
            for p, (_, i, j) in enumerate(parts):
                row_t[p | 1 << b] = (got, start, start + j - i)
                start += j - i

    core_t, core_s = {0: whole(swapped[0])}, {0: whole(swapped[1])}
    ones = [1 << b for b in range(len(plane_masks))]
    rest = [p for p in range(1 << len(plane_masks)) if p.bit_count() > 1]
    swaps = [
        [(col_t, core_t, p) for p in ones] + [(col_s, core_s, p) for p in col_s if p and not p & 1],
        [(col_t, core_t, p) for p in rest],
        [(col_s, core_s, p) for p in col_s if p & 1],
    ]
    for swap in swaps:
        arrays = list({id(side[p][0]): side[p][0] for side, _, p in swap}.values())
        got = send(join(*arrays) if len(arrays) > 1 else arrays[0], core_mask, count)
        starts = {id(array): sum(a.shape[1] for a in arrays[:k]) for k, array in enumerate(arrays)}
        for side, core, p in swap:
            array, start, stop = side[p]
            core[p] = (got, starts[id(array)] + start, starts[id(array)] + stop)
    places = sorted(col_t)
    return (
        [row_t[p] for p in sorted(row_t)],
        [row_s[p] for p in sorted(row_s)],
        [col_t[p] for p in places] + [core_t[p] for p in places],
        [col_s[p] for p in places] + [core_s[p] for p in places],
    )


def operands_of(*groups):
    arrays = []
    for array, _, _ in sum(groups, []):
        if not any(array is other for other in arrays):
            arrays.append(array)
    number = {id(array): k for k, array in enumerate(arrays)}
    return arrays, [[(number[id(array)], start, stop) for array, start, stop in group] for group in groups]


def load(refs, group):
    return jnp.concatenate([refs[k][:, start:stop] for k, start, stop in group])


def tree_sum(values):
    while len(values) > 1:
        values = [values[i] + values[i + 1] for i in range(0, len(values), 2)]
    return values[0]


def join_kernel(*refs):
    *parts, both = refs
    start = 0
    for part in parts:
        both[:, start : start + part.shape[1]] = part[...]
        start += part.shape[1]


def put_sums(parts, row_part, col_part):
    pad = jnp.zeros((parts[0].shape[0], 128 - len(parts)), jnp.float32)
    by_row = jnp.transpose(jnp.concatenate([jnp.sum(p, 1, keepdims=True) for p in parts] + [pad], 1))
    for k, part in enumerate(parts):
        by_col = jnp.sum(part, 0, keepdims=True)
        for source, sums in ((by_row[k : k + 1], row_part), (by_col, col_part)):
            rows = sums.shape[2]
            for p in range(sums.shape[1]):
                sums[k, p : p + 1, :] = source[:, p * rows : (p + 1) * rows]


def early_kernel(groups, *refs):
    *arrays, gram_s, gram_t = refs
    row_t, row_s, col_t, col_s = [load(arrays, group) for group in groups]
    dims = (((1,), (1,)), ((), ()))
    gram_s[...] = lax.dot_general(row_s, col_s, dims, preferred_element_type=jnp.float32)
    gram_t[...] = lax.dot_general(row_t, col_t, dims, preferred_element_type=jnp.float32)


def gram_kernel(groups, early_s, early_t, *refs):
    *arrays, gram_s, gram_t, row_part, col_part = refs
    late_t, col_t = [load(arrays, group) for group in groups]
    dims = (((1,), (1,)), ((), ()))
    late = lax.dot_general(late_t, col_t, dims, preferred_element_type=jnp.float32)
    student, teacher = early_s[...], jnp.concatenate([early_t[...], late])
    gram_s[...], gram_t[...] = student, teacher
    put_sums([student * student, teacher * teacher, student * teacher], row_part, col_part)


def call(kernel, operands, outputs, flops=0, **options):
    size = sum(math.prod(a.shape) * a.dtype.itemsize for a in [*operands, *jax.tree.leaves(outputs)])
    return pl.pallas_call(
        kernel,
        out_shape=outputs,
        **options,
        compiler_params=pltpu.CompilerParams(vmem_limit_bytes=VMEM),
        cost_estimate=pl.CostEstimate(flops=flops, bytes_accessed=size, transcendentals=0),
    )(*operands)


def output_kernel(n_arrays, group, total, gram_s, gram_t, row_sum, col_sum, *refs):
    col_s = load(refs[:n_arrays], group)
    own, share, *pieces = refs[n_arrays:]
    row_alpha, row_beta, _ = coefficients(row_sum[0], row_sum[1], row_sum[2], total)
    col_alpha, col_beta, terms = coefficients(col_sum[0], col_sum[1], col_sum[2], total)
    row_ab = jnp.transpose(jnp.concatenate([row_alpha, row_beta] * 4))
    row_w = row_ab[:, 0:1] * gram_s[...] - row_ab[:, 1:2] * gram_t[...]
    col_w = col_alpha * gram_s[...] - col_beta * gram_t[...]
    out = jnp.dot(row_w.astype(jnp.bfloat16), col_s, preferred_element_type=jnp.float32)
    out += jnp.dot(col_w.astype(jnp.bfloat16), col_s, preferred_element_type=jnp.float32)

    rows, width = own.shape
    own[...] = out[:rows]
    term = jnp.sum(terms, axis=1, keepdims=True)
    share[...] = jnp.broadcast_to(term, share.shape)
    largest = jnp.max(jnp.max(jnp.abs(out), axis=0, keepdims=True), axis=1, keepdims=True)
    power = jnp.clip(jnp.floor(jnp.log2(jnp.maximum(largest, 1e-30))), -100.0, 100.0)
    term = term * SHARE_SCALE
    high = term.astype(jnp.bfloat16).astype(jnp.float32)
    middle = (term - high).astype(jnp.bfloat16).astype(jnp.float32)
    low = term - high - middle
    lane = lax.broadcasted_iota(jnp.int32, (EXTRA, 128), 1)
    extra = jnp.where(lane == 0, power, jnp.where(lane == 1, high, jnp.where(lane == 2, middle, low)))
    scaled = out * jnp.exp2(13.0 - power)
    for k, piece in enumerate(pieces):
        for c in range(width // 128):
            block = scaled[(k + 1) * rows : (k + 2) * rows, c * 128 : (c + 1) * 128]
            piece[c * rows : (c + 1) * rows, :] = block
        piece[width // 128 * rows :, :] = extra


def final_kernel(total, own, share, *refs):
    *pieces, grad, loss = refs
    width = own.shape[1]
    grads, terms = [own[...]], [share[0:1, 0:1]]
    rows = own.shape[0]
    for piece in pieces:
        extra = piece[width // 128 * rows :, :]
        blocks = [piece[c * rows : (c + 1) * rows, :] for c in range(width // 128)]
        grads.append(jnp.concatenate(blocks, 1) * jnp.exp2(extra[0:1, 0:1] - 13.0))
        terms.append((extra[0:1, 1:2] + extra[0:1, 2:3] + extra[0:1, 3:4]) * (1.0 / SHARE_SCALE))
    grad[...] = tree_sum(grads)
    loss[...] = tree_sum(terms) * (1.0 / total)


def exchange_sums(row_part, col_part, row_masks, col_masks, count):
    *plane_masks, core_mask = col_masks
    n_row, n_col, rows = row_part.shape[1], col_part.shape[1], row_part.shape[2]

    def other_core_first(cols):
        return jnp.roll(cols, n_col // 2, 1)

    got = send(jnp.concatenate([row_part, col_part], 1), core_mask, count)
    all_rows = jnp.concatenate([row_part, got[:, :n_row]], 1)
    all_cols = col_part + other_core_first(got[:, n_row:])
    all_cols = jnp.pad(all_cols, ((0, 0), (0, 2 * n_row - n_col), (0, 0)))
    first = (lax.axis_index("blk") & 1) == 0
    sums = jnp.where(first, all_rows, all_cols)
    for b in range(len(row_masks)):
        pairs = []
        for i in range(count):
            masks = plane_masks if i & core_mask else row_masks
            if b < len(masks):
                pairs.append((i, i ^ masks[b]))
        got = lax.ppermute(sums, AXES, pairs).reshape(3, -1, 2, 1 << b, rows)
        sums += jnp.flip(got, 2).reshape(sums.shape)
    got = send(sums, core_mask, count)
    return (
        jnp.where(first, sums[:, :n_row], got[:, n_row:]),
        jnp.where(first, other_core_first(got[:, :n_col]), sums[:, :n_col]),
    )


def per_device(teacher, student):
    rows = teacher.shape[0]
    blocks = lax.axis_size("blk")
    inner = lax.axis_size("inner")
    count = blocks * inner
    total = rows * count
    row_masks, col_masks = subgroups(blocks, inner)
    n_row, n_col = 1 << len(row_masks), 1 << len(col_masks)

    pieces = gather(teacher, student, row_masks, col_masks, count)
    shape, width = (n_row * rows, n_col * rows), student.shape[1]

    def f32(*dims):
        return jax.ShapeDtypeStruct(dims, jnp.float32)

    row_t, row_s, col_t, col_s = pieces
    half = n_row // 2
    flops = 2 * math.prod(shape) * (teacher.shape[1] + width)
    arrays, groups = operands_of(row_t[:half], row_s, col_t, col_s)
    early = call(
        functools.partial(early_kernel, groups),
        arrays,
        [f32(*shape), f32(half * rows, shape[1])],
        flops // 2,
    )
    arrays, groups = operands_of(row_t[half:], col_t)
    gram_s, gram_t, row_part, col_part = call(
        functools.partial(gram_kernel, groups),
        [*early, *arrays],
        [f32(*shape), f32(*shape), f32(3, n_row, rows), f32(3, n_col, rows)],
        flops // 2,
    )
    row_part, col_part = exchange_sums(row_part, col_part, row_masks, col_masks, count)
    row_sum, col_sum = row_part.reshape(3, 1, -1), col_part.reshape(3, 1, -1)

    arrays, (group,) = operands_of(pieces[3])
    own, share, *pieces = call(
        functools.partial(output_kernel, len(arrays), group, total),
        [gram_s, gram_t, row_sum, col_sum, *arrays],
        [f32(rows, width), f32(8, 128)] + [f32(width // 128 * rows + EXTRA, 128)] * (n_row - 1),
        4 * math.prod(shape) * width,
    )
    got = [
        send(value.astype(jnp.float16), mask, count).astype(jnp.float32)
        for value, mask in zip(pieces, span(row_masks)[1:])
    ]
    grad, loss = call(
        functools.partial(final_kernel, total), [own, share, *got], [f32(rows, width), f32(1, 1)]
    )
    return (loss[0, 0], grad)


def solution(mesh):
    return jax.shard_map(
        per_device,
        mesh=mesh,
        in_specs=(P(AXES, None), P(AXES, None)),
        out_specs=(P(), P(AXES, None)),
        check_vma=False,
    )
```

```python
import functools
import math

import jax
import jax.numpy as jnp
from jax import lax
from jax.experimental import pallas as pl
from jax.experimental.pallas import tpu as pltpu
from jax.sharding import PartitionSpec as P

DS = 768
AXES = ("blk", "inner")
VMEM = 48 * 2**20
SHARE_SCALE = 8.0
EXTRA = 16


EPSILON = 1e-06


def coefficients(sq_student, sq_teacher, cross, total):
    norm_student = jnp.sqrt(sq_student + EPSILON)
    norm_teacher = jnp.sqrt(sq_teacher + EPSILON)
    factor = 2.0 * math.sqrt(total * DS) / total
    cubed = norm_student * norm_student * norm_student
    alpha = factor * (EPSILON / norm_student + cross / norm_teacher) / cubed
    beta = factor / (norm_student * norm_teacher)
    terms = (
        sq_student / (norm_student * norm_student)
        + sq_teacher / (norm_teacher * norm_teacher)
        - 2.0 * cross / (norm_student * norm_teacher)
    )
    return (alpha, beta, terms)


def span(masks):
    out = [0]
    for mask in masks:
        out += [mask ^ other for other in out]
    return out


def subgroups(blocks, inner):
    bits = [1 << b for b in range((inner - 1).bit_length())]
    bits += [inner << b for b in range(1, (blocks - 1).bit_length())]
    return (bits[0::2], bits[1::2] + [inner])


def send(value, mask, count):
    return lax.ppermute(value, AXES, [(i, i ^ mask) for i in range(count)])


def after(value, other):
    return lax.optimization_barrier((value, other))[0]


def join(*values):
    shape = (values[0].shape[0], sum(value.shape[1] for value in values))
    return call(join_kernel, values, jax.ShapeDtypeStruct(shape, values[0].dtype))


def gather(teacher, student, row_masks, col_masks, count):
    *plane_masks, core_mask = col_masks
    row_t, row_s, col_t, col_s = {}, {}, {}, {}
    sides = ((row_t, row_s, row_masks), (col_t, col_s, plane_masks))

    def whole(value):
        return (value, 0, value.shape[1])

    def forward(side, masks, keep):
        for level in range(2, len(masks) + 1):
            for place in range(1 << len(masks)):
                if place.bit_count() == level and keep(place):
                    top = place.bit_length() - 1
                    side[place] = whole(send(side[place ^ (1 << top)][0], masks[top], count))

    for side_t, _, masks in reversed(sides):
        side_t[1] = whole(send(teacher, masks[0], count))
    swapped = [send(value, core_mask, count) for value in (teacher, student)]
    own = join(teacher, student)
    late_t, late_s = after((teacher, student), swapped)
    for side_t, side_s, masks in reversed(sides):
        side_t[0] = (own, 0, teacher.shape[1])
        for b, mask in enumerate(masks):
            if b:
                side_s[1 << b] = whole(send(late_s, mask, count))
                if side_t is col_t:
                    side_t[1 << b] = whole(send(late_t, mask, count))

    def long_way(side_s, masks, gate):
        forward(side_s, masks, lambda place: not place & 1)
        half = range(0, 1 << len(masks), 2)
        parts = [own[:, teacher.shape[1] :]] + [side_s[p][0] for p in half if p]
        side_s[0] = (own, teacher.shape[1], own.shape[1])
        got = send(after(join(*parts), gate), masks[0], count)
        for k, p in enumerate(half):
            side_s[p | 1] = (got, k * student.shape[1], (k + 1) * student.shape[1])

    first = (row_t[1][0], col_t[1][0])
    long_way(col_s, plane_masks, row_s[2][0])
    long_way(row_s, row_masks, first)
    row_t[1], col_t[1] = map(whole, after(first, col_t[2][0]))
    forward(col_t, plane_masks, lambda place: True)
    for b, mask in enumerate(row_masks):
        if b:
            parts = [row_t[p] for p in range(1 << b)]
            got, start = send(join(*(array[:, i:j] for array, i, j in parts)), mask, count), 0
            for p, (_, i, j) in enumerate(parts):
                row_t[p | 1 << b] = (got, start, start + j - i)
                start += j - i

    core_t, core_s = {0: whole(swapped[0])}, {0: whole(swapped[1])}
    ones = [1 << b for b in range(len(plane_masks))]
    rest = [p for p in range(1 << len(plane_masks)) if p.bit_count() > 1]
    swaps = [
        [(col_t, core_t, p) for p in ones] + [(col_s, core_s, p) for p in col_s if p and not p & 1],
        [(col_t, core_t, p) for p in rest] + [(col_s, core_s, p) for p in col_s if p & 1],
    ]
    for swap in swaps:
        arrays = list({id(side[p][0]): side[p][0] for side, _, p in swap}.values())
        got = send(after(join(*arrays), row_s[1][0]) if swap is swaps[1] else join(*arrays), core_mask, count)
        starts = {id(array): sum(a.shape[1] for a in arrays[:k]) for k, array in enumerate(arrays)}
        for side, core, p in swap:
            array, start, stop = side[p]
            core[p] = (got, starts[id(array)] + start, starts[id(array)] + stop)
    places = sorted(col_t)
    return (
        [row_t[p] for p in sorted(row_t)],
        [row_s[p] for p in sorted(row_s)],
        [col_t[p] for p in places] + [core_t[p] for p in places],
        [col_s[p] for p in places] + [core_s[p] for p in places],
    )


def operands_of(*groups):
    arrays = []
    for array, _, _ in sum(groups, []):
        if not any(array is other for other in arrays):
            arrays.append(array)
    number = {id(array): k for k, array in enumerate(arrays)}
    return arrays, [[(number[id(array)], start, stop) for array, start, stop in group] for group in groups]


def load(refs, group):
    return jnp.concatenate([refs[k][:, start:stop] for k, start, stop in group])


def tree_sum(values):
    while len(values) > 1:
        values = [values[i] + values[i + 1] for i in range(0, len(values), 2)]
    return values[0]


def join_kernel(*refs):
    *parts, both = refs
    start = 0
    for part in parts:
        both[:, start : start + part.shape[1]] = part[...]
        start += part.shape[1]


def put_sums(parts, row_part, col_part):
    pad = jnp.zeros((parts[0].shape[0], 128 - len(parts)), jnp.float32)
    by_row = jnp.transpose(jnp.concatenate([jnp.sum(p, 1, keepdims=True) for p in parts] + [pad], 1))
    for k, part in enumerate(parts):
        by_col = jnp.sum(part, 0, keepdims=True)
        for source, sums in ((by_row[k : k + 1], row_part), (by_col, col_part)):
            rows = sums.shape[2]
            for p in range(sums.shape[1]):
                sums[k, p : p + 1, :] = source[:, p * rows : (p + 1) * rows]


def gram_kernel(groups, *refs):
    *arrays, gram_s, gram_t, row_part, col_part = refs
    row_t, row_s, col_t, col_s = [load(arrays, group) for group in groups]
    dims = (((1,), (1,)), ((), ()))
    student = lax.dot_general(row_s, col_s, dims, preferred_element_type=jnp.float32)
    teacher = lax.dot_general(row_t, col_t, dims, preferred_element_type=jnp.float32)
    gram_s[...], gram_t[...] = student, teacher
    put_sums([student * student, teacher * teacher, student * teacher], row_part, col_part)


def call(kernel, operands, outputs, flops=0, **options):
    size = sum(math.prod(a.shape) * a.dtype.itemsize for a in [*operands, *jax.tree.leaves(outputs)])
    return pl.pallas_call(
        kernel,
        out_shape=outputs,
        **options,
        compiler_params=pltpu.CompilerParams(vmem_limit_bytes=VMEM),
        cost_estimate=pl.CostEstimate(flops=flops, bytes_accessed=size, transcendentals=0),
    )(*operands)


def output_kernel(n_arrays, group, total, gram_s, gram_t, row_sum, col_sum, *refs):
    col_s = load(refs[:n_arrays], group)
    own, share, *pieces = refs[n_arrays:]
    row_alpha, row_beta, _ = coefficients(row_sum[0], row_sum[1], row_sum[2], total)
    col_alpha, col_beta, terms = coefficients(col_sum[0], col_sum[1], col_sum[2], total)
    row_ab = jnp.transpose(jnp.concatenate([row_alpha, row_beta] * 4))
    row_w = row_ab[:, 0:1] * gram_s[...] - row_ab[:, 1:2] * gram_t[...]
    col_w = col_alpha * gram_s[...] - col_beta * gram_t[...]
    out = jnp.dot(row_w.astype(jnp.bfloat16), col_s, preferred_element_type=jnp.float32)
    out += jnp.dot(col_w.astype(jnp.bfloat16), col_s, preferred_element_type=jnp.float32)

    rows, width = own.shape
    own[...] = out[:rows]
    term = jnp.sum(terms, axis=1, keepdims=True)
    share[...] = jnp.broadcast_to(term, share.shape)
    largest = jnp.max(jnp.max(jnp.abs(out), axis=0, keepdims=True), axis=1, keepdims=True)
    power = jnp.clip(jnp.floor(jnp.log2(jnp.maximum(largest, 1e-30))), -100.0, 100.0)
    term = term * SHARE_SCALE
    high = term.astype(jnp.bfloat16).astype(jnp.float32)
    middle = (term - high).astype(jnp.bfloat16).astype(jnp.float32)
    low = term - high - middle
    lane = lax.broadcasted_iota(jnp.int32, (EXTRA, 128), 1)
    extra = jnp.where(lane == 0, power, jnp.where(lane == 1, high, jnp.where(lane == 2, middle, low)))
    scaled = out * jnp.exp2(13.0 - power)
    for k, piece in enumerate(pieces):
        for c in range(width // 128):
            block = scaled[(k + 1) * rows : (k + 2) * rows, c * 128 : (c + 1) * 128]
            piece[c * rows : (c + 1) * rows, :] = block
        piece[width // 128 * rows :, :] = extra


def final_kernel(total, own, share, *refs):
    *pieces, grad, loss = refs
    width = own.shape[1]
    grads, terms = [own[...]], [share[0:1, 0:1]]
    rows = own.shape[0]
    for piece in pieces:
        extra = piece[width // 128 * rows :, :]
        blocks = [piece[c * rows : (c + 1) * rows, :] for c in range(width // 128)]
        grads.append(jnp.concatenate(blocks, 1) * jnp.exp2(extra[0:1, 0:1] - 13.0))
        terms.append((extra[0:1, 1:2] + extra[0:1, 2:3] + extra[0:1, 3:4]) * (1.0 / SHARE_SCALE))
    grad[...] = tree_sum(grads)
    loss[...] = tree_sum(terms) * (1.0 / total)


def exchange_sums(row_part, col_part, row_masks, col_masks, count):
    *plane_masks, core_mask = col_masks
    n_row, n_col, rows = row_part.shape[1], col_part.shape[1], row_part.shape[2]

    def other_core_first(cols):
        return jnp.roll(cols, n_col // 2, 1)

    got = send(jnp.concatenate([row_part, col_part], 1), core_mask, count)
    all_rows = jnp.concatenate([row_part, got[:, :n_row]], 1)
    all_cols = col_part + other_core_first(got[:, n_row:])
    all_cols = jnp.pad(all_cols, ((0, 0), (0, 2 * n_row - n_col), (0, 0)))
    first = (lax.axis_index("blk") & 1) == 0
    sums = jnp.where(first, all_rows, all_cols)
    for b in range(len(row_masks)):
        pairs = []
        for i in range(count):
            masks = plane_masks if i & core_mask else row_masks
            if b < len(masks):
                pairs.append((i, i ^ masks[b]))
        got = lax.ppermute(sums, AXES, pairs).reshape(3, -1, 2, 1 << b, rows)
        sums += jnp.flip(got, 2).reshape(sums.shape)
    got = send(sums, core_mask, count)
    return (
        jnp.where(first, sums[:, :n_row], got[:, n_row:]),
        jnp.where(first, other_core_first(got[:, :n_col]), sums[:, :n_col]),
    )


def per_device(teacher, student):
    rows = teacher.shape[0]
    blocks = lax.axis_size("blk")
    inner = lax.axis_size("inner")
    count = blocks * inner
    total = rows * count
    row_masks, col_masks = subgroups(blocks, inner)
    n_row, n_col = 1 << len(row_masks), 1 << len(col_masks)

    pieces = gather(teacher, student, row_masks, col_masks, count)
    shape, width = (n_row * rows, n_col * rows), student.shape[1]

    def f32(*dims):
        return jax.ShapeDtypeStruct(dims, jnp.float32)

    arrays, groups = operands_of(*pieces)
    gram_s, gram_t, row_part, col_part = call(
        functools.partial(gram_kernel, groups),
        arrays,
        [f32(*shape), f32(*shape), f32(3, n_row, rows), f32(3, n_col, rows)],
        2 * math.prod(shape) * (teacher.shape[1] + width),
    )
    row_part, col_part = exchange_sums(row_part, col_part, row_masks, col_masks, count)
    row_sum, col_sum = row_part.reshape(3, 1, -1), col_part.reshape(3, 1, -1)

    arrays, (group,) = operands_of(pieces[3])
    own, share, *pieces = call(
        functools.partial(output_kernel, len(arrays), group, total),
        [gram_s, gram_t, row_sum, col_sum, *arrays],
        [f32(rows, width), f32(8, 128)] + [f32(width // 128 * rows + EXTRA, 128)] * (n_row - 1),
        4 * math.prod(shape) * width,
    )
    got = [
        send(value.astype(jnp.float16), mask, count).astype(jnp.float32)
        for value, mask in zip(pieces, span(row_masks)[1:])
    ]
    grad, loss = call(
        functools.partial(final_kernel, total), [own, share, *got], [f32(rows, width), f32(1, 1)]
    )
    return (loss[0, 0], grad)


def solution(mesh):
    return jax.shard_map(
        per_device,
        mesh=mesh,
        in_specs=(P(AXES, None), P(AXES, None)),
        out_specs=(P(), P(AXES, None)),
        check_vma=False,
    )
```

```python
import functools
import math

import jax
import jax.numpy as jnp
from jax import lax
from jax.experimental import pallas as pl
from jax.experimental.pallas import tpu as pltpu
from jax.sharding import PartitionSpec as P

DS = 768
AXES = ("blk", "inner")
VMEM = 48 * 2**20
SHARE_SCALE = 8.0
EXTRA = 16


EPSILON = 1e-06


def coefficients(sq_student, sq_teacher, cross, total):
    norm_student = jnp.sqrt(sq_student + EPSILON)
    norm_teacher = jnp.sqrt(sq_teacher + EPSILON)
    factor = 2.0 * math.sqrt(total * DS) / total
    cubed = norm_student * norm_student * norm_student
    alpha = factor * (EPSILON / norm_student + cross / norm_teacher) / cubed
    beta = factor / (norm_student * norm_teacher)
    terms = (
        sq_student / (norm_student * norm_student)
        + sq_teacher / (norm_teacher * norm_teacher)
        - 2.0 * cross / (norm_student * norm_teacher)
    )
    return (alpha, beta, terms)


def span(masks):
    out = [0]
    for mask in masks:
        out += [mask ^ other for other in out]
    return out


def subgroups(blocks, inner):
    bits = [1 << b for b in range((inner - 1).bit_length())]
    bits += [inner << b for b in range(1, (blocks - 1).bit_length())]
    return (bits[0::2], bits[1::2] + [inner])


def send(value, mask, count):
    return lax.ppermute(value, AXES, [(i, i ^ mask) for i in range(count)])


def after(value, other):
    return lax.optimization_barrier((value, other))[0]


def join(*values):
    shape = (values[0].shape[0], sum(value.shape[1] for value in values))
    return call(join_kernel, values, jax.ShapeDtypeStruct(shape, values[0].dtype))


def gather(teacher, student, row_masks, col_masks, count):
    *plane_masks, core_mask = col_masks
    row_t, row_s, col_t, col_s = {}, {}, {}, {}
    sides = ((row_t, row_s, row_masks), (col_t, col_s, plane_masks))

    def whole(value):
        return (value, 0, value.shape[1])

    def forward(side, masks, keep):
        for level in range(2, len(masks) + 1):
            for place in range(1 << len(masks)):
                if place.bit_count() == level and keep(place):
                    top = place.bit_length() - 1
                    side[place] = whole(send(side[place ^ (1 << top)][0], masks[top], count))

    col_t[1] = whole(send(teacher, plane_masks[0], count))
    swapped = [send(value, core_mask, count) for value in (teacher, student)]
    own = join(teacher, student)
    late_t, late_s = after((teacher, student), swapped)
    row_t[1] = whole(send(after(teacher, swapped[1]), row_masks[0], count))
    for side_t, side_s, masks in reversed(sides):
        side_t[0] = (own, 0, teacher.shape[1])
        for b, mask in enumerate(masks):
            if b:
                side_s[1 << b] = whole(send(late_s, mask, count))
                if side_t is col_t:
                    side_t[1 << b] = whole(send(late_t, mask, count))

    def long_way(side_s, masks, gate):
        forward(side_s, masks, lambda place: not place & 1)
        half = range(0, 1 << len(masks), 2)
        parts = [own[:, teacher.shape[1] :]] + [side_s[p][0] for p in half if p]
        side_s[0] = (own, teacher.shape[1], own.shape[1])
        got = send(after(join(*parts), gate), masks[0], count)
        for k, p in enumerate(half):
            side_s[p | 1] = (got, k * student.shape[1], (k + 1) * student.shape[1])

    first = (row_t[1][0], col_t[1][0])
    long_way(col_s, plane_masks, row_s[2][0])
    long_way(row_s, row_masks, first)
    row_t[1], col_t[1] = map(whole, after(first, col_t[2][0]))
    forward(col_t, plane_masks, lambda place: True)
    for b, mask in enumerate(row_masks):
        if b:
            parts = [row_t[p] for p in range(1 << b)]
            got, start = send(join(*(array[:, i:j] for array, i, j in parts)), mask, count), 0
            for p, (_, i, j) in enumerate(parts):
                row_t[p | 1 << b] = (got, start, start + j - i)
                start += j - i

    core_t, core_s = {0: whole(swapped[0])}, {0: whole(swapped[1])}
    ones = [1 << b for b in range(len(plane_masks))]
    rest = [p for p in range(1 << len(plane_masks)) if p.bit_count() > 1]
    swaps = [
        [(col_t, core_t, p) for p in ones] + [(col_s, core_s, p) for p in col_s if p and not p & 1],
        [(col_t, core_t, p) for p in rest] + [(col_s, core_s, p) for p in col_s if p & 1],
    ]
    for swap in swaps:
        arrays = list({id(side[p][0]): side[p][0] for side, _, p in swap}.values())
        got = send(after(join(*arrays), row_s[1][0]) if swap is swaps[1] else join(*arrays), core_mask, count)
        starts = {id(array): sum(a.shape[1] for a in arrays[:k]) for k, array in enumerate(arrays)}
        for side, core, p in swap:
            array, start, stop = side[p]
            core[p] = (got, starts[id(array)] + start, starts[id(array)] + stop)
    places = sorted(col_t)
    return (
        [row_t[p] for p in sorted(row_t)],
        [row_s[p] for p in sorted(row_s)],
        [col_t[p] for p in places] + [core_t[p] for p in places],
        [col_s[p] for p in places] + [core_s[p] for p in places],
    )


def operands_of(*groups):
    arrays = []
    for array, _, _ in sum(groups, []):
        if not any(array is other for other in arrays):
            arrays.append(array)
    number = {id(array): k for k, array in enumerate(arrays)}
    return arrays, [[(number[id(array)], start, stop) for array, start, stop in group] for group in groups]


def load(refs, group):
    return jnp.concatenate([refs[k][:, start:stop] for k, start, stop in group])


def tree_sum(values):
    while len(values) > 1:
        values = [values[i] + values[i + 1] for i in range(0, len(values), 2)]
    return values[0]


def join_kernel(*refs):
    *parts, both = refs
    start = 0
    for part in parts:
        both[:, start : start + part.shape[1]] = part[...]
        start += part.shape[1]


def put_sums(parts, row_part, col_part):
    pad = jnp.zeros((parts[0].shape[0], 128 - len(parts)), jnp.float32)
    by_row = jnp.transpose(jnp.concatenate([jnp.sum(p, 1, keepdims=True) for p in parts] + [pad], 1))
    for k, part in enumerate(parts):
        by_col = jnp.sum(part, 0, keepdims=True)
        for source, sums in ((by_row[k : k + 1], row_part), (by_col, col_part)):
            rows = sums.shape[2]
            for p in range(sums.shape[1]):
                sums[k, p : p + 1, :] = source[:, p * rows : (p + 1) * rows]


def gram_kernel(groups, *refs):
    *arrays, gram_s, gram_t, row_part, col_part = refs
    row_t, row_s, col_t, col_s = [load(arrays, group) for group in groups]
    dims = (((1,), (1,)), ((), ()))
    student = lax.dot_general(row_s, col_s, dims, preferred_element_type=jnp.float32)
    teacher = lax.dot_general(row_t, col_t, dims, preferred_element_type=jnp.float32)
    gram_s[...], gram_t[...] = student, teacher
    put_sums([student * student, teacher * teacher, student * teacher], row_part, col_part)


def call(kernel, operands, outputs, flops=0, **options):
    size = sum(math.prod(a.shape) * a.dtype.itemsize for a in [*operands, *jax.tree.leaves(outputs)])
    return pl.pallas_call(
        kernel,
        out_shape=outputs,
        **options,
        compiler_params=pltpu.CompilerParams(vmem_limit_bytes=VMEM),
        cost_estimate=pl.CostEstimate(flops=flops, bytes_accessed=size, transcendentals=0),
    )(*operands)


def output_kernel(n_arrays, group, total, gram_s, gram_t, row_sum, col_sum, *refs):
    col_s = load(refs[:n_arrays], group)
    own, share, *pieces = refs[n_arrays:]
    row_alpha, row_beta, _ = coefficients(row_sum[0], row_sum[1], row_sum[2], total)
    col_alpha, col_beta, terms = coefficients(col_sum[0], col_sum[1], col_sum[2], total)
    row_ab = jnp.transpose(jnp.concatenate([row_alpha, row_beta] * 4))
    row_w = row_ab[:, 0:1] * gram_s[...] - row_ab[:, 1:2] * gram_t[...]
    col_w = col_alpha * gram_s[...] - col_beta * gram_t[...]
    out = jnp.dot(row_w.astype(jnp.bfloat16), col_s, preferred_element_type=jnp.float32)
    out += jnp.dot(col_w.astype(jnp.bfloat16), col_s, preferred_element_type=jnp.float32)

    rows, width = own.shape
    own[...] = out[:rows]
    term = jnp.sum(terms, axis=1, keepdims=True)
    share[...] = jnp.broadcast_to(term, share.shape)
    largest = jnp.max(jnp.max(jnp.abs(out), axis=0, keepdims=True), axis=1, keepdims=True)
    power = jnp.clip(jnp.floor(jnp.log2(jnp.maximum(largest, 1e-30))), -100.0, 100.0)
    term = term * SHARE_SCALE
    high = term.astype(jnp.bfloat16).astype(jnp.float32)
    middle = (term - high).astype(jnp.bfloat16).astype(jnp.float32)
    low = term - high - middle
    lane = lax.broadcasted_iota(jnp.int32, (EXTRA, 128), 1)
    extra = jnp.where(lane == 0, power, jnp.where(lane == 1, high, jnp.where(lane == 2, middle, low)))
    scaled = out * jnp.exp2(13.0 - power)
    for k, piece in enumerate(pieces):
        for c in range(width // 128):
            block = scaled[(k + 1) * rows : (k + 2) * rows, c * 128 : (c + 1) * 128]
            piece[c * rows : (c + 1) * rows, :] = block
        piece[width // 128 * rows :, :] = extra


def final_kernel(total, own, share, *refs):
    *pieces, grad, loss = refs
    width = own.shape[1]
    grads, terms = [own[...]], [share[0:1, 0:1]]
    rows = own.shape[0]
    for piece in pieces:
        extra = piece[width // 128 * rows :, :]
        blocks = [piece[c * rows : (c + 1) * rows, :] for c in range(width // 128)]
        grads.append(jnp.concatenate(blocks, 1) * jnp.exp2(extra[0:1, 0:1] - 13.0))
        terms.append((extra[0:1, 1:2] + extra[0:1, 2:3] + extra[0:1, 3:4]) * (1.0 / SHARE_SCALE))
    grad[...] = tree_sum(grads)
    loss[...] = tree_sum(terms) * (1.0 / total)


def exchange_sums(row_part, col_part, row_masks, col_masks, count):
    *plane_masks, core_mask = col_masks
    n_row, n_col, rows = row_part.shape[1], col_part.shape[1], row_part.shape[2]

    def other_core_first(cols):
        return jnp.roll(cols, n_col // 2, 1)

    got = send(jnp.concatenate([row_part, col_part], 1), core_mask, count)
    all_rows = jnp.concatenate([row_part, got[:, :n_row]], 1)
    all_cols = col_part + other_core_first(got[:, n_row:])
    all_cols = jnp.pad(all_cols, ((0, 0), (0, 2 * n_row - n_col), (0, 0)))
    first = (lax.axis_index("blk") & 1) == 0
    sums = jnp.where(first, all_rows, all_cols)
    for b in range(len(row_masks)):
        pairs = []
        for i in range(count):
            masks = plane_masks if i & core_mask else row_masks
            if b < len(masks):
                pairs.append((i, i ^ masks[b]))
        got = lax.ppermute(sums, AXES, pairs).reshape(3, -1, 2, 1 << b, rows)
        sums += jnp.flip(got, 2).reshape(sums.shape)
    got = send(sums, core_mask, count)
    return (
        jnp.where(first, sums[:, :n_row], got[:, n_row:]),
        jnp.where(first, other_core_first(got[:, :n_col]), sums[:, :n_col]),
    )


def per_device(teacher, student):
    rows = teacher.shape[0]
    blocks = lax.axis_size("blk")
    inner = lax.axis_size("inner")
    count = blocks * inner
    total = rows * count
    row_masks, col_masks = subgroups(blocks, inner)
    n_row, n_col = 1 << len(row_masks), 1 << len(col_masks)

    pieces = gather(teacher, student, row_masks, col_masks, count)
    shape, width = (n_row * rows, n_col * rows), student.shape[1]

    def f32(*dims):
        return jax.ShapeDtypeStruct(dims, jnp.float32)

    arrays, groups = operands_of(*pieces)
    gram_s, gram_t, row_part, col_part = call(
        functools.partial(gram_kernel, groups),
        arrays,
        [f32(*shape), f32(*shape), f32(3, n_row, rows), f32(3, n_col, rows)],
        2 * math.prod(shape) * (teacher.shape[1] + width),
    )
    row_part, col_part = exchange_sums(row_part, col_part, row_masks, col_masks, count)
    row_sum, col_sum = row_part.reshape(3, 1, -1), col_part.reshape(3, 1, -1)

    arrays, (group,) = operands_of(pieces[3])
    own, share, *pieces = call(
        functools.partial(output_kernel, len(arrays), group, total),
        [gram_s, gram_t, row_sum, col_sum, *arrays],
        [f32(rows, width), f32(8, 128)] + [f32(width // 128 * rows + EXTRA, 128)] * (n_row - 1),
        4 * math.prod(shape) * width,
    )
    got = [
        send(value.astype(jnp.float16), mask, count).astype(jnp.float32)
        for value, mask in zip(pieces, span(row_masks)[1:])
    ]
    grad, loss = call(
        functools.partial(final_kernel, total), [own, share, *got], [f32(rows, width), f32(1, 1)]
    )
    return (loss[0, 0], grad)


def solution(mesh):
    return jax.shard_map(
        per_device,
        mesh=mesh,
        in_specs=(P(AXES, None), P(AXES, None)),
        out_specs=(P(), P(AXES, None)),
        check_vma=False,
    )
```
